32 devices in a mesh: dp: 8 (over z, x), row: 2 (over core), col: 2 (over y).
Axes of the slice: x: 2, y: 2, z: 4, core: 2. Of those that a mesh axis runs over, the one named last changes fastest.
Arguments:
- block_input: bfloat16 [8192, 1536], P(('dp', 'row'), 'col'), may hold values from -6 to 6
- segment_ids: int32 [8192], P('dp'), may hold values from 0 to 2, as said below
- first_gain: float32 [1536], P('col'), may hold values from 0.25 to 1.75
- qkv_weight: bfloat16 [2, 2, 768, 1024], P('col', 'row'), may hold values from -0.15625 to 0.15625
- qkv_bias: float32 [2, 1024], P('row'), may hold values from -3 to 3
- output_weight: bfloat16 [2, 2, 768, 768], P('row', 'col'), may hold values from -0.625 to 0.625
- second_gain: float32 [1536], P('col'), may hold values from 0.25 to 1.75
- gate_up_weight: bfloat16 [2, 2, 768, 8960], P('col', 'row'), may hold values from -0.15625 to 0.15625
- down_weight: bfloat16 [2, 2, 4480, 768], P('row', 'col'), may hold values from -0.0625 to 0.0625
- output_grad: bfloat16 [8192, 1536], P(('dp', 'row'), 'col'), may hold values from -6 to 6
Outputs:
- block_output: bfloat16 [8192, 1536], P(('dp', 'row'), 'col')
- input_grad: float32 [8192, 1536], P(('dp', 'row'), 'col')
- first_gain_grad: float32 [1536], P('col')
- qkv_weight_grad: float32 [2, 2, 768, 1024], P('col', 'row', 'dp')
- qkv_bias_grad: float32 [2, 1024], P('row', 'dp')
- output_weight_grad: float32 [2, 2, 768, 768], P('row', 'col', 'dp')
- second_gain_grad: float32 [1536], P('col')
- gate_up_grad: float32 [2, 2, 768, 8960], P('col', 'row', 'dp')
- down_grad: float32 [2, 2, 4480, 768], P('row', 'col', 'dp')
The draws below stay inside these ranges and needn't reach their ends.
Inputs may be any that keep to these rules, and one draw needn't show every extreme that they name: `segment_ids`: in each sequence of 1024 tokens the segment numbers start at 0, never fall, and rise by one at exactly 2 tokens; no document starts within 64 tokens of the sequence's middle token 512.
All inputs are finite; a program needn't handle non-finite values.
Results may differ from the reference program's by a relative error of at most 0.012.
Values may be sent and summed in bfloat16 or wider, within the bound.
No kernel may reach another device: no remote copies, remote signals or barrier semaphores. Data moves between devices by JAX's collectives and lax.ppermute only.
A program may use at most 256 MiB of HBM per device.

```python
import jax
import jax.numpy as jnp
from jax import lax

D = 1536
FF = 8960
HEADS = 12
KV_HEADS = 2
HEAD_DIM = 128
SEQ_LEN = 1024
MIN_DOC = 200
TOKENS = 8192
N_ROW = 2
N_COL = 2


def offset_below(raw_bits, extent):
    return raw_bits % (extent + 1)


def draw_segment_ids(key, part):
    key = jax.random.fold_in(key, 11)
    sequences = TOKENS // SEQ_LEN
    middle = SEQ_LEN // 2
    margin = SEQ_LEN // 16
    left_high = middle - margin
    right_low = middle + margin
    right_high = SEQ_LEN - MIN_DOC
    key_side, key_one, key_two = jax.random.split(key, 3)
    side_count = jax.random.randint(key_side, (sequences,), 0, 3, dtype=jnp.int32)
    bits_one = jax.random.randint(key_one, (sequences,), 0, 1048576, dtype=jnp.int32)
    bits_two = jax.random.randint(key_two, (sequences,), 0, 1048576, dtype=jnp.int32)
    two_left_first = MIN_DOC + offset_below(bits_one, left_high - 2 * MIN_DOC)
    two_left_second = two_left_first + MIN_DOC + offset_below(bits_two, left_high - two_left_first - MIN_DOC)
    two_right_first = right_low + offset_below(bits_one, right_high - MIN_DOC - right_low)
    two_right_second = two_right_first + MIN_DOC + offset_below(bits_two, right_high - two_right_first - MIN_DOC)
    split_first = MIN_DOC + offset_below(bits_one, left_high - MIN_DOC)
    split_second = right_low + offset_below(bits_two, right_high - right_low)
    first_start = jnp.where(side_count == 2, two_left_first, jnp.where(side_count == 0, two_right_first, split_first))
    second_start = jnp.where(side_count == 2, two_left_second, jnp.where(side_count == 0, two_right_second, split_second))
    position_index = jnp.arange(SEQ_LEN, dtype=jnp.int32)
    segments = (position_index[None, :] >= first_start[:, None]).astype(jnp.int32)
    segments = segments + (position_index[None, :] >= second_start[:, None]).astype(jnp.int32)
    return segments.astype(jnp.int32).reshape(-1)


def raised(values, own_key, source, target, blocks, factor):
    def block_of(position):
        return (jnp.arange(values.shape[position]) // (values.shape[position] // blocks)).reshape((-1,) + (1,) * (values.ndim - 1 - position))

    one_side = jax.random.permutation(own_key, blocks)[block_of(target)]
    second = (block_of(target) + blocks // 2) % blocks
    return jnp.where((block_of(source) == one_side) | (block_of(source) == second), factor * values, values)


def block_levels(key, shape, cuts, low, top_value):
    factor_of = 1.0
    for position, parts in cuts:
        steps = jax.random.uniform(jax.random.fold_in(jax.random.fold_in(key, 6), position), (parts,), jnp.float32, low / len(cuts), top_value / len(cuts))
        factor_of = factor_of * jnp.repeat(jnp.exp(steps), shape[position] // parts).reshape((-1,) + (1,) * (len(shape) - 1 - position))
    return factor_of


def bell_draw(rng, shape, width, most, cuts=(), kind=jnp.bfloat16):
    values = width * jax.random.normal(rng, shape, jnp.float32)
    if cuts:
        values = values * block_levels(rng, shape, cuts, -0.22, 0.18)
    return jnp.clip(values, -most, most).astype(kind)


def bell_draw_with(rng, dims, spread, most, cuts, heavy, held_as=jnp.bfloat16):
    drawn = spread * jax.random.normal(rng, dims, jnp.float32)
    if cuts:
        drawn = drawn * block_levels(rng, dims, cuts, -0.22, 0.18)
    return jnp.clip(raised(drawn, jax.random.fold_in(rng, 3), *heavy), -most, most).astype(held_as)


def setup_inputs(seed: int = 0) -> dict:
    key_of = jax.random.split(jax.random.key(seed), 11)
    return {
        "block_input": bell_draw_with(key_of[0], (TOKENS, D), 1.0, 6.0, ((0, 16), (1, 2)), (0, 1, 16, 2.0)),
        "segment_ids": draw_segment_ids(jax.random.fold_in(key_of[10], 71), 0),
        "first_gain": jnp.clip(1.0 + 0.15 * jax.random.normal(key_of[2], (D,), jnp.float32), 0.25, 1.75),
        "qkv_weight": bell_draw(key_of[3], (N_COL, N_ROW, D // N_COL, (HEADS + 2 * KV_HEADS) * HEAD_DIM // N_ROW), D ** -0.5, 0.15625, ((0, 2), (1, 2))),
        "qkv_bias": bell_draw(key_of[4], (N_ROW, (HEADS + 2 * KV_HEADS) * HEAD_DIM // N_ROW), 0.5, 3.0, ((0, 2),), jnp.float32),
        "output_weight": bell_draw(key_of[5], (N_ROW, N_COL, HEADS * HEAD_DIM // N_ROW, D // N_COL), (HEADS * HEAD_DIM // 16) ** -0.5, 0.625, ((0, 2), (1, 2))),
        "second_gain": jnp.clip(1.0 + 0.15 * jax.random.normal(key_of[6], (D,), jnp.float32), 0.25, 1.75),
        "gate_up_weight": bell_draw(key_of[7], (N_COL, N_ROW, D // N_COL, 2 * FF // N_ROW), D ** -0.5, 0.15625, ((0, 2), (1, 2))),
        "down_weight": bell_draw(key_of[8], (N_ROW, N_COL, FF // N_ROW, D // N_COL), FF ** -0.5, 0.0625, ((0, 2), (1, 2))),
        "output_grad": bell_draw_with(key_of[9], (TOKENS, D), 1.0, 6.0, ((0, 16), (1, 2)), (0, 1, 16, 2.0)),
    }


EPSILON = 1e-06
ROPE_BASE = 1000000.0
MASKED = -1e+30

@jax.custom_vjp
def low(v):
    return lax.optimization_barrier(v.astype(jnp.bfloat16)).astype(jnp.float32)

@jax.custom_vjp
def low_back(v):
    return v

def low_keep(v):
    return (low(v), None)

def low_pass(kept, grad):
    return (grad,)

def back_keep(v):
    return (v, None)

def back_low(kept, grad):
    return (low(grad),)
low.defvjp(low_keep, low_pass)
low_back.defvjp(back_keep, back_low)

def full_matrix(blocks):
    return blocks.transpose(0, 2, 1, 3).reshape(blocks.shape[0] * blocks.shape[2], blocks.shape[1] * blocks.shape[3])

def product(left_side, right_side):
    return jnp.dot(left_side, right_side, precision=lax.Precision.HIGHEST, preferred_element_type=jnp.float32)

def root_norm(stream, gain_vector):
    scaling = lax.rsqrt(lax.optimization_barrier(jnp.mean(stream * stream, axis=-1, keepdims=True)) + EPSILON)
    return stream * scaling * gain_vector

def positions_of(segment_row):
    position_index = jnp.arange(segment_row.shape[0], dtype=jnp.int32)
    doc_first = jnp.concatenate([jnp.ones((1,), jnp.bool_), segment_row[1:] != segment_row[:-1]])
    return position_index - lax.cummax(jnp.where(doc_first, position_index, 0), axis=0)

def rope_tables(positions):
    frequency = ROPE_BASE ** (-jnp.arange(0, HEAD_DIM, 2, dtype=jnp.float32) / HEAD_DIM)
    angles = positions.astype(jnp.float32)[:, None] * frequency[None, :]
    angles = jnp.concatenate([angles, angles], axis=1)
    return (jnp.cos(angles)[:, None, :], jnp.sin(angles)[:, None, :])

def rotate(values, cosine, sine):
    half_dim = values.shape[-1] // 2
    turned = jnp.concatenate([-values[..., half_dim:], values[..., :half_dim]], axis=-1)
    return values * cosine + turned * sine

def attend(query, key_part, value_part, segment_row):
    groups = HEADS // KV_HEADS
    key_wide = jnp.repeat(key_part, groups, axis=1)
    value_wide = jnp.repeat(value_part, groups, axis=1)
    scores = jnp.einsum('qhd,khd->hqk', query, key_wide, precision=lax.Precision.HIGHEST) * HEAD_DIM ** (-0.5)
    scores = low_back(scores)
    position_index = jnp.arange(segment_row.shape[0], dtype=jnp.int32)
    allowed = (position_index[None, :] <= position_index[:, None]) & (segment_row[None, :] == segment_row[:, None])
    scores = jnp.where(allowed[None], scores, MASKED)
    row_top = lax.optimization_barrier(jnp.max(scores, axis=-1, keepdims=True))
    exponent = jnp.exp(scores - row_top)
    softmax_p = low(exponent / lax.optimization_barrier(jnp.sum(exponent, axis=-1, keepdims=True)))
    return jnp.einsum('hqk,khd->qhd', softmax_p, value_wide, precision=lax.Precision.HIGHEST)

def block_forward(stream, gain_one, weight_qkv, bias_qkv, weight_out, gain_two, weight_gate_up, weight_down, segment_ids, cosine, sine):
    token_count = stream.shape[0]
    query_width = HEADS // N_ROW * HEAD_DIM
    key_width = KV_HEADS // N_ROW * HEAD_DIM
    first_normed = low(root_norm(stream, gain_one))
    projected = low_back(product(first_normed, full_matrix(weight_qkv)) + bias_qkv.reshape(-1))
    projected = projected.reshape(token_count, N_ROW, -1)
    query = projected[:, :, :query_width].reshape(token_count, HEADS, HEAD_DIM)
    key_part = projected[:, :, query_width:query_width + key_width].reshape(token_count, KV_HEADS, HEAD_DIM)
    value_part = projected[:, :, query_width + key_width:].reshape(token_count, KV_HEADS, HEAD_DIM)
    query = low(rotate(query, cosine, sine))
    key_part = low(rotate(key_part, cosine, sine))
    value_part = low(value_part)
    sequences = token_count // SEQ_LEN
    attended = lax.map(jax.checkpoint(lambda block_item: attend(*block_item)), (query.reshape(sequences, SEQ_LEN, HEADS, HEAD_DIM), key_part.reshape(sequences, SEQ_LEN, KV_HEADS, HEAD_DIM), value_part.reshape(sequences, SEQ_LEN, KV_HEADS, HEAD_DIM), segment_ids.reshape(sequences, SEQ_LEN)))
    attended = low(low_back(attended.reshape(token_count, HEADS * HEAD_DIM)))
    hidden_one = stream + low_back(product(attended, full_matrix(weight_out)))
    second_normed = low(root_norm(hidden_one, gain_two))
    gate_up = low_back(product(second_normed, full_matrix(weight_gate_up))).reshape(token_count, N_ROW, 2, FF // N_ROW)
    gate_part = gate_up[:, :, 0].reshape(token_count, FF)
    up_part = gate_up[:, :, 1].reshape(token_count, FF)
    activated = low(jax.nn.silu(gate_part) * up_part)
    return hidden_one + low_back(product(activated, full_matrix(weight_down)))

def reference(block_input, segment_ids, first_gain, qkv_weight, qkv_bias, output_weight, second_gain, gate_up_weight, down_weight, output_grad):
    positions = jax.vmap(positions_of)(segment_ids.reshape(-1, SEQ_LEN)).reshape(-1)
    cosine, sine = rope_tables(positions)

    def forward(stream, gain_one, weight_qkv, bias_qkv, weight_out, gain_two, weight_gate_up, weight_down):
        return block_forward(stream, gain_one, weight_qkv, bias_qkv, weight_out, gain_two, weight_gate_up, weight_down, segment_ids, cosine, sine)
    result, pullback = jax.vjp(forward, block_input.astype(jnp.float32), first_gain, qkv_weight.astype(jnp.float32), qkv_bias, output_weight.astype(jnp.float32), second_gain, gate_up_weight.astype(jnp.float32), down_weight.astype(jnp.float32))
    gradients = pullback(output_grad.astype(jnp.float32))
    return (result.astype(jnp.bfloat16), gradients[0], gradients[1], gradients[2], gradients[3], gradients[4], gradients[5], gradients[6], gradients[7])
```

```python
import jax
import jax.numpy as jnp
from jax import lax
from jax.sharding import PartitionSpec as P

HEADS = 12
KV_HEADS = 2
HEAD_DIM = 128
EPSILON = 1e-06
ROPE_BASE = 1000000.0
MASKED = -1e30
F32 = jnp.float32
BF16 = jnp.bfloat16


def dot(left, right, left_dim, right_dim):
    return lax.dot_general(
        left, right, (((left_dim,), (right_dim,)), ((), ())), preferred_element_type=F32
    )


def swap(part, axis_name):
    return lax.ppermute(part, axis_name, [(0, 1), (1, 0)])


def pick(array, index, axis):
    return lax.dynamic_index_in_dim(array, index, axis, keepdims=False)


def in_order(index, own, other, axis):
    first = jnp.where(index == 0, own, other)
    second = jnp.where(index == 0, other, own)
    return jnp.concatenate([first, second], axis=axis)


def ring_of(count):
    return list(range(0, count, 2)) + list(range(count - 1, 0, -2))


def ring_gather(part, rank):
    count = lax.axis_size("dp")
    ring = ring_of(count)
    place = [0] * count
    for position, device in enumerate(ring):
        place[device] = position
    onward = [(ring[i], ring[(i + 1) % count]) for i in range(count)]
    back = [(b, a) for a, b in onward]
    ring_table = jnp.array(ring, jnp.int32)
    here = jnp.array(place, jnp.int32)[rank]
    gathered = jnp.zeros((count,) + part.shape, part.dtype)
    gathered = lax.dynamic_update_index_in_dim(gathered, part, rank, 0)
    right, left = part, part
    for step in range(1, count // 2 + 1):
        right = lax.ppermute(right, "dp", onward)
        source = ring_table[(here - step) % count]
        gathered = lax.dynamic_update_index_in_dim(gathered, right, source, 0)
        if step < count - count // 2:
            left = lax.ppermute(left, "dp", back)
            source = ring_table[(here + step) % count]
            gathered = lax.dynamic_update_index_in_dim(gathered, left, source, 0)
    return gathered


def line_scatter(terms, place, axis):
    length = terms.shape[axis]
    count = 2 * length

    def term(index):
        return pick(terms, jnp.clip(index, 0, length - 1), axis).astype(F32)

    up = down = None
    for step in range(1, length):
        up_send = term(place + length - step)
        down_send = term(place - length + step)
        if step > 1:
            up_send = up_send + up.astype(F32)
            down_send = down_send + down.astype(F32)
        up_pairs = [
            (i, i + 2) for i in range(count - 2) if i // 2 <= step - 1
        ]
        down_pairs = [
            (i, i - 2) for i in range(2, count) if i // 2 >= length - step
        ]
        up = lax.ppermute(up_send.astype(BF16), "dp", up_pairs)
        down = lax.ppermute(down_send.astype(BF16), "dp", down_pairs)
    total = term(place)
    if length > 1:
        total = total + (up.astype(F32) + down.astype(F32))
    return total


def pair_scatter(terms, side, axis):
    count = lax.axis_size("dp")
    pairs = [(i, i ^ 1) for i in range(count)]
    arrived = lax.ppermute(pick(terms, 1 - side, axis).astype(BF16), "dp", pairs)
    return pick(terms, side, axis).astype(F32) + arrived.astype(F32)


def dp_scatter(terms, rank, axis, pair_first=True):
    shape = terms.shape
    half = shape[axis] // 2
    split = terms.reshape(shape[:axis] + (half, 2) + shape[axis + 1 :])
    if pair_first:
        return line_scatter(
            pair_scatter(split, rank % 2, axis + 1).astype(BF16), rank // 2, axis
        )
    return pair_scatter(line_scatter(split, rank // 2, axis).astype(BF16), rank % 2, axis)


def dp_sum(part):
    count = lax.axis_size("dp")
    distance = 1
    while distance < count:
        part = part + lax.ppermute(part, "dp", [(i, i ^ distance) for i in range(count)])
        distance *= 2
    return part


def rope_tables(positions, head_size):
    frequency = ROPE_BASE ** (-jnp.arange(0, head_size, 2, dtype=F32) / head_size)
    angles = positions.astype(F32)[:, None] * frequency[None, :]
    angles = jnp.concatenate([angles, angles], axis=1)
    return (jnp.cos(angles)[:, None, :], jnp.sin(angles)[:, None, :])


def rotate(values, cosine, sine):
    half_dim = values.shape[-1] // 2
    turned = jnp.concatenate([-values[..., half_dim:], values[..., :half_dim]], axis=-1)
    return values * cosine + turned * sine


def unrotate(cotangent, cosine, sine):
    half_dim = cotangent.shape[-1] // 2
    sine_part = cotangent * sine
    turned = jnp.concatenate([sine_part[..., half_dim:], -sine_part[..., :half_dim]], axis=-1)
    return cotangent * cosine + turned


def masked_scores(query, key, allowed):
    scores = jnp.einsum("qhd,sd->hqs", query, key, preferred_element_type=F32) * HEAD_DIM ** (-0.5)
    return jnp.where(allowed[None], scores, MASKED)


def shards(
    block_input,
    segment_ids,
    first_gain,
    qkv_weight,
    qkv_bias,
    output_weight,
    second_gain,
    gate_up_weight,
    down_weight,
    output_grad,
):
    count = lax.axis_size("dp")
    rank = lax.axis_index("dp")
    row = lax.axis_index("row")
    col = lax.axis_index("col")
    qkv_block = qkv_weight[0, 0]
    out_block = output_weight[0, 0]
    gate_up_block = gate_up_weight[0, 0]
    down_block = down_weight[0, 0]
    seq_len = segment_ids.shape[0]
    own_rows, half_width = block_input.shape
    model_width = 2 * half_width
    head_size = HEAD_DIM
    own_heads = HEADS // 4
    query_width = own_heads * head_size
    key_width = (KV_HEADS // 2) * head_size
    group_units = down_block.shape[0]
    own_units = group_units // 2
    segment = own_units // count

    def own_tokens(array):
        return lax.dynamic_slice_in_dim(array, row * own_rows, own_rows, 0)

    def other_tokens(array):
        return lax.dynamic_slice_in_dim(array, (1 - row) * own_rows, own_rows, 0)

    def gather_block(part):
        far = swap(part, "col")
        near = swap(part, "row")
        far_near = swap(far, "row")
        return jnp.concatenate(
            [in_order(row, part, near, 0), in_order(row, far, far_near, 0)], axis=1
        )

    def row_sum_own(partial_sum, kind):
        arrived = swap(other_tokens(partial_sum).astype(kind), "row")
        return own_tokens(partial_sum).astype(F32) + arrived.astype(F32)

    def qkv_columns(side):
        heads = lax.dynamic_slice_in_dim(qkv_block, side * query_width, query_width, 1)
        return jnp.concatenate([heads, qkv_block[:, 2 * query_width :]], axis=1)

    stream_bf = gather_block(block_input)
    qkv_own = jnp.concatenate([qkv_columns(col), swap(qkv_columns(1 - col), "col")], axis=0)
    bias = qkv_bias[0]
    bias_own = jnp.concatenate(
        [lax.dynamic_slice_in_dim(bias, col * query_width, query_width, 0), bias[2 * query_width :]]
    )
    gains = jnp.stack([first_gain, second_gain])
    gains = jnp.concatenate([gains, swap(gains, "col")], axis=1)

    out_far = swap(out_block, "col")
    out_wide = jnp.concatenate([out_block, out_far], axis=1)
    out_full = jnp.concatenate([out_wide, swap(out_wide, "row")], axis=0)

    feature_rows = half_width // count

    def unit_columns(array, side):
        split = array.reshape(array.shape[0], 2, count, 2, segment)
        return pick(split, side, 3).reshape(array.shape[0], 2 * own_units)

    gate_up_slice = lax.dynamic_slice_in_dim(gate_up_block, rank * feature_rows, feature_rows, 0)
    gate_up_far = ring_gather(swap(unit_columns(gate_up_slice, 1 - col), "col"), rank)
    gate_up_own = jnp.concatenate(
        [unit_columns(gate_up_block, col), gate_up_far.reshape(half_width, 2 * own_units)], axis=0
    )
    down_split = down_block.reshape(count, 2, segment, half_width)
    down_far = ring_gather(swap(pick(pick(down_split, rank, 0), 1 - col, 0), "col"), rank)
    down_own = jnp.concatenate(
        [
            pick(down_split, col, 1).reshape(own_units, half_width),
            down_far.reshape(own_units, half_width),
        ],
        axis=1,
    )
    grad_bf = gather_block(output_grad)

    position_index = jnp.arange(seq_len, dtype=jnp.int32)
    doc_first = jnp.concatenate([jnp.ones((1,), jnp.bool_), segment_ids[1:] != segment_ids[:-1]])
    positions = position_index - lax.cummax(jnp.where(doc_first, position_index, 0), axis=0)
    cosine, sine = rope_tables(positions, head_size)
    allowed = (position_index[None, :] <= position_index[:, None]) & (
        segment_ids[None, :] == segment_ids[:, None]
    )
    stream = stream_bf.astype(F32)
    first_scale = lax.rsqrt(jnp.sum(stream * stream, axis=1) / model_width + EPSILON)[:, None]
    first_normed = (stream * first_scale * gains[0]).astype(BF16)
    projected = dot(first_normed, qkv_own, 1, 0) + bias_own
    query = rotate(
        projected[:, :query_width].reshape(seq_len, own_heads, head_size), cosine, sine
    ).astype(BF16)
    key = rotate(
        projected[:, query_width : query_width + key_width].reshape(seq_len, 1, head_size),
        cosine,
        sine,
    ).astype(BF16)[:, 0]
    value = projected[:, query_width + key_width :].astype(BF16)
    scores = masked_scores(query, key, allowed)
    row_top = jnp.max(scores, axis=-1, keepdims=True)
    exponent = jnp.exp(scores - row_top)
    row_total = jnp.sum(exponent, axis=-1, keepdims=True)
    attn_probs = (exponent / row_total).astype(BF16)
    attended = (
        jnp.einsum("hqs,sd->qhd", attn_probs, value, preferred_element_type=F32)
        .reshape(seq_len, query_width)
        .astype(BF16)
    )
    log_total = row_top + jnp.log(row_total)
    attended_group = in_order(col, attended, swap(attended, "col"), 1)
    attended_full = jnp.concatenate([attended_group, swap(attended_group, "row")], axis=1)
    hidden_one = stream + dot(attended_full, out_full, 1, 0)
    second_scale = lax.rsqrt(jnp.sum(hidden_one * hidden_one, axis=1) / model_width + EPSILON)[
        :, None
    ]
    second_normed = (hidden_one * second_scale * gains[1]).astype(BF16)

    gate_up = dot(second_normed, gate_up_own, 1, 0)
    gate_part = gate_up[:, :own_units]
    up_part = gate_up[:, own_units:]
    sigmoid_gate = jax.nn.sigmoid(gate_part)
    activated = (gate_part * sigmoid_gate * up_part).astype(BF16)
    down_terms = dot(activated, grad_bf, 0, 0).astype(BF16).reshape(count, segment, model_width)
    down_sum = dp_scatter(down_terms, rank, 0)

    d_activated = dot(grad_bf, down_own, 1, 1)
    d_gate = (
        d_activated * up_part * (sigmoid_gate * (1.0 + gate_part * (1.0 - sigmoid_gate)))
    ).astype(BF16)
    d_up = (d_activated * gate_part * sigmoid_gate).astype(BF16)
    gate_terms = dot(second_normed, d_gate, 0, 0).astype(BF16)
    gate_sum = dp_scatter(gate_terms.reshape(2, count, feature_rows, own_units), rank, 1)
    up_terms = dot(second_normed, d_up, 0, 0).astype(BF16)
    up_sum = dp_scatter(up_terms.reshape(2, count, feature_rows, own_units), rank, 1)
    d_gate_up = jnp.concatenate([d_gate, d_up], axis=1)
    d_second_chip = row_sum_own(dot(d_gate_up, gate_up_own, 1, 1), BF16)
    d_second_far = swap(d_second_chip.astype(BF16), "col").astype(F32)
    d_second = d_second_chip + jnp.concatenate(
        [d_second_far[:, half_width:], d_second_far[:, :half_width]], axis=1
    )

    hidden_own = own_tokens(hidden_one)
    scale_own = own_tokens(second_scale)
    weighted = d_second * gains[1]
    inner = jnp.sum(weighted * hidden_own, axis=1, keepdims=True)
    d_hidden = own_tokens(grad_bf).astype(F32) + scale_own * (
        weighted - hidden_own * (scale_own * scale_own) * (inner / model_width)
    )
    second_gain_part = jnp.sum(
        d_second[:, :half_width] * hidden_own[:, :half_width] * scale_own, axis=0
    )
    d_hidden_low = d_hidden.astype(BF16)
    d_hidden_full = in_order(row, d_hidden_low, swap(d_hidden_low, "row"), 0)

    out_terms = dot(attended_group, d_hidden_full[:, :half_width], 0, 0).astype(BF16)
    out_sum = dp_scatter(out_terms.reshape(count, feature_rows, half_width), rank, 0)

    out_rows = lax.dynamic_slice_in_dim(out_full, col * query_width, query_width, 0)
    d_attended = dot(d_hidden_full, out_rows, 1, 1).astype(BF16)
    d_attended = d_attended.reshape(seq_len, own_heads, head_size)
    probs = jnp.exp(masked_scores(query, key, allowed) - log_total)
    probs_low = probs.astype(BF16)
    d_probs = jnp.einsum("qhd,sd->hqs", d_attended, value, preferred_element_type=F32)
    d_scores = (probs * (d_probs - jnp.sum(d_probs * probs, axis=-1, keepdims=True))).astype(BF16)
    scaling = head_size ** (-0.5)
    d_query = jnp.einsum("hqs,sd->qhd", d_scores, key, preferred_element_type=F32) * scaling
    d_key = jnp.einsum("hqs,qhd->sd", d_scores, query, preferred_element_type=F32) * scaling
    d_value = jnp.einsum("hqs,qhd->sd", probs_low, d_attended, preferred_element_type=F32)
    d_query = unrotate(d_query, cosine, sine).reshape(seq_len, query_width).astype(BF16)
    d_key = unrotate(d_key[:, None, :], cosine, sine)[:, 0]
    d_key_value = jnp.concatenate([d_key, d_value], axis=1)
    arrived = swap(jnp.concatenate([d_query, d_key_value.astype(BF16)], axis=1), "col")
    d_key_value = (d_key_value + arrived[:, query_width:].astype(F32)).astype(BF16)
    d_projected = jnp.concatenate(
        [in_order(col, d_query, arrived[:, :query_width], 1), d_key_value], axis=1
    )
    qkv_terms = dot(first_normed[:, :half_width], d_projected, 0, 0).astype(BF16)
    qkv_sum = dp_scatter(qkv_terms.reshape(count, feature_rows, -1), rank, 0)
    bias_part = jnp.sum(d_projected, axis=0, dtype=F32)
    d_first = row_sum_own(dot(d_projected, qkv_block, 1, 1), F32)
    stream_own = block_input.astype(F32)
    first_scale_own = own_tokens(first_scale)
    first_gain_part = jnp.sum(d_first * stream_own * first_scale_own, axis=0)
    weighted = d_first * first_gain
    inner = jnp.sum(weighted * stream_own, axis=1)
    inner = (inner + swap(inner, "col"))[:, None]
    input_grad = d_hidden[:, :half_width] + first_scale_own * (
        weighted - stream_own * (first_scale_own * first_scale_own) * (inner / model_width)
    )

    mlp_chip = row_sum_own(dot(activated, down_own, 1, 0), BF16)
    mlp_far = swap(mlp_chip[:, half_width:].astype(BF16), "col").astype(F32)
    block_output = (hidden_own[:, :half_width] + (mlp_chip[:, :half_width] + mlp_far)).astype(BF16)

    gain_parts = jnp.concatenate([first_gain_part, second_gain_part])
    gain_parts = gain_parts + swap(gain_parts, "row")
    small = dp_sum(jnp.concatenate([gain_parts, bias_part]))
    bias_width = bias.shape[0] // count
    bias_grad = lax.dynamic_slice_in_dim(small[model_width:], rank * bias_width, bias_width, 0)

    down_far_sum = swap(down_sum[:, half_width:].astype(BF16), "col").astype(F32)
    down_grad = in_order(col, down_sum[:, :half_width], down_far_sum, 0)
    gate_up_sum = jnp.stack([gate_sum, up_sum], axis=2)
    far_sum = swap(gate_up_sum[1].astype(BF16), "col").astype(F32)
    own_sum = gate_up_sum[0].reshape(feature_rows, 2, count, segment)
    far_sum = far_sum.reshape(feature_rows, 2, count, segment)
    gate_up_grad = jnp.stack(
        [jnp.where(col == 0, own_sum, far_sum), jnp.where(col == 0, far_sum, own_sum)], axis=3
    ).reshape(feature_rows, 2 * group_units)

    return (
        block_output,
        input_grad,
        small[:half_width],
        qkv_sum[None, None],
        bias_grad[None],
        out_sum[None, None],
        small[half_width:model_width],
        gate_up_grad[None, None],
        down_grad[None, None],
    )


def solution(mesh):
    placed = (
        P(("dp", "row"), "col"),
        P("dp"),
        P("col"),
        P("col", "row", None, None),
        P("row", None),
        P("row", "col", None, None),
        P("col"),
        P("col", "row", None, None),
        P("row", "col", None, None),
        P(("dp", "row"), "col"),
    )
    return jax.shard_map(
        shards,
        mesh=mesh,
        in_specs=placed,
        out_specs=(
            P(("dp", "row"), "col"),
            P(("dp", "row"), "col"),
            P("col"),
            P("col", "row", "dp", None),
            P("row", "dp"),
            P("row", "col", "dp", None),
            P("col"),
            P("col", "row", "dp", None),
            P("row", "col", "dp", None),
        ),
        check_vma=False,
    )
```

```python
import functools
import jax
import jax.numpy as jnp
from jax import lax
from jax.experimental import pallas as pl
from jax.experimental.pallas import tpu as pltpu
from jax.sharding import PartitionSpec as P

HEADS = 12
KV_HEADS = 2
HEAD_DIM = 128
EPSILON = 1e-06
ROPE_BASE = 1000000.0
MASKED = -1e30
F32 = jnp.float32
BF16 = jnp.bfloat16
VMEM_LIMIT = 60 * 1024 * 1024


def dot(left, right, left_dim, right_dim):
    return lax.dot_general(
        left, right, (((left_dim,), (right_dim,)), ((), ())), preferred_element_type=F32
    )


def params(*semantics):
    return pltpu.CompilerParams(
        dimension_semantics=semantics or None, vmem_limit_bytes=VMEM_LIMIT
    )


def cost(flops, moved):
    return pl.CostEstimate(flops=1, bytes_accessed=1, transcendentals=0)


def whole(shape):
    return pl.BlockSpec(shape, lambda *_: (0,) * len(shape))


ROW, COL, LOW, HIGH = range(4)
BITS = 2


def with_bit(index, place, value):
    return ((index >> place) << (place + 1)) | (value << place) | (index & ((1 << place) - 1))


def ordered(table, parts, columns=slice(None)):
    if len(parts) == 1:
        return parts[0][:, columns]
    first, second, first_other, second_other = [part[:, columns] for part in parts]
    high, low = table[HIGH] == 0, table[LOW] == 0
    return jnp.concatenate(
        [
            jnp.where(high, first, first_other),
            jnp.where(high, first_other, first),
            jnp.where(low, second, second_other),
            jnp.where(low, second_other, second),
        ],
        axis=0,
    )


def halves_of(segment, padded):
    first = padded // 2
    return ((0, first), (first, segment - first))


def units_kernel(count, segment, padded, halves, table, block_ref, *out_refs):
    rows = block_ref.shape[0]

    def write(side):
        for out_ref, half in zip(out_refs, halves):
            begin, width = halves_of(segment, padded)[half]
            parts = []
            for kind in range(2):
                for k in range(count):
                    start = ((kind * count + k) * 2 + side) * segment + begin
                    parts.append(block_ref[:, start : start + width])
                    if width < padded // 2:
                        parts.append(jnp.zeros((rows, padded // 2 - width), block_ref.dtype))
            out_ref[0] = jnp.concatenate(parts, axis=1)

    @pl.when(table[0] == 0)
    def _():
        write(0)

    @pl.when(table[0] != 0)
    def _():
        write(1)


def unit_columns(block, side, slots, count, rows, padded, halves=(0, 1)):
    columns = block.shape[1]
    segment = columns // (4 * count)
    units = padded * count
    steps = slots.shape[0]
    table = jnp.concatenate([side.reshape(1), slots]).astype(jnp.int32)
    return pl.pallas_call(
        functools.partial(units_kernel, count, segment, padded, halves),
        grid_spec=pltpu.PrefetchScalarGridSpec(
            num_scalar_prefetch=1,
            grid=(steps,),
            in_specs=[pl.BlockSpec((rows, columns), lambda i, t: (t[1 + i], 0))],
            out_specs=[pl.BlockSpec((1, rows, units), lambda i, t: (i, 0, 0))] * len(halves),
        ),
        out_shape=[jax.ShapeDtypeStruct((steps, rows, units), block.dtype)] * len(halves),
        compiler_params=params("arbitrary"),
        cost_estimate=cost(0, 4 * steps * rows * units * 2),
        name="unit_columns",
    )(table, block)


def unit_rows_kernel(segment, table, block_ref, out_ref):
    half, width = out_ref.shape[1], block_ref.shape[3]
    rows = block_ref[0, 0].astype(F32)
    out_ref[0, :, :width] = rows[:half].astype(out_ref.dtype)
    rest = jnp.concatenate([rows[half:], jnp.zeros((2 * half - segment, width), F32)], axis=0)
    out_ref[0, :, width:] = rest.astype(out_ref.dtype)


def unit_rows(block, side, ranks, count, padded):
    rows, width = block.shape
    segment = rows // (2 * count)
    steps = ranks.shape[0]
    table = jnp.concatenate([side.reshape(1), ranks]).astype(jnp.int32)
    return pl.pallas_call(
        functools.partial(unit_rows_kernel, segment),
        grid_spec=pltpu.PrefetchScalarGridSpec(
            num_scalar_prefetch=1,
            grid=(steps,),
            in_specs=[pl.BlockSpec((1, 1, segment, width), lambda i, t: (t[1 + i], t[0], 0, 0))],
            out_specs=pl.BlockSpec((1, padded // 2, 2 * width), lambda i, t: (i, 0, 0)),
        ),
        out_shape=jax.ShapeDtypeStruct((steps, padded // 2, 2 * width), block.dtype),
        compiler_params=params("arbitrary"),
        cost_estimate=cost(0, 4 * steps * segment * width),
        name="unit_rows",
    )(table, block.reshape(count, 2, segment, width))


def spread_kernel(count, segment, padded, table, own0_ref, own1_ref, far0_ref, far1_ref, out_ref):
    def write(sides):
        pieces = []
        half = padded // 2
        for kind in range(2):
            for k in range(count):
                for side in sides:
                    for ref, (_, width) in zip(side, halves_of(segment, padded)):
                        start = (kind * count + k) * half
                        pieces.append(ref[:, start : start + width].astype(F32))
        out_ref[...] = jnp.concatenate(pieces, axis=1)

    own, far = (own0_ref, own1_ref), (far0_ref, far1_ref)

    @pl.when(table[COL] == 0)
    def _():
        write((own, far))

    @pl.when(table[COL] != 0)
    def _():
        write((far, own))


def spread_columns(table, own, far, count, segment, padded):
    rows, units = own[0].shape
    step = rows // 3 if rows % 24 == 0 else rows
    part = pl.BlockSpec((step, units), lambda i, t: (i, 0))
    columns = 4 * count * segment
    return pl.pallas_call(
        functools.partial(spread_kernel, count, segment, padded),
        grid_spec=pltpu.PrefetchScalarGridSpec(
            num_scalar_prefetch=1,
            grid=(rows // step,),
            in_specs=[part] * 4,
            out_specs=pl.BlockSpec((step, columns), lambda i, t: (i, 0)),
        ),
        out_shape=jax.ShapeDtypeStruct((rows, columns), F32),
        compiler_params=params("arbitrary"),
        cost_estimate=cost(0, 28 * rows * units),
        name="spread_columns",
    )(table, *own, *far)


def project_kernel(
    width, table, own_ref, near_ref, far_ref, far_near_ref, gain_ref, weight_ref, part0_ref, part1_ref, part2_ref,
    part3_ref, bias_ref, cosine_ref, sine_ref, stream_ref, normed_ref, scale_ref, query_ref, key_ref, value_ref,
):
    half = pl.program_id(0) * 2 // pl.num_programs(0)
    mine = half == table[ROW]
    left = jnp.where(mine, own_ref[...], near_ref[...]).astype(F32)
    right = jnp.where(mine, far_ref[...], far_near_ref[...]).astype(F32)
    squares = jnp.sum(left * left, axis=1, keepdims=True) + jnp.sum(
        right * right, axis=1, keepdims=True
    )
    scale = lax.rsqrt(squares / (2 * width) + EPSILON)
    left_normed = (left * scale * gain_ref[:, :width]).astype(BF16)
    right_normed = (right * scale * gain_ref[:, width:]).astype(BF16)
    stream_ref[:, :width] = left.astype(BF16)
    stream_ref[:, width:] = right.astype(BF16)
    normed_ref[...] = left_normed
    scale_ref[...] = jnp.broadcast_to(scale, scale_ref.shape)
    far_weight = ordered(table, (part0_ref, part1_ref, part2_ref, part3_ref))
    projected = (
        dot(left_normed, weight_ref[...], 1, 0) + dot(right_normed, far_weight, 1, 0) + bias_ref[...]
    )
    cosine, sine = cosine_ref[...], sine_ref[...]

    def rotated(values):
        return (values * cosine + pltpu.roll(values, HEAD_DIM // 2, 1) * sine).astype(BF16)

    query_width = query_ref.shape[1]
    for start in range(0, query_width, HEAD_DIM):
        query_ref[:, start : start + HEAD_DIM] = rotated(projected[:, start : start + HEAD_DIM])
    key_ref[...] = rotated(projected[:, query_width : query_width + HEAD_DIM])
    value_ref[...] = projected[:, query_width + HEAD_DIM :].astype(BF16)


def project(table, own, near, far, far_near, gain, weight, far_parts, bias, cosine, sine):
    rows, width = own.shape
    seq_len = 2 * rows
    block = min(256, rows)
    per_half = rows // block
    out_width = weight.shape[1]
    query_width = out_width - 2 * HEAD_DIM
    part = pl.BlockSpec((block, width), lambda i, t: (i % per_half, 0))

    def tokens(columns):
        return pl.BlockSpec((block, columns), lambda i, t: (i, 0))

    return pl.pallas_call(
        functools.partial(project_kernel, width),
        grid_spec=pltpu.PrefetchScalarGridSpec(
            num_scalar_prefetch=1,
            grid=(seq_len // block,),
            in_specs=[part, part, part, part, whole((1, 2 * width)), whole(weight.shape)]
            + [whole((piece.shape[0], out_width)) for piece in far_parts]
            + [whole((1, out_width)), tokens(HEAD_DIM), tokens(HEAD_DIM)],
            out_specs=[
                tokens(2 * width), tokens(width), tokens(128),
                tokens(query_width), tokens(HEAD_DIM), tokens(HEAD_DIM),
            ],
        ),
        out_shape=[
            jax.ShapeDtypeStruct((seq_len, 2 * width), BF16),
            jax.ShapeDtypeStruct((seq_len, width), BF16),
            jax.ShapeDtypeStruct((seq_len, 128), F32),
            jax.ShapeDtypeStruct((seq_len, query_width), BF16),
            jax.ShapeDtypeStruct((seq_len, HEAD_DIM), BF16),
            jax.ShapeDtypeStruct((seq_len, HEAD_DIM), BF16),
        ],
        compiler_params=params("arbitrary"),
        cost_estimate=cost(4 * seq_len * width * out_width, 12 * seq_len * width),
        name="project",
    )(table, own, near, far, far_near, gain, weight, *far_parts, bias, cosine, sine)


def join_kernel(width, table, own_ref, near_ref, far_ref, far_near_ref, out_ref):
    mine = pl.program_id(0) * 2 // pl.num_programs(0) == table[ROW]
    out_ref[:, :width] = jnp.where(mine, own_ref[...], near_ref[...])
    out_ref[:, width:] = jnp.where(mine, far_ref[...], far_near_ref[...])


def join(table, own, near, far, far_near):
    rows, width = own.shape
    block = min(256, rows)
    per_half = rows // block
    part = pl.BlockSpec((block, width), lambda i, t: (i % per_half, 0))
    return pl.pallas_call(
        functools.partial(join_kernel, width),
        grid_spec=pltpu.PrefetchScalarGridSpec(
            num_scalar_prefetch=1,
            grid=(2 * rows // block,),
            in_specs=[part] * 4,
            out_specs=pl.BlockSpec((block, 2 * width), lambda i, t: (i, 0)),
        ),
        out_shape=jax.ShapeDtypeStruct((2 * rows, 2 * width), own.dtype),
        compiler_params=params("arbitrary"),
        cost_estimate=cost(0, 16 * rows * width),
        name="join",
    )(table, own, near, far, far_near)


def block_probs(query, key, seg_col, seg_row, start, stop):
    scores = dot(query, key, 1, 1) * HEAD_DIM ** (-0.5)
    rows = stop - start
    query_index = start + lax.broadcasted_iota(jnp.int32, (rows, stop), 0)
    key_index = lax.broadcasted_iota(jnp.int32, (rows, stop), 1)
    allowed = (key_index <= query_index) & (seg_col == seg_row)
    scores = jnp.where(allowed, scores, MASKED)
    exponent = jnp.exp(scores - jnp.max(scores, axis=1, keepdims=True))
    return exponent / jnp.sum(exponent, axis=1, keepdims=True)


def attend_kernel(block, query_ref, key_ref, value_ref, seg_col_ref, seg_row_ref, out_ref):
    for start in range(0, query_ref.shape[0], block):
        stop = start + block
        probs = block_probs(
            query_ref[start:stop], key_ref[:stop], seg_col_ref[start:stop], seg_row_ref[:, :stop], start, stop
        )
        out_ref[start:stop] = dot(probs.astype(BF16), value_ref[:stop], 1, 0).astype(BF16)


def attend(query, key, value, seg_col, seg_row):
    seq_len, width = query.shape
    head = pl.BlockSpec((seq_len, HEAD_DIM), lambda h: (0, h))
    shared = whole((seq_len, HEAD_DIM))
    return pl.pallas_call(
        functools.partial(attend_kernel, 256),
        grid=(width // HEAD_DIM,),
        in_specs=[head, shared, shared, whole((seq_len, 1)), whole((1, seq_len))],
        out_specs=head,
        out_shape=jax.ShapeDtypeStruct(query.shape, BF16),
        compiler_params=params("arbitrary"),
        cost_estimate=cost(6 * seq_len * seq_len * width, 8 * seq_len * width),
        name="attend",
    )(query, key, value, seg_col, seg_row)


def attend_back_kernel(
    block, width, table, query_ref, key_ref, value_ref, seg_col_ref, seg_row_ref, own_ref, near_ref, weight_ref,
    far_weight_ref, cosine_ref, sine_ref, sent_ref, key_value_ref,
):
    scaling = HEAD_DIM ** (-0.5)
    own_rows = own_ref.shape[0]

    @pl.when(pl.program_id(0) == 0)
    def _():
        key_value_ref[...] = jnp.zeros_like(key_value_ref)

    for start in range(0, query_ref.shape[0], block):
        stop = start + block
        mine = table[ROW] == start // own_rows
        place = slice(start % own_rows, start % own_rows + block)
        d_hidden = jnp.where(mine, own_ref[place], near_ref[place])
        grad = (
            dot(d_hidden[:, :width], weight_ref[...], 1, 1)
            + dot(d_hidden[:, width:], far_weight_ref[...], 1, 1)
        ).astype(BF16)
        query = query_ref[start:stop]
        key, value = key_ref[:stop], value_ref[:stop]
        probs = block_probs(
            query, key, seg_col_ref[start:stop], seg_row_ref[:, :stop], start, stop
        )
        d_probs = dot(grad, value, 1, 1)
        d_scores = probs * (d_probs - jnp.sum(d_probs * probs, axis=1, keepdims=True))
        d_scores = d_scores.astype(BF16)
        d_query = dot(d_scores, key, 1, 0) * scaling
        turned = pltpu.roll(d_query * sine_ref[start:stop], HEAD_DIM // 2, 1)
        sent_ref[start:stop] = (d_query * cosine_ref[start:stop] + turned).astype(BF16)
        key_value_ref[:stop, :HEAD_DIM] += dot(d_scores, query, 0, 0) * scaling
        key_value_ref[:stop, HEAD_DIM:] += dot(probs.astype(BF16), grad, 0, 0)

    @pl.when(pl.program_id(0) == pl.num_programs(0) - 1)
    def _():
        d_key = key_value_ref[:, :HEAD_DIM]
        turned = pltpu.roll(d_key * sine_ref[...], HEAD_DIM // 2, 1)
        key_value_ref[:, :HEAD_DIM] = d_key * cosine_ref[...] + turned


def attend_back(table, query, key, value, seg_col, seg_row, own, near, weight, far_weight, cosine, sine):
    seq_len, width = query.shape
    features = weight.shape[1]
    heads = width // HEAD_DIM
    head = pl.BlockSpec((seq_len, HEAD_DIM), lambda h, t: (0, h))
    rows = pl.BlockSpec((HEAD_DIM, features), lambda h, t: (heads * t[COL] + h, 0))
    shared = whole((seq_len, HEAD_DIM))
    return pl.pallas_call(
        functools.partial(attend_back_kernel, 256, features),
        grid_spec=pltpu.PrefetchScalarGridSpec(
            num_scalar_prefetch=1,
            grid=(heads,),
            in_specs=[
                head, shared, shared, whole((seq_len, 1)), whole((1, seq_len)), whole(own.shape), whole(near.shape),
                rows, rows, shared, shared,
            ],
            out_specs=[head, whole((seq_len, 2 * HEAD_DIM))],
        ),
        out_shape=[
            jax.ShapeDtypeStruct(query.shape, BF16),
            jax.ShapeDtypeStruct((seq_len, 2 * HEAD_DIM), F32),
        ],
        compiler_params=params("arbitrary"),
        cost_estimate=cost(12 * seq_len * seq_len * width, 12 * seq_len * width),
        name="attend_back",
    )(table, query, key, value, seg_col, seg_row, own, near, weight, far_weight, cosine, sine)


def residual_kernel(
    table, stream_ref, own_ref, far_ref, near_ref, near_far_ref, own_w_ref, far_w_ref, near_w_ref, near_far_w_ref,
    gain_ref, hidden_ref, normed_ref, scale_ref, group_ref,
):
    first = table[COL] == 0
    part = own_ref.shape[1]
    group = [jnp.where(first, own_ref[...], far_ref[...]), jnp.where(first, far_ref[...], own_ref[...])]
    other = [jnp.where(first, near_ref[...], near_far_ref[...]), jnp.where(first, near_far_ref[...], near_ref[...])]
    group_ref[:, :part] = group[0]
    group_ref[:, part:] = group[1]
    width = own_w_ref.shape[1]
    halves = []
    for index, (mine, theirs) in enumerate(((own_w_ref, near_w_ref), (far_w_ref, near_far_w_ref))):
        total = stream_ref[:, index * width : (index + 1) * width].astype(F32)
        for place in range(2):
            rows = slice(place * part, (place + 1) * part)
            total = total + dot(group[place], mine[rows], 1, 0)
            total = total + dot(other[place], theirs[rows], 1, 0)
        halves.append(total)
    squares = sum(jnp.sum(total * total, axis=1, keepdims=True) for total in halves)
    scale = lax.rsqrt(squares / (2 * width) + EPSILON)
    scale_ref[...] = jnp.broadcast_to(scale, scale_ref.shape)
    for index, total in enumerate(halves):
        columns = slice(index * width, (index + 1) * width)
        hidden_ref[:, columns] = total
        normed_ref[:, columns] = (total * scale * gain_ref[:, columns]).astype(BF16)


def residual(table, stream, own, far, near, near_far, weights, gain):
    seq_len, width = stream.shape
    part = own.shape[1]
    block = min(256, seq_len)

    def tokens(columns):
        return pl.BlockSpec((block, columns), lambda i, t: (i, 0))

    return pl.pallas_call(
        residual_kernel,
        grid_spec=pltpu.PrefetchScalarGridSpec(
            num_scalar_prefetch=1,
            grid=(seq_len // block,),
            in_specs=[tokens(width)]
            + [tokens(part)] * 4
            + [whole(weights[0].shape)] * 4
            + [whole((1, width))],
            out_specs=[tokens(width), tokens(width), tokens(128), tokens(2 * part)],
        ),
        out_shape=[
            jax.ShapeDtypeStruct((seq_len, width), F32),
            jax.ShapeDtypeStruct((seq_len, width), BF16),
            jax.ShapeDtypeStruct((seq_len, 128), F32),
            jax.ShapeDtypeStruct((seq_len, 2 * part), BF16),
        ],
        compiler_params=params("arbitrary"),
        cost_estimate=cost(2 * seq_len * width * width, 14 * seq_len * width),
        name="residual",
    )(table, stream, own, far, near, near_far, *weights, gain)


def activate_kernel(width, table, normed_ref, own_gate_ref, own_up_ref, *refs):
    (act_ref, gate_factor_ref, up_factor_ref), refs = refs[-3:], refs[:-3]
    gate_parts, up_parts = refs[: len(refs) // 2], refs[len(refs) // 2 :]
    left, right = normed_ref[:, :width], normed_ref[:, width:]
    gate = dot(left, own_gate_ref[...], 1, 0) + dot(right, ordered(table, gate_parts), 1, 0)
    up = dot(left, own_up_ref[...], 1, 0) + dot(right, ordered(table, up_parts), 1, 0)
    sigmoid = jax.nn.sigmoid(gate)
    silu = gate * sigmoid
    act_ref[...] = (silu * up).astype(BF16)
    gate_factor_ref[...] = (up * (sigmoid * (1.0 + gate * (1.0 - sigmoid)))).astype(BF16)
    up_factor_ref[...] = silu.astype(BF16)


def tile_of(units):
    return next(t for t in (384, 256, 128, units) if units % t == 0)


def activate(table, normed, own, far_parts):
    seq_len, width = normed.shape
    units = own.shape[1] // 2
    tile = tile_of(units)
    steps = units // tile

    def gate(rows):
        return pl.BlockSpec((rows, tile), lambda j, t: (0, j))

    def up(rows):
        return pl.BlockSpec((rows, tile), lambda j, t: (0, steps + j))

    rows = far_parts[0].shape[0]
    out = pl.BlockSpec((seq_len, tile), lambda j, t: (0, j))
    return pl.pallas_call(
        functools.partial(activate_kernel, width // 2),
        grid_spec=pltpu.PrefetchScalarGridSpec(
            num_scalar_prefetch=1,
            grid=(steps,),
            in_specs=[whole(normed.shape), gate(width // 2), up(width // 2)]
            + [gate(rows)] * len(far_parts)
            + [up(rows)] * len(far_parts),
            out_specs=[out] * 3,
        ),
        out_shape=[jax.ShapeDtypeStruct((seq_len, units), BF16)] * 3,
        compiler_params=params("arbitrary"),
        cost_estimate=cost(4 * seq_len * width * units, 6 * seq_len * units + 4 * width * units),
        name="activate",
    )(table, normed, own, own, *far_parts, *far_parts)


def activate_back_kernel(tile, width, table, grad_ref, own_ref, *refs):
    part_refs, (gate_factor_ref, up_factor_ref, d_gate_ref, d_up_ref, far_scr) = refs[:4], refs[4:]

    @pl.when(pl.program_id(0) == 0)
    def _():
        far_scr[...] = ordered(table, part_refs)

    far = far_scr[pl.ds(pl.multiple_of(pl.program_id(0) * tile, tile), tile)]
    d_act = dot(grad_ref[:, :width], own_ref[...], 1, 1) + dot(grad_ref[:, width:], far, 1, 1)
    d_gate_ref[...] = (d_act * gate_factor_ref[...].astype(F32)).astype(BF16)
    d_up_ref[...] = (d_act * up_factor_ref[...].astype(F32)).astype(BF16)


def activate_back(table, grad, own, far_parts, half, gate_factor, up_factor):
    seq_len, width = grad.shape
    units = own.shape[0]
    tile = tile_of(units)
    weight = pl.BlockSpec((tile, width // 2), lambda j, t: (j, half))
    out = pl.BlockSpec((seq_len, tile), lambda j, t: (0, j))
    return pl.pallas_call(
        functools.partial(activate_back_kernel, tile, width // 2),
        grid_spec=pltpu.PrefetchScalarGridSpec(
            num_scalar_prefetch=1,
            grid=(units // tile,),
            in_specs=[whole(grad.shape), weight]
            + [pl.BlockSpec((piece.shape[0], width // 2), lambda j, t: (0, half)) for piece in far_parts]
            + [out, out],
            out_specs=[out] * 2,
            scratch_shapes=[pltpu.VMEM((units, width // 2), BF16)],
        ),
        out_shape=[jax.ShapeDtypeStruct((seq_len, units), BF16)] * 2,
        compiler_params=params("arbitrary"),
        cost_estimate=cost(2 * seq_len * width * units, 8 * seq_len * units + 2 * width * units),
        name="activate_back",
    )(table, grad, own, *far_parts, gate_factor, up_factor)


def down_kernel(halves, table, *refs):
    act_refs, own_refs, part_refs = refs[:halves], refs[halves : halves + 1], refs[halves + 1 : -3]
    own_out_ref, other_out_ref, total_scr = refs[-3:]

    def write(weights):
        total_scr[...] = sum(dot(act[...], weight, 1, 0) for act, weight in zip(act_refs, weights))
        rows = own_out_ref.shape[0]
        own_out_ref[...] = total_scr[pl.ds(pl.multiple_of(table[ROW] * rows, rows), rows)]
        other = pl.multiple_of((1 - table[ROW]) * rows, rows)
        other_out_ref[...] = total_scr[pl.ds(other, rows)].astype(BF16)

    def write_halves(weight_refs):
        width = own_out_ref.shape[1]
        write(
            [ordered(table, weight_refs, slice(half * width, (half + 1) * width)) for half in range(halves)]
        )

    @pl.when(pl.program_id(0) == 0)
    def _():
        write_halves(own_refs)

    @pl.when(pl.program_id(0) == 1)
    def _():
        write_halves(part_refs)


def down(table, acts, own, far_parts):
    seq_len, units = acts[0].shape
    features = own.shape[1] // 2
    parts = far_parts
    return pl.pallas_call(
        functools.partial(down_kernel, len(acts)),
        grid_spec=pltpu.PrefetchScalarGridSpec(
            num_scalar_prefetch=1,
            grid=(2,),
            in_specs=[whole(array.shape) for array in (*acts, own, *parts)],
            out_specs=[pl.BlockSpec((seq_len // 2, features), lambda j, t: (0, j))] * 2,
            scratch_shapes=[pltpu.VMEM((seq_len, features), F32)],
        ),
        out_shape=[
            jax.ShapeDtypeStruct((seq_len // 2, 2 * features), F32),
            jax.ShapeDtypeStruct((seq_len // 2, 2 * features), BF16),
        ],
        compiler_params=params("arbitrary"),
        cost_estimate=cost(
            4 * len(acts) * seq_len * units * features, 8 * seq_len * features + 8 * units * (seq_len + features)
        ),
        name="down",
    )(table, *acts, own, *parts)


def split_product(table, left, rights, tile, groups, count, bits):
    seq_len, height = left.shape
    rows = height // (groups * count)
    columns = sum(right.shape[1] for right in rights)
    steps = [right.shape[1] // tile for right in rights]
    starts = [sum(steps[:index]) for index in range(len(rights))]

    def kernel(table, left_ref, *refs):
        right_refs, out_refs, total_scr = refs[: len(rights)], refs[len(rights) : -1], refs[-1]
        step = pl.program_id(0)
        for right_ref, start, length in zip(right_refs, starts, steps):

            @pl.when((step >= start) & (step < start + length))
            def _():
                total_scr[...] = dot(left_ref[...], right_ref[...], 0, 0)

        for group, bit in enumerate(bits):
            side = table[BITS + bit]
            for out_ref, value in ((out_refs[2 * group], 1 - side), (out_refs[2 * group + 1], side)):
                for index in range(count // 2):
                    begin = (group * count + with_bit(index, bit, value)) * rows
                    if rows % 8 == 0:
                        begin = pl.multiple_of(begin, 8)
                    out_ref[index] = total_scr[pl.ds(begin, rows)].astype(BF16)

    def right_spec(start, length):
        return pl.BlockSpec((seq_len, tile), lambda i, t: (0, jnp.clip(i - start, 0, length - 1)))

    return pl.pallas_call(
        kernel,
        grid_spec=pltpu.PrefetchScalarGridSpec(
            num_scalar_prefetch=1,
            grid=(sum(steps),),
            in_specs=[whole(left.shape)]
            + [right_spec(start, length) for start, length in zip(starts, steps)],
            out_specs=[pl.BlockSpec((count // 2, rows, tile), lambda i, t: (0, 0, i))] * (2 * groups),
            scratch_shapes=[pltpu.VMEM((height, tile), F32)],
        ),
        out_shape=[jax.ShapeDtypeStruct((count // 2, rows, columns), BF16)] * (2 * groups),
        compiler_params=params("arbitrary"),
        cost_estimate=cost(
            2 * seq_len * height * columns, 2 * (seq_len * (height + columns) + height * columns)
        ),
        name="split_product",
    )(table, left, *rights)


def relay_kernel(table, kept_sent_ref, arrived_sent_ref, kept_ref, arrived_ref, sent_out_ref, kept_out_ref):
    sent_out_ref[...] = (kept_sent_ref[...].astype(F32) + arrived_sent_ref[...].astype(F32)).astype(BF16)
    kept_out_ref[...] = (kept_ref[...].astype(F32) + arrived_ref[...].astype(F32)).astype(BF16)


def relay(table, kept, arrived, place, bit):
    count, rows, columns = kept.shape

    def block(sent):
        def index(i, t):
            value = t[BITS + bit]
            return (with_bit(i, place, 1 - value if sent else value), 0, 0)

        return pl.BlockSpec((1, rows, columns), index)

    out = pl.BlockSpec((1, rows, columns), lambda i, t: (i, 0, 0))
    return pl.pallas_call(
        relay_kernel,
        grid_spec=pltpu.PrefetchScalarGridSpec(
            num_scalar_prefetch=1,
            grid=(count // 2,),
            in_specs=[block(True), block(True), block(False), block(False)],
            out_specs=[out, out],
        ),
        out_shape=[jax.ShapeDtypeStruct((count // 2, rows, columns), BF16)] * 2,
        compiler_params=params("arbitrary"),
        cost_estimate=cost(0, 6 * count * rows * columns),
        name="relay",
    )(table, kept, arrived, kept, arrived)


def normed_grad_kernel(halves, steps, tile, counts, table, *refs):
    d_refs, own_refs, refs = refs[: 2 * halves], refs[2 * halves : 3 * halves], refs[3 * halves :]
    part_refs = []
    for parts in counts:
        part_refs.append(refs[:parts])
        refs = refs[parts:]
    own_out_ref, other_out_ref, *far_scrs, total_scr = refs
    units = d_refs[0].shape[1]

    @pl.when(pl.program_id(0) == 0)
    def _():
        for half in range(halves):
            far_scrs[half][...] = ordered(table, part_refs[half])

    def write(weights):
        total = None
        for half in range(halves):
            for kind in range(2):
                term = dot(
                    d_refs[2 * half + kind][...], weights[half][:, kind * units : (kind + 1) * units], 1, 1
                )
                total = term if total is None else total + term
        total_scr[...] = total
        rows = own_out_ref.shape[0]
        own_out_ref[...] = total_scr[pl.ds(pl.multiple_of(table[ROW] * rows, rows), rows)]
        other = pl.multiple_of((1 - table[ROW]) * rows, rows)
        other_out_ref[...] = total_scr[pl.ds(other, rows)].astype(BF16)

    @pl.when(pl.program_id(0) < steps)
    def _():
        write(own_refs)

    @pl.when(pl.program_id(0) >= steps)
    def _():
        start = pl.multiple_of((pl.program_id(0) - steps) * tile, tile)
        write([scr.at[pl.ds(start, tile)] for scr in far_scrs])


def normed_grad(table, d_parts, own, far_parts):
    seq_len, units = d_parts[0].shape
    features = own[0].shape[0]
    tile = 256
    steps = features // tile
    halves = len(own)
    parts = [piece for half in far_parts for piece in half]
    own_spec = pl.BlockSpec((tile, 2 * units), lambda j, t: (jnp.minimum(j, steps - 1), 0))
    return pl.pallas_call(
        functools.partial(normed_grad_kernel, halves, steps, tile, [len(half) for half in far_parts]),
        grid_spec=pltpu.PrefetchScalarGridSpec(
            num_scalar_prefetch=1,
            grid=(2 * steps,),
            in_specs=[whole((seq_len, units))] * (2 * halves)
            + [own_spec] * halves
            + [whole(piece.shape) for piece in parts],
            out_specs=[pl.BlockSpec((seq_len // 2, tile), lambda j, t: (0, j))] * 2,
            scratch_shapes=[pltpu.VMEM((features, 2 * units), BF16)] * halves
            + [pltpu.VMEM((seq_len, tile), F32)],
        ),
        out_shape=[
            jax.ShapeDtypeStruct((seq_len // 2, 2 * features), F32),
            jax.ShapeDtypeStruct((seq_len // 2, 2 * features), BF16),
        ],
        compiler_params=params("arbitrary"),
        cost_estimate=cost(
            8 * seq_len * features * units * halves, 8 * units * halves * (seq_len + features)
        ),
        name="normed_grad",
    )(table, *d_parts, *own, *parts)


def chip_sum_kernel(own_ref, near_ref, out_ref, low_ref):
    total = own_ref[...] + near_ref[...].astype(F32)
    out_ref[...] = total
    low_ref[...] = total.astype(BF16)


def chip_sum(own, near):
    rows, width = own.shape
    block = pl.BlockSpec((rows // 4, width), lambda i: (i, 0))
    return pl.pallas_call(
        chip_sum_kernel,
        grid=(4,),
        in_specs=[block, block],
        out_specs=[block, block],
        out_shape=[jax.ShapeDtypeStruct(own.shape, F32), jax.ShapeDtypeStruct(own.shape, BF16)],
        compiler_params=params("arbitrary"),
        cost_estimate=cost(0, 12 * rows * width),
        name="chip_sum",
    )(own, near)


def norm_back_kernel(
    width, table, chip_ref, far_ref, hidden_ref, scale_ref, grad_ref, gain_ref, out_ref, low_ref, gain_grad_ref
):
    @pl.when(pl.program_id(0) == 0)
    def _():
        gain_grad_ref[...] = jnp.zeros_like(gain_grad_ref)

    far = far_ref[...].astype(F32)
    d_left = chip_ref[:, :width] + far[:, width:]
    d_right = chip_ref[:, width:] + far[:, :width]
    left, right = hidden_ref[:, :width], hidden_ref[:, width:]
    scale = scale_ref[:, :1]
    gain_grad_ref[...] += jnp.sum(d_left * left * scale, axis=0, keepdims=True)
    left_weighted, right_weighted = d_left * gain_ref[:, :width], d_right * gain_ref[:, width:]
    inner = jnp.sum(left_weighted * left, axis=1, keepdims=True) + jnp.sum(
        right_weighted * right, axis=1, keepdims=True
    )
    factor = scale * scale * (inner / (2 * width))
    d_left = grad_ref[:, :width].astype(F32) + scale * (left_weighted - left * factor)
    d_right = grad_ref[:, width:].astype(F32) + scale * (right_weighted - right * factor)
    out_ref[...] = d_left
    low_ref[:, :width] = d_left.astype(BF16)
    low_ref[:, width:] = d_right.astype(BF16)


def norm_back(table, chip, far, hidden, scale, grad, gain):
    rows, width = chip.shape
    block = rows // 4

    def own(columns):
        return pl.BlockSpec((block, columns), lambda i, t: (i, 0))

    def tokens(columns):
        return pl.BlockSpec((block, columns), lambda i, t: (4 * t[ROW] + i, 0))

    return pl.pallas_call(
        functools.partial(norm_back_kernel, width // 2),
        grid_spec=pltpu.PrefetchScalarGridSpec(
            num_scalar_prefetch=1,
            grid=(4,),
            in_specs=[own(width), own(width), tokens(width), tokens(128), tokens(width), whole((1, width))],
            out_specs=[own(width // 2), own(width), whole((1, width // 2))],
        ),
        out_shape=[
            jax.ShapeDtypeStruct((rows, width // 2), F32),
            jax.ShapeDtypeStruct((rows, width), BF16),
            jax.ShapeDtypeStruct((1, width // 2), F32),
        ],
        compiler_params=params("arbitrary"),
        cost_estimate=cost(0, 20 * rows * width),
        name="norm_back",
    )(table, chip, far, hidden, scale, grad, gain)


def project_back_kernel(
    count, bit, query_width, table, query_ref, key_value_ref, arrived_ref, normed_ref, weight_ref,
    sent_ref, kept_ref, own_ref, other_ref, bias_ref, d_scr, total_scr,
):
    first = table[COL] == 0
    own, far = query_ref[...], arrived_ref[:, :query_width]
    d_scr[:, :query_width] = jnp.where(first, own, far)
    d_scr[:, query_width : 2 * query_width] = jnp.where(first, far, own)
    d_key_value = key_value_ref[...] + arrived_ref[:, query_width:].astype(F32)
    d_scr[:, 2 * query_width :] = d_key_value.astype(BF16)
    d_projected = d_scr[...]
    bias_ref[...] = jnp.sum(d_projected.astype(F32), axis=0, keepdims=True)
    total_scr[...] = dot(normed_ref[...], d_projected, 0, 0)
    rows = sent_ref.shape[1]
    side = table[BITS + bit]
    for out_ref, value in ((sent_ref, 1 - side), (kept_ref, side)):
        for index in range(count // 2):
            start = with_bit(index, bit, value) * rows
            if rows % 8 == 0:
                start = pl.multiple_of(start, 8)
            out_ref[index] = total_scr[pl.ds(start, rows)].astype(BF16)
    tokens = own_ref.shape[0]
    for out_ref, half in ((own_ref, table[ROW]), (other_ref, 1 - table[ROW])):
        d_half = d_scr[pl.ds(pl.multiple_of(half * tokens, tokens), tokens)]
        out_ref[...] = dot(d_half, weight_ref[...], 1, 1)


def project_back(table, d_query, d_key_value, arrived, normed, weight, count, bit):
    seq_len, query_width = d_query.shape
    width, columns = weight.shape
    rows = width // count
    return pl.pallas_call(
        functools.partial(project_back_kernel, count, bit, query_width),
        grid_spec=pltpu.PrefetchScalarGridSpec(
            num_scalar_prefetch=1,
            grid=(1,),
            in_specs=[
                whole(array.shape) for array in (d_query, d_key_value, arrived, normed, weight)
            ],
            out_specs=[
                whole((count // 2, rows, columns)), whole((count // 2, rows, columns)),
                whole((seq_len // 2, width)), whole((seq_len // 2, width)), whole((1, columns)),
            ],
            scratch_shapes=[pltpu.VMEM((seq_len, columns), BF16), pltpu.VMEM((width, columns), F32)],
        ),
        out_shape=[
            jax.ShapeDtypeStruct((count // 2, rows, columns), BF16),
            jax.ShapeDtypeStruct((count // 2, rows, columns), BF16),
            jax.ShapeDtypeStruct((seq_len // 2, width), F32),
            jax.ShapeDtypeStruct((seq_len // 2, width), F32),
            jax.ShapeDtypeStruct((1, columns), F32),
        ],
        compiler_params=params("arbitrary"),
        cost_estimate=cost(4 * seq_len * width * columns, 8 * seq_len * columns),
        name="project_back",
    )(table, d_query, d_key_value, arrived, normed, weight)


def swap(part, axis_name):
    return lax.ppermute(part, axis_name, [(0, 1), (1, 0)])


def dp_swap(part, bit):
    count = lax.axis_size("dp")
    return lax.ppermute(part, "dp", [(i, i ^ (1 << bit)) for i in range(count)])


def after(value, *earlier):
    return lax.optimization_barrier((value,) + earlier)[0]


def pick(array, index, axis):
    return lax.dynamic_index_in_dim(array, index, axis, keepdims=False)


def in_order(index, own, other, axis):
    first = jnp.where(index == 0, own, other)
    second = jnp.where(index == 0, other, own)
    return jnp.concatenate([first, second], axis=axis)


def quad_slots(rank):
    low, high = rank % 2, rank // 2 % 2
    return jnp.stack([2 * high + low, 4 + 2 * low + high])


class Line:
    def __init__(self):
        self.last = ()

    def step(self, value):
        return after(value, *self.last) if self.last else value

    def mark(self, *values):
        self.last = values


class Quad:
    def __init__(self, part, rank):
        self.part = part
        self.low, self.high = rank % 2, rank // 2 % 2

    def first_round(self, line):
        part = line.step(self.part)
        self.sent = lax.optimization_barrier((part[0], part[1]))
        line.mark(*self.sent)
        self.arriving = dp_swap(self.sent[0], 0), dp_swap(self.sent[1], 1)

    def second_round(self, line):
        arrived = [line.step(value) for value in self.arriving]
        pairs = lax.optimization_barrier(
            (in_order(self.low, self.sent[0], arrived[0], 0), in_order(self.high, self.sent[1], arrived[1], 0))
        )
        line.mark(*pairs)
        self.parts = [*pairs, dp_swap(pairs[0], 1), dp_swap(pairs[1], 0)]
        return self.parts


def laid_out(parts, rank):
    low, high = rank % 2, rank // 2 % 2
    return jnp.concatenate(
        [in_order(high, parts[0], parts[2], 0), in_order(low, parts[1], parts[3], 0)], axis=0
    )


class Scatter:
    def __init__(self, table, sent, kept, order, line):
        self.table, self.kept = table, kept
        bits = lax.axis_size("dp").bit_length() - 1
        self.order = list(order) + [bit for bit in range(bits) if bit not in order]
        self.left = list(range(bits))
        self.pass_on(sent, line)

    def pass_on(self, sent, line):
        bit = self.order.pop(0)
        self.left.remove(bit)
        self.arriving = dp_swap(line.step(sent), bit)

    def relay(self, line):
        bit = self.order[0]
        sent, self.kept = relay(
            self.table, self.kept, line.step(self.arriving), self.left.index(bit), bit
        )
        line.mark(sent)
        self.pass_on(sent, line)

    def finish(self, line):
        while self.order:
            self.relay(line)
        return self.kept[0].astype(F32) + self.arriving[0].astype(F32)


def dp_sum(part):
    for bit in range(lax.axis_size("dp").bit_length() - 1):
        part = part + dp_swap(part, bit)
    return part


def shards(
    block_input,
    segment_ids,
    first_gain,
    qkv_weight,
    qkv_bias,
    output_weight,
    second_gain,
    gate_up_weight,
    down_weight,
    output_grad,
):
    count = lax.axis_size("dp")
    rank = lax.axis_index("dp")
    row = lax.axis_index("row")
    col = lax.axis_index("col")
    qkv_block = qkv_weight[0, 0]
    out_block = output_weight[0, 0]
    gate_up_block = gate_up_weight[0, 0]
    down_block = down_weight[0, 0]
    seq_len = segment_ids.shape[0]
    own_rows, half_width = block_input.shape
    model_width = 2 * half_width
    query_width = HEADS // 4 * HEAD_DIM
    own_units = down_block.shape[0] // 2
    segment = own_units // count
    step = max(16, 128 // count)
    padded = pl.cdiv(segment, 2 * step) * 2 * step
    feature_rows = half_width // count
    slot_rows = half_width // 8
    slots = quad_slots(rank)
    bits = count.bit_length() - 1

    def own_tokens(array):
        return lax.dynamic_slice_in_dim(array, row * own_rows, own_rows, 0)

    def slot_pair(array):
        parts = array.reshape((8, array.shape[0] // 8) + array.shape[1:])
        return jnp.stack([pick(parts, slots[0], 0), pick(parts, slots[1], 0)])

    table = jnp.stack([row, col] + [(rank >> bit) & 1 for bit in range(bits)]).astype(jnp.int32)
    line = Line()
    half_rows = padded // 2
    pair_first, line_first = [0, 1, 2], [1, 2, 0]

    def qkv_columns(side):
        heads = lax.dynamic_slice_in_dim(qkv_block, side * query_width, query_width, 1)
        return jnp.concatenate([heads, qkv_block[:, 2 * query_width :]], axis=1)

    gains = jnp.stack([first_gain, second_gain])
    gains = jnp.concatenate([gains, swap(gains, "col")], axis=1)
    early_send = slot_pair(jnp.concatenate([qkv_columns(1 - col), out_block], axis=1))
    early_quad = Quad(swap(early_send, "col"), rank)
    qkv_own = qkv_columns(col)
    qkv_width = qkv_own.shape[1]
    bias = qkv_bias[0]
    bias_own = jnp.concatenate(
        [lax.dynamic_slice_in_dim(bias, col * query_width, query_width, 0), bias[2 * query_width :]]
    )

    (send,) = unit_columns(
        after(gate_up_block, early_send, gains), 1 - col, slots, count, slot_rows, padded, (0,)
    )
    line.mark(send)

    near = swap(block_input, "row")
    far = swap(line.step(block_input), "col")
    far_near = swap(far, "row")

    position_index = jnp.arange(seq_len, dtype=jnp.int32)
    doc_first = jnp.concatenate([jnp.ones((1,), jnp.bool_), segment_ids[1:] != segment_ids[:-1]])
    positions = position_index - lax.cummax(jnp.where(doc_first, position_index, 0), axis=0)
    frequency = ROPE_BASE ** (-jnp.arange(0, HEAD_DIM, 2, dtype=F32) / HEAD_DIM)
    angles = positions.astype(F32)[:, None] * frequency[None, :]
    cosine, sine = jnp.cos(angles), jnp.sin(angles)
    cosine = jnp.concatenate([cosine, cosine], axis=1)
    sine = jnp.concatenate([-sine, sine], axis=1)
    seg_col, seg_row = segment_ids[:, None], segment_ids[None, :]

    early_quad.first_round(line)
    gate_up_quad = Quad(swap(line.step(send), "col"), rank)
    line.mark(*early_quad.sent, cosine, sine)
    early_far = early_quad.second_round(line)
    gate_up_own = unit_columns(
        line.step(gate_up_block), col, jnp.arange(8), count, slot_rows, padded
    )
    line.mark(*gate_up_own)
    gate_up_own = [part.reshape(half_width, -1) for part in gate_up_own]
    stream, first_normed, first_scale, query, key, value = project(
        table, line.step(block_input), near, far, far_near, gains[:1], qkv_own, early_far,
        bias_own[None], cosine, sine,
    )
    line.mark(query)
    attended = attend(line.step(query), key, value, seg_col, seg_row)
    line.mark(attended)
    attended_far = swap(attended, "col")
    attended_near = swap(attended, "row")

    gate_up_quad.first_round(line)
    out_far = lax.optimization_barrier(
        laid_out([line.step(part)[:, qkv_width:] for part in early_far], rank)
    )
    line.mark(out_far)
    out_near = swap(line.step(out_block), "row")
    out_far_near = swap(out_far, "row")
    share = count // 8
    send_ranks = (slots[:, None] * share + jnp.arange(share)[None, :]).reshape(-1)
    down_send = unit_rows(line.step(down_block), 1 - col, send_ranks, count, padded)
    line.mark(down_send)
    gate_up_far = [gate_up_quad.second_round(line)]
    attended_far = line.step(attended_far)
    line.mark(attended_far)
    attended_far_near = swap(attended_far, "row")
    grad_far = swap(line.step(output_grad), "col")
    down_quad = Quad(
        swap(line.step(down_send).reshape(2, share * half_rows, model_width), "col"), rank
    )
    hidden_one, second_normed, second_scale, attended_group = residual(
        table, line.step(stream), attended, attended_far, attended_near, attended_far_near,
        [out_block, out_far, out_near, out_far_near], gains[1:],
    )
    line.mark(second_normed)
    (send,) = unit_columns(
        line.step(gate_up_block), 1 - col, jnp.arange(8), count, slot_rows, padded, (1,)
    )
    line.mark(send)

    act0, gate_factor0, up_factor0 = activate(
        table, line.step(second_normed), gate_up_own[0], gate_up_far[0]
    )
    line.mark(act0)
    grad_far = line.step(grad_far)
    line.mark(grad_far)
    grad_near = swap(line.step(output_grad), "row")
    grad_far_near = swap(grad_far, "row")
    gate_up_far.append([swap(line.step(send).reshape(half_width, -1), "col")])
    down_quad.first_round(line)
    down_own = unit_rows(line.step(down_block), col, jnp.arange(count), count, padded)
    line.mark(down_own)
    down_own = down_own.reshape(count * half_rows, model_width)
    grad_full = join(table, line.step(output_grad), grad_near, grad_far, grad_far_near)
    line.mark(grad_full)

    def down_terms(act, order):
        sent, kept = split_product(table, line.step(act), [grad_full], 768, 1, count, [order[0]])
        line.mark(sent)
        return sent, kept

    def gate_up_terms(d_gate, d_up, orders):
        bits = [order[0] for order in orders]
        terms = split_product(
            table, line.step(second_normed), [d_gate, d_up], tile_of(d_gate.shape[1]), 2, count, bits
        )
        line.mark(terms[0])
        return terms

    down_far = down_quad.second_round(line)
    sent, kept = down_terms(act0, pair_first)
    down_far = [line.step(part) for part in down_far]
    line.mark(*down_far)
    down_sum0 = Scatter(table, sent, kept, pair_first, line)
    d_gate0, d_up0 = activate_back(
        table, line.step(grad_full), down_own, down_far, 0, gate_factor0, up_factor0
    )
    line.mark(d_gate0)
    own_sent0, own_kept0, far_sent0, far_kept0 = gate_up_terms(d_gate0, d_up0, (pair_first, pair_first))
    act1, gate_factor1, up_factor1 = activate(
        table, line.step(second_normed), gate_up_own[1], gate_up_far[1]
    )
    line.mark(act1)
    down_sum0.relay(line)
    far_sum0 = Scatter(table, far_sent0, far_kept0, pair_first, line)
    sent1, kept1 = down_terms(act1, pair_first)
    d_gate1, d_up1 = activate_back(
        table, line.step(grad_full), down_own, down_far, 1, gate_factor1, up_factor1
    )
    line.mark(d_gate1)
    down_sum0.relay(line)
    own_sent1, own_kept1, far_sent1, far_kept1 = gate_up_terms(d_gate1, d_up1, (line_first, pair_first))
    far_sum0.relay(line)
    own_sum0 = Scatter(table, own_sent0, own_kept0, pair_first, line)
    own_sum1 = Scatter(table, own_sent1, own_kept1, line_first, line)
    d_second_own, d_second_other = normed_grad(
        table, [line.step(d_gate0), d_up0, d_gate1, d_up1], gate_up_own, gate_up_far
    )
    line.mark(d_second_other)
    far_sum0.relay(line)
    d_second_near = swap(line.step(d_second_other), "row")
    mlp_own, mlp_other = down(table, [line.step(act0), act1], down_own, down_far)
    line.mark(mlp_other)
    own_sum0.relay(line)
    down_sum1 = Scatter(table, sent1, kept1, pair_first, line)
    d_second_chip, d_second_low = chip_sum(line.step(d_second_own), d_second_near)
    line.mark(d_second_low)
    d_second_far = swap(d_second_low, "col")
    own_sum1.relay(line)

    d_hidden, d_hidden_low, second_gain_part = norm_back(
        table, line.step(d_second_chip), d_second_far, hidden_one, second_scale, grad_full, gains[1:]
    )
    line.mark(d_hidden_low)
    down_sum1.relay(line)
    far_sum1 = Scatter(table, far_sent1, far_kept1, pair_first, line)
    d_hidden_near = swap(line.step(d_hidden_low), "row")
    own_sum0.relay(line)
    d_hidden_full = in_order(row, d_hidden_low[:, :half_width], d_hidden_near[:, :half_width], 0)
    sent_out, kept_out = split_product(
        table, line.step(attended_group), [d_hidden_full], tile_of(half_width), 1, count, [0]
    )
    line.mark(sent_out)

    d_query, d_key_value = attend_back(
        table, line.step(query), key, value, seg_col, seg_row, d_hidden_low, d_hidden_near,
        out_block, out_far, cosine, sine,
    )
    d_projected_sent = jnp.concatenate([d_query, d_key_value.astype(BF16)], axis=1)
    d_projected_sent = lax.optimization_barrier(d_projected_sent)
    line.mark(d_projected_sent)
    arrived = swap(d_projected_sent, "col")
    down_sum1.relay(line)
    own_sum1.relay(line)
    out_sum = Scatter(table, sent_out, kept_out, pair_first, line)
    far_sum1.relay(line)
    sent, kept, d_first_own, d_first_other, bias_part = project_back(
        table, line.step(d_query), d_key_value, arrived, first_normed, qkv_block, count, 0
    )
    line.mark(sent)
    qkv_sum = Scatter(table, sent, kept, pair_first, line)

    d_first = line.step(d_first_own) + swap(line.step(d_first_other), "row")
    stream_own = block_input.astype(F32)
    first_scale_own = own_tokens(first_scale)[:, :1]
    first_gain_part = jnp.sum(d_first * stream_own * first_scale_own, axis=0)
    weighted = d_first * first_gain
    inner = jnp.sum(weighted * stream_own, axis=1)
    inner = (inner + swap(inner, "col"))[:, None]
    input_grad = d_hidden + first_scale_own * (
        weighted - stream_own * (first_scale_own * first_scale_own) * (inner / model_width)
    )

    mlp_chip = mlp_own + swap(line.step(mlp_other), "row").astype(F32)
    mlp_far = swap(mlp_chip[:, half_width:].astype(BF16), "col").astype(F32)
    hidden_own = own_tokens(hidden_one)[:, :half_width]
    block_output = (hidden_own + (mlp_chip[:, :half_width] + mlp_far)).astype(BF16)

    down_sum0 = down_sum0.finish(line)
    far_sum0 = far_sum0.finish(line)
    own_sum0 = own_sum0.finish(line)
    down_sum0_far = swap(line.step(down_sum0[:, half_width:].astype(BF16)), "col")
    far_sum0 = swap(line.step(far_sum0.astype(BF16)), "col")
    far_sum1.relay(line)
    out_sum.relay(line)
    qkv_sum.relay(line)
    own_sum1 = own_sum1.finish(line)
    down_sum1 = down_sum1.finish(line)
    out_sum.relay(line)
    qkv_sum.relay(line)
    far_sum1 = far_sum1.finish(line)
    out_sum, qkv_sum = out_sum.finish(line), qkv_sum.finish(line)
    down_sum1_far = swap(down_sum1[:, half_width:].astype(BF16), "col")
    far_sum1 = swap(far_sum1.astype(BF16), "col")

    gain_parts = jnp.concatenate([first_gain_part, second_gain_part[0]])
    gain_parts = gain_parts + swap(gain_parts, "row")
    small = dp_sum(jnp.concatenate([gain_parts, bias_part[0]]))
    bias_width = bias.shape[0] // count
    bias_grad = lax.dynamic_slice_in_dim(small[model_width:], rank * bias_width, bias_width, 0)

    widths = [width for _, width in halves_of(segment, padded)]
    own_rows_sum = [
        part[:width, :half_width] for part, width in zip((down_sum0, down_sum1), widths)
    ]
    far_rows_sum = [
        part[:width].astype(F32) for part, width in zip((down_sum0_far, down_sum1_far), widths)
    ]
    down_grad = in_order(
        col, jnp.concatenate(own_rows_sum, axis=0), jnp.concatenate(far_rows_sum, axis=0), 0
    )
    gate_up_grad = spread_columns(
        table, (own_sum0, own_sum1), (far_sum0, far_sum1), count, segment, padded
    )

    return (
        block_output,
        input_grad,
        small[:half_width],
        qkv_sum[None, None],
        bias_grad[None],
        out_sum[None, None],
        small[half_width:model_width],
        gate_up_grad[None, None],
        down_grad[None, None],
    )


def solution(mesh):
    placed = (
        P(("dp", "row"), "col"),
        P("dp"),
        P("col"),
        P("col", "row", None, None),
        P("row", None),
        P("row", "col", None, None),
        P("col"),
        P("col", "row", None, None),
        P("row", "col", None, None),
        P(("dp", "row"), "col"),
    )
    return jax.shard_map(
        shards,
        mesh=mesh,
        in_specs=placed,
        out_specs=(
            P(("dp", "row"), "col"),
            P(("dp", "row"), "col"),
            P("col"),
            P("col", "row", "dp", None),
            P("row", "dp"),
            P("row", "col", "dp", None),
            P("col"),
            P("col", "row", "dp", None),
            P("row", "col", "dp", None),
        ),
        check_vma=False,
    )
```

```python
import functools
import jax
import jax.numpy as jnp
from jax import lax
from jax.experimental import pallas as pl
from jax.experimental.pallas import tpu as pltpu
from jax.sharding import PartitionSpec as P

HEADS = 12
KV_HEADS = 2
HEAD_DIM = 128
EPSILON = 1e-06
ROPE_BASE = 1000000.0
MASKED = -1e30
F32 = jnp.float32
BF16 = jnp.bfloat16
VMEM_LIMIT = 60 * 1024 * 1024


def dot(left, right, left_dim, right_dim):
    return lax.dot_general(
        left, right, (((left_dim,), (right_dim,)), ((), ())), preferred_element_type=F32
    )


def params(*semantics):
    return pltpu.CompilerParams(
        dimension_semantics=semantics or None, vmem_limit_bytes=VMEM_LIMIT
    )


def cost(flops, moved):
    return pl.CostEstimate(flops=1, bytes_accessed=1, transcendentals=0)


def whole(shape):
    return pl.BlockSpec(shape, lambda *_: (0,) * len(shape))


ROW, COL, LOW, HIGH = range(4)
BITS = 2


def with_bit(index, place, value):
    return ((index >> place) << (place + 1)) | (value << place) | (index & ((1 << place) - 1))


def ordered(table, parts, columns=slice(None)):
    if len(parts) == 1:
        return parts[0][:, columns]
    first, second, first_other, second_other = [part[:, columns] for part in parts]
    high, low = table[HIGH] == 0, table[LOW] == 0
    return jnp.concatenate(
        [
            jnp.where(high, first, first_other),
            jnp.where(high, first_other, first),
            jnp.where(low, second, second_other),
            jnp.where(low, second_other, second),
        ],
        axis=0,
    )


def halves_of(segment, padded):
    first = 2 * padded // 3
    return ((0, first, first), (first, segment - first, padded - first))


def units_kernel(count, segment, padded, halves, table, block_ref, *refs):
    rows = block_ref.shape[0]
    out_refs = refs[-len(halves) :]

    def write(side):
        for out_ref, half in zip(out_refs, halves):
            begin, width, full = halves_of(segment, padded)[half]
            parts = []
            for kind in range(2):
                for k in range(count):
                    start = ((kind * count + k) * 2 + side) * segment + begin
                    parts.append(block_ref[:, start : start + width])
                    if width < full:
                        parts.append(jnp.zeros((rows, full - width), block_ref.dtype))
            out_ref[0] = jnp.concatenate(parts, axis=1)

    @pl.when(table[0] == 0)
    def _():
        write(0)

    @pl.when(table[0] != 0)
    def _():
        write(1)


def unit_columns(block, side, slots, count, rows, padded, halves=(0, 1), places=None, depth=None, begun=None):
    columns = block.shape[1]
    segment = columns // (4 * count)
    units = [2 * count * halves_of(segment, padded)[half][2] for half in halves]
    steps = slots.shape[0]
    depth = steps if depth is None else depth
    places = jnp.arange(steps) if places is None else places
    begun = [] if begun is None else begun
    table = jnp.concatenate([side.reshape(1), slots, places]).astype(jnp.int32)
    return pl.pallas_call(
        functools.partial(units_kernel, count, segment, padded, halves),
        grid_spec=pltpu.PrefetchScalarGridSpec(
            num_scalar_prefetch=1,
            grid=(steps,),
            in_specs=[pl.BlockSpec((rows, columns), lambda i, t: (t[1 + i], 0))]
            + [pl.BlockSpec(memory_space=pl.ANY)] * len(begun),
            out_specs=[pl.BlockSpec((1, rows, wide), lambda i, t: (t[1 + steps + i], 0, 0)) for wide in units],
        ),
        out_shape=[jax.ShapeDtypeStruct((depth, rows, wide), block.dtype) for wide in units],
        input_output_aliases={2 + index: index for index in range(len(begun))},
        compiler_params=params("arbitrary"),
        cost_estimate=cost(0, 4 * steps * rows * sum(units)),
        name="unit_columns",
    )(table, block, *begun)


def unit_rows_kernel(parts, table, block_ref, *out_refs):
    for out_ref, (begin, width, full) in zip(out_refs, parts):
        if width == full and begin % 16 == 0 and full % 16 == 0:
            out_ref[0] = block_ref[0, 0, begin : begin + width]
        else:
            part = block_ref[0, 0].astype(F32)[begin : begin + width]
            part = jnp.concatenate([part, jnp.zeros((full - width, part.shape[1]), F32)], axis=0)
            out_ref[0] = part.astype(out_ref.dtype)


def unit_rows(block, side, ranks, count, padded, halves=(0, 1)):
    rows, width = block.shape
    segment = rows // (2 * count)
    parts = [halves_of(segment, padded)[half] for half in halves]
    steps = ranks.shape[0]
    table = jnp.concatenate([side.reshape(1), ranks]).astype(jnp.int32)
    return pl.pallas_call(
        functools.partial(unit_rows_kernel, parts),
        grid_spec=pltpu.PrefetchScalarGridSpec(
            num_scalar_prefetch=1,
            grid=(steps,),
            in_specs=[pl.BlockSpec((1, 1, segment, width), lambda i, t: (t[1 + i], t[0], 0, 0))],
            out_specs=[pl.BlockSpec((1, full, width), lambda i, t: (i, 0, 0)) for _, _, full in parts],
        ),
        out_shape=[jax.ShapeDtypeStruct((steps, full, width), block.dtype) for _, _, full in parts],
        compiler_params=params("arbitrary"),
        cost_estimate=cost(0, 4 * steps * segment * width),
        name="unit_rows",
    )(table, block.reshape(count, 2, segment, width))


def spread_kernel(count, segment, padded, table, own0_ref, own1_ref, far0_ref, far1_ref, out_ref):
    def write(sides):
        pieces = []
        for kind in range(2):
            for k in range(count):
                for side in sides:
                    for ref, (_, width, full) in zip(side, halves_of(segment, padded)):
                        start = (kind * count + k) * full
                        pieces.append(ref[:, start : start + width].astype(F32))
        out_ref[...] = jnp.concatenate(pieces, axis=1)

    own, far = (own0_ref, own1_ref), (far0_ref, far1_ref)

    @pl.when(table[COL] == 0)
    def _():
        write((own, far))

    @pl.when(table[COL] != 0)
    def _():
        write((far, own))


def spread_columns(table, own, far, count, segment, padded):
    rows = own[0].shape[0]
    step = rows // 3 if rows % 24 == 0 else rows
    parts = [pl.BlockSpec((step, part.shape[1]), lambda i, t: (i, 0)) for part in (*own, *far)]
    columns = 4 * count * segment
    return pl.pallas_call(
        functools.partial(spread_kernel, count, segment, padded),
        grid_spec=pltpu.PrefetchScalarGridSpec(
            num_scalar_prefetch=1,
            grid=(rows // step,),
            in_specs=parts,
            out_specs=pl.BlockSpec((step, columns), lambda i, t: (i, 0)),
        ),
        out_shape=jax.ShapeDtypeStruct((rows, columns), F32),
        compiler_params=params("arbitrary"),
        cost_estimate=cost(0, 7 * rows * columns),
        name="spread_columns",
    )(table, *own, *far)


def project_kernel(
    width, table, own_ref, near_ref, far_ref, far_near0_ref, far_near1_ref, gain_ref, weight_ref,
    part0_ref, part1_ref, part2_ref, part3_ref, bias_ref, cosine_ref, sine_ref, stream_ref, normed_ref, scale_ref, query_ref, key_ref, value_ref,
):
    half = pl.program_id(0) * 2 // pl.num_programs(0)
    mine = half == table[ROW]
    left = jnp.where(mine, own_ref[...], near_ref[...]).astype(F32)
    even = pl.program_id(0) % 2 == 0
    right = jnp.where(
        mine,
        far_ref[...],
        jnp.where(even, far_near0_ref[...], far_near1_ref[...]),
    ).astype(F32)
    squares = jnp.sum(left * left, axis=1, keepdims=True) + jnp.sum(
        right * right, axis=1, keepdims=True
    )
    scale = lax.rsqrt(squares / (2 * width) + EPSILON)
    left_normed = (left * scale * gain_ref[:, :width]).astype(BF16)
    right_normed = (right * scale * gain_ref[:, width:]).astype(BF16)
    stream_ref[:, :width] = left.astype(BF16)
    stream_ref[:, width:] = right.astype(BF16)
    normed_ref[...] = left_normed
    scale_ref[...] = jnp.broadcast_to(scale, scale_ref.shape)
    far_weight = ordered(table, (part0_ref, part1_ref, part2_ref, part3_ref))
    projected = (
        dot(left_normed, weight_ref[...], 1, 0) + dot(right_normed, far_weight, 1, 0) + bias_ref[...]
    )
    cosine, sine = cosine_ref[...], sine_ref[...]

    def rotated(values):
        return (values * cosine + pltpu.roll(values, HEAD_DIM // 2, 1) * sine).astype(BF16)

    query_width = query_ref.shape[1]
    for start in range(0, query_width, HEAD_DIM):
        query_ref[:, start : start + HEAD_DIM] = rotated(projected[:, start : start + HEAD_DIM])
    key_ref[...] = rotated(projected[:, query_width : query_width + HEAD_DIM])
    value_ref[...] = projected[:, query_width + HEAD_DIM :].astype(BF16)


def project(table, own, near, far, far_near, gain, weight, far_parts, bias, cosine, sine):
    rows, width = own.shape
    seq_len = 2 * rows
    block = rows // 2
    per_half = 2
    out_width = weight.shape[1]
    query_width = out_width - 2 * HEAD_DIM
    part = pl.BlockSpec((block, width), lambda i, t: (i % per_half, 0))

    def tokens(columns):
        return pl.BlockSpec((block, columns), lambda i, t: (i, 0))

    return pl.pallas_call(
        functools.partial(project_kernel, width),
        grid_spec=pltpu.PrefetchScalarGridSpec(
            num_scalar_prefetch=1,
            grid=(seq_len // block,),
            in_specs=[part, part, part]
            + [whole((block, width))] * 2
            + [whole((1, 2 * width)), whole(weight.shape)]
            + [whole((piece.shape[0], out_width)) for piece in far_parts]
            + [whole((1, out_width)), tokens(HEAD_DIM), tokens(HEAD_DIM)],
            out_specs=[
                tokens(2 * width), tokens(width), tokens(128),
                tokens(query_width), tokens(HEAD_DIM), tokens(HEAD_DIM),
            ],
        ),
        out_shape=[
            jax.ShapeDtypeStruct((seq_len, 2 * width), BF16),
            jax.ShapeDtypeStruct((seq_len, width), BF16),
            jax.ShapeDtypeStruct((seq_len, 128), F32),
            jax.ShapeDtypeStruct((seq_len, query_width), BF16),
            jax.ShapeDtypeStruct((seq_len, HEAD_DIM), BF16),
            jax.ShapeDtypeStruct((seq_len, HEAD_DIM), BF16),
        ],
        compiler_params=params("arbitrary"),
        cost_estimate=cost(4 * seq_len * width * out_width, 12 * seq_len * width),
        name="project",
    )(table, own, near, far, *far_near, gain, weight, *far_parts, bias, cosine, sine)


def join_kernel(width, table, own_ref, near_ref, far_ref, far_near_ref, out_ref):
    mine = pl.program_id(0) * 2 // pl.num_programs(0) == table[ROW]
    out_ref[:, :width] = jnp.where(mine, own_ref[...], near_ref[...])
    out_ref[:, width:] = jnp.where(mine, far_ref[...], far_near_ref[...])


def join(table, own, near, far, far_near):
    rows, width = own.shape
    block = min(256, rows)
    per_half = rows // block
    part = pl.BlockSpec((block, width), lambda i, t: (i % per_half, 0))
    return pl.pallas_call(
        functools.partial(join_kernel, width),
        grid_spec=pltpu.PrefetchScalarGridSpec(
            num_scalar_prefetch=1,
            grid=(2 * rows // block,),
            in_specs=[part] * 4,
            out_specs=pl.BlockSpec((block, 2 * width), lambda i, t: (i, 0)),
        ),
        out_shape=jax.ShapeDtypeStruct((2 * rows, 2 * width), own.dtype),
        compiler_params=params("arbitrary"),
        cost_estimate=cost(0, 16 * rows * width),
        name="join",
    )(table, own, near, far, far_near)


def block_probs(query, key, seg_col, seg_row, start, stop):
    scores = dot(query, key, 1, 1) * HEAD_DIM ** (-0.5)
    rows = stop - start
    query_index = start + lax.broadcasted_iota(jnp.int32, (rows, stop), 0)
    key_index = lax.broadcasted_iota(jnp.int32, (rows, stop), 1)
    allowed = (key_index <= query_index) & (seg_col == seg_row)
    scores = jnp.where(allowed, scores, MASKED)
    exponent = jnp.exp(scores - jnp.max(scores, axis=1, keepdims=True))
    return exponent / jnp.sum(exponent, axis=1, keepdims=True)


def attend_kernel(block, query_ref, key_ref, value_ref, seg_col_ref, seg_row_ref, out_ref, last_ref):
    last = pl.program_id(0) == pl.num_programs(0) - 1
    for start in range(0, query_ref.shape[0], block):
        stop = start + block
        probs = block_probs(
            query_ref[start:stop], key_ref[:stop], seg_col_ref[start:stop], seg_row_ref[:, :stop], start, stop
        )
        out = dot(probs.astype(BF16), value_ref[:stop], 1, 0).astype(BF16)

        @pl.when(last)
        def _():
            last_ref[start:stop] = out

        @pl.when(jnp.logical_not(last))
        def _():
            out_ref[start:stop] = out


def attend(query, key, value, seg_col, seg_row):
    seq_len, width = query.shape
    heads = width // HEAD_DIM
    head = pl.BlockSpec((seq_len, HEAD_DIM), lambda h: (0, h))
    shared = whole((seq_len, HEAD_DIM))
    return pl.pallas_call(
        functools.partial(attend_kernel, 256),
        grid=(width // HEAD_DIM,),
        in_specs=[head, shared, shared, whole((seq_len, 1)), whole((1, seq_len))],
        out_specs=[pl.BlockSpec((seq_len, HEAD_DIM), lambda h: (0, jnp.minimum(h, heads - 2))), shared],
        out_shape=[
            jax.ShapeDtypeStruct((seq_len, width - HEAD_DIM), BF16),
            jax.ShapeDtypeStruct((seq_len, HEAD_DIM), BF16),
        ],
        compiler_params=params("arbitrary"),
        cost_estimate=cost(6 * seq_len * seq_len * width, 8 * seq_len * width),
        name="attend",
    )(query, key, value, seg_col, seg_row)


def attend_back_kernel(
    block, table, query_ref, key_ref, value_ref, seg_col_ref, seg_row_ref, own_ref, far_ref, near_ref, far_near_ref,
    weight_ref, far_top_ref, far_bottom_ref, cosine_ref, sine_ref, sent_ref, key_value_ref,
):
    scaling = HEAD_DIM ** (-0.5)
    own_rows = own_ref.shape[0]
    far_weight = jnp.where(table[COL] == 0, far_top_ref[...], far_bottom_ref[...])

    @pl.when(pl.program_id(0) == 0)
    def _():
        key_value_ref[...] = jnp.zeros_like(key_value_ref)

    for start in range(0, query_ref.shape[0], block):
        stop = start + block
        mine = table[ROW] == start // own_rows
        place = slice(start % own_rows, start % own_rows + block)
        grad = (
            dot(jnp.where(mine, own_ref[place], near_ref[place]), weight_ref[...], 1, 1)
            + dot(jnp.where(mine, far_ref[place], far_near_ref[place]), far_weight, 1, 1)
        ).astype(BF16)
        query = query_ref[start:stop]
        key, value = key_ref[:stop], value_ref[:stop]
        probs = block_probs(
            query, key, seg_col_ref[start:stop], seg_row_ref[:, :stop], start, stop
        )
        d_probs = dot(grad, value, 1, 1)
        d_scores = probs * (d_probs - jnp.sum(d_probs * probs, axis=1, keepdims=True))
        d_scores = d_scores.astype(BF16)
        d_query = dot(d_scores, key, 1, 0) * scaling
        turned = pltpu.roll(d_query * sine_ref[start:stop], HEAD_DIM // 2, 1)
        sent_ref[start:stop] = (d_query * cosine_ref[start:stop] + turned).astype(BF16)
        key_value_ref[:stop, :HEAD_DIM] += dot(d_scores, query, 0, 0) * scaling
        key_value_ref[:stop, HEAD_DIM:] += dot(probs.astype(BF16), grad, 0, 0)

    @pl.when(pl.program_id(0) == pl.num_programs(0) - 1)
    def _():
        d_key = key_value_ref[:, :HEAD_DIM]
        turned = pltpu.roll(d_key * sine_ref[...], HEAD_DIM // 2, 1)
        key_value_ref[:, :HEAD_DIM] = d_key * cosine_ref[...] + turned


def attend_back(table, query, key, value, seg_col, seg_row, d_hidden, weight, far_weights, cosine, sine):
    seq_len, width = query.shape
    features = weight.shape[1]
    heads = width // HEAD_DIM
    head = pl.BlockSpec((seq_len, HEAD_DIM), lambda h, t: (0, h))
    rows = pl.BlockSpec((HEAD_DIM, features), lambda h, t: (heads * t[COL] + h, 0))
    far_rows = pl.BlockSpec((HEAD_DIM, features), lambda h, t: (h, 0))
    shared = whole((seq_len, HEAD_DIM))
    return pl.pallas_call(
        functools.partial(attend_back_kernel, 256),
        grid_spec=pltpu.PrefetchScalarGridSpec(
            num_scalar_prefetch=1,
            grid=(heads,),
            in_specs=[
                head, shared, shared, whole((seq_len, 1)), whole((1, seq_len)),
                *[whole(part.shape) for part in d_hidden], rows, far_rows, far_rows, shared, shared,
            ],
            out_specs=[head, whole((seq_len, 2 * HEAD_DIM))],
        ),
        out_shape=[
            jax.ShapeDtypeStruct(query.shape, BF16),
            jax.ShapeDtypeStruct((seq_len, 2 * HEAD_DIM), F32),
        ],
        compiler_params=params("arbitrary"),
        cost_estimate=cost(12 * seq_len * seq_len * width, 12 * seq_len * width),
        name="attend_back",
    )(table, query, key, value, seg_col, seg_row, *d_hidden, weight, *far_weights, cosine, sine)


def residual_kernel(table, stream_ref, *refs):
    pieces, weights, (gain_ref, hidden_ref, normed_ref, scale_ref, group_ref) = refs[:8], refs[8:14], refs[14:]
    first = table[COL] == 0
    own, far, near, near_far = (
        jnp.concatenate([pieces[2 * index][...], pieces[2 * index + 1][...]], axis=1) for index in range(4)
    )
    part = own.shape[1]
    group = [jnp.where(first, own, far), jnp.where(first, far, own)]
    other = [jnp.where(first, near, near_far), jnp.where(first, near_far, near)]
    group_ref[:, :part] = group[0]
    group_ref[:, part:] = group[1]
    own_w, near_w, *far_w = weights
    width = own_w.shape[1]
    halves = []
    for index in range(2):
        total = stream_ref[:, index * width : (index + 1) * width].astype(F32)
        for place in range(2):
            rows = slice(place * part, (place + 1) * part)
            mine, theirs = (own_w[rows], near_w[rows]) if index == 0 else (far_w[place][...], far_w[2 + place][...])
            total = total + dot(group[place], mine, 1, 0)
            total = total + dot(other[place], theirs, 1, 0)
        halves.append(total)
    squares = sum(jnp.sum(total * total, axis=1, keepdims=True) for total in halves)
    scale = lax.rsqrt(squares / (2 * width) + EPSILON)
    scale_ref[...] = jnp.broadcast_to(scale, scale_ref.shape)
    for index, total in enumerate(halves):
        columns = slice(index * width, (index + 1) * width)
        hidden_ref[:, columns] = total
        normed_ref[:, columns] = (total * scale * gain_ref[:, columns]).astype(BF16)


def residual(table, stream, attended, own_weight, near_weight, far_weights, near_far_weights, gain):
    seq_len, width = stream.shape
    pieces = [piece for pair in attended for piece in pair]
    part = attended[0][0].shape[1] + attended[0][1].shape[1]
    weights = [own_weight, near_weight, *far_weights, *near_far_weights]
    block = min(256, seq_len)

    def tokens(columns):
        return pl.BlockSpec((block, columns), lambda i, t: (i, 0))

    return pl.pallas_call(
        residual_kernel,
        grid_spec=pltpu.PrefetchScalarGridSpec(
            num_scalar_prefetch=1,
            grid=(seq_len // block,),
            in_specs=[tokens(width)]
            + [tokens(piece.shape[1]) for piece in pieces]
            + [whole(weight.shape) for weight in weights]
            + [whole((1, width))],
            out_specs=[tokens(width), tokens(width), tokens(128), tokens(2 * part)],
        ),
        out_shape=[
            jax.ShapeDtypeStruct((seq_len, width), F32),
            jax.ShapeDtypeStruct((seq_len, width), BF16),
            jax.ShapeDtypeStruct((seq_len, 128), F32),
            jax.ShapeDtypeStruct((seq_len, 2 * part), BF16),
        ],
        compiler_params=params("arbitrary"),
        cost_estimate=cost(2 * seq_len * width * width, 14 * seq_len * width),
        name="residual",
    )(table, stream, *pieces, *weights, gain)


def activate_kernel(width, table, normed_ref, own_gate_ref, own_up_ref, *refs):
    (act_ref, gate_factor_ref, up_factor_ref), refs = refs[-3:], refs[:-3]
    gate_parts, up_parts = refs[: len(refs) // 2], refs[len(refs) // 2 :]
    left, right = normed_ref[:, :width], normed_ref[:, width:]
    gate = dot(left, own_gate_ref[...], 1, 0) + dot(right, ordered(table, gate_parts), 1, 0)
    up = dot(left, own_up_ref[...], 1, 0) + dot(right, ordered(table, up_parts), 1, 0)
    sigmoid = jax.nn.sigmoid(gate)
    silu = gate * sigmoid
    act_ref[...] = (silu * up).astype(BF16)
    gate_factor_ref[...] = (up * (sigmoid * (1.0 + gate * (1.0 - sigmoid)))).astype(BF16)
    up_factor_ref[...] = silu.astype(BF16)


def tile_of(units):
    return next(t for t in (384, 256, 128, units) if units % t == 0)


def activate(table, normed, own, far_parts):
    seq_len, width = normed.shape
    units = own.shape[1] // 2
    tile = tile_of(units)
    steps = units // tile

    def gate(rows):
        return pl.BlockSpec((rows, tile), lambda j, t: (0, j))

    def up(rows):
        return pl.BlockSpec((rows, tile), lambda j, t: (0, steps + j))

    rows = far_parts[0].shape[0]
    out = pl.BlockSpec((seq_len, tile), lambda j, t: (0, j))
    return pl.pallas_call(
        functools.partial(activate_kernel, width // 2),
        grid_spec=pltpu.PrefetchScalarGridSpec(
            num_scalar_prefetch=1,
            grid=(steps,),
            in_specs=[whole(normed.shape), gate(width // 2), up(width // 2)]
            + [gate(rows)] * len(far_parts)
            + [up(rows)] * len(far_parts),
            out_specs=[out] * 3,
        ),
        out_shape=[jax.ShapeDtypeStruct((seq_len, units), BF16)] * 3,
        compiler_params=params("arbitrary"),
        cost_estimate=cost(4 * seq_len * width * units, 6 * seq_len * units + 4 * width * units),
        name="activate",
    )(table, normed, own, own, *far_parts, *far_parts)


def activate_back_kernel(tile, width, table, grad_ref, own_ref, *refs):
    (gate_factor_ref, up_factor_ref, d_gate_ref, d_up_ref, far_scr), part_refs = refs[-5:], refs[:-5]

    @pl.when(pl.program_id(0) == 0)
    def _():
        far_scr[...] = ordered(table, part_refs)

    far = far_scr[pl.ds(pl.multiple_of(pl.program_id(0) * tile, tile), tile)]
    d_act = dot(grad_ref[:, :width], own_ref[...], 1, 1) + dot(grad_ref[:, width:], far, 1, 1)
    d_gate_ref[...] = (d_act * gate_factor_ref[...].astype(F32)).astype(BF16)
    d_up_ref[...] = (d_act * up_factor_ref[...].astype(F32)).astype(BF16)


def activate_back(table, grad, own, far_parts, gate_factor, up_factor):
    seq_len, width = grad.shape
    units = own.shape[0]
    tile = tile_of(units)
    out = pl.BlockSpec((seq_len, tile), lambda j, t: (0, j))
    return pl.pallas_call(
        functools.partial(activate_back_kernel, tile, width // 2),
        grid_spec=pltpu.PrefetchScalarGridSpec(
            num_scalar_prefetch=1,
            grid=(units // tile,),
            in_specs=[whole(grad.shape), pl.BlockSpec((tile, width // 2), lambda j, t: (j, 0))]
            + [whole(piece.shape) for piece in far_parts]
            + [out, out],
            out_specs=[out] * 2,
            scratch_shapes=[pltpu.VMEM((units, width // 2), BF16)],
        ),
        out_shape=[jax.ShapeDtypeStruct((seq_len, units), BF16)] * 2,
        compiler_params=params("arbitrary"),
        cost_estimate=cost(2 * seq_len * width * units, 8 * seq_len * units + 2 * width * units),
        name="activate_back",
    )(table, grad, own, *far_parts, gate_factor, up_factor)


def down_kernel(counts, table, *refs):
    halves = len(counts)
    act_refs, own_refs, refs = refs[:halves], refs[halves : 2 * halves], refs[2 * halves :]
    own_out_ref, other_out_ref, total_scr = refs[-3:]
    part_refs = []
    for parts in counts:
        part_refs.append(refs[:parts])
        refs = refs[parts:]

    def write(weights):
        total_scr[...] = sum(dot(act_ref[...], weight, 1, 0) for act_ref, weight in zip(act_refs, weights))
        rows = own_out_ref.shape[0]
        own_out_ref[...] = total_scr[pl.ds(pl.multiple_of(table[ROW] * rows, rows), rows)]
        other = pl.multiple_of((1 - table[ROW]) * rows, rows)
        other_out_ref[...] = total_scr[pl.ds(other, rows)].astype(BF16)

    @pl.when(pl.program_id(0) == 0)
    def _():
        write([own_ref[...] for own_ref in own_refs])

    @pl.when(pl.program_id(0) == 1)
    def _():
        write([ordered(table, parts) for parts in part_refs])


def down(table, acts, own, far_parts):
    seq_len = acts[0].shape[0]
    features = own[0].shape[1]
    units = sum(part.shape[0] for part in own)
    arrays = (*acts, *own, *[piece for parts in far_parts for piece in parts])
    return pl.pallas_call(
        functools.partial(down_kernel, [len(parts) for parts in far_parts]),
        grid_spec=pltpu.PrefetchScalarGridSpec(
            num_scalar_prefetch=1,
            grid=(2,),
            in_specs=[whole(array.shape) for array in arrays],
            out_specs=[pl.BlockSpec((seq_len // 2, features), lambda j, t: (0, j))] * 2,
            scratch_shapes=[pltpu.VMEM((seq_len, features), F32)],
        ),
        out_shape=[
            jax.ShapeDtypeStruct((seq_len // 2, 2 * features), F32),
            jax.ShapeDtypeStruct((seq_len // 2, 2 * features), BF16),
        ],
        compiler_params=params("arbitrary"),
        cost_estimate=cost(4 * seq_len * units * features, 8 * seq_len * features + 8 * units * (seq_len + features)),
        name="down",
    )(table, *arrays)


def split_product(table, left, rights, tile, groups, count, bits, merge=False):
    seq_len, height = left.shape
    rows = height // (groups * count)
    place = [(0, group) if merge else (group, 0) for group in range(groups)]
    outs, depth = (1, groups * count // 2) if merge else (groups, count // 2)
    firsts = [first for _, first, _ in rights]
    steps = [length for _, _, length in rights]
    rights = [right for right, _, _ in rights]
    columns = sum(steps) * tile
    starts = [sum(steps[:index]) for index in range(len(rights))]

    def kernel(table, left_ref, *refs):
        right_refs, out_refs, total_scr = refs[: len(rights)], refs[len(rights) : -1], refs[-1]
        step = pl.program_id(0)
        for right_ref, start, length in zip(right_refs, starts, steps):

            @pl.when((step >= start) & (step < start + length))
            def _():
                total_scr[...] = dot(left_ref[...], right_ref[...], 0, 0)

        for group, bit in enumerate(bits):
            side = table[BITS + bit]
            sent_ref, kept_ref = out_refs[2 * place[group][0] : 2 * place[group][0] + 2]
            for out_ref, value in ((sent_ref, 1 - side), (kept_ref, side)):
                for index in range(count // 2):
                    begin = (group * count + with_bit(index, bit, value)) * rows
                    if rows % 8 == 0:
                        begin = pl.multiple_of(begin, 8)
                    out_ref[place[group][1] * (count // 2) + index] = total_scr[pl.ds(begin, rows)].astype(BF16)

    def right_spec(first, start, length):
        return pl.BlockSpec((seq_len, tile), lambda i, t: (0, first + jnp.clip(i - start, 0, length - 1)))

    return pl.pallas_call(
        kernel,
        grid_spec=pltpu.PrefetchScalarGridSpec(
            num_scalar_prefetch=1,
            grid=(sum(steps),),
            in_specs=[whole(left.shape)]
            + [right_spec(*place) for place in zip(firsts, starts, steps)],
            out_specs=[pl.BlockSpec((depth, rows, tile), lambda i, t: (0, 0, i))] * (2 * outs),
            scratch_shapes=[pltpu.VMEM((height, tile), F32)],
        ),
        out_shape=[jax.ShapeDtypeStruct((depth, rows, columns), BF16)] * (2 * outs),
        compiler_params=params("arbitrary"),
        cost_estimate=cost(
            2 * seq_len * height * columns, 2 * (seq_len * (height + columns) + height * columns)
        ),
        name="split_product",
    )(table, left, *rights)


def relay_kernel(table, kept_sent_ref, arrived_sent_ref, kept_ref, arrived_ref, sent_out_ref, kept_out_ref):
    sent_out_ref[...] = (kept_sent_ref[...].astype(F32) + arrived_sent_ref[...].astype(F32)).astype(BF16)
    kept_out_ref[...] = (kept_ref[...].astype(F32) + arrived_ref[...].astype(F32)).astype(BF16)


def relay(table, kept, arrived, place, bit):
    count, rows, columns = kept.shape

    def block(sent):
        def index(i, t):
            value = t[BITS + bit]
            return (with_bit(i, place, 1 - value if sent else value), 0, 0)

        return pl.BlockSpec((1, rows, columns), index)

    out = pl.BlockSpec((1, rows, columns), lambda i, t: (i, 0, 0))
    return pl.pallas_call(
        relay_kernel,
        grid_spec=pltpu.PrefetchScalarGridSpec(
            num_scalar_prefetch=1,
            grid=(count // 2,),
            in_specs=[block(True), block(True), block(False), block(False)],
            out_specs=[out, out],
        ),
        out_shape=[jax.ShapeDtypeStruct((count // 2, rows, columns), BF16)] * 2,
        compiler_params=params("arbitrary"),
        cost_estimate=cost(0, 6 * count * rows * columns),
        name="relay",
    )(table, kept, arrived, kept, arrived)


def normed_grad_kernel(halves, steps, tile, counts, table, *refs):
    d_refs, own_refs, refs = refs[: 2 * halves], refs[2 * halves : 3 * halves], refs[3 * halves :]
    part_refs = []
    for parts in counts:
        part_refs.append(refs[:parts])
        refs = refs[parts:]
    own_out_ref, other_refs, far_scrs, total_scr = refs[0], refs[1:4], refs[4:-1], refs[-1]
    share = 2 * steps // 3

    @pl.when(pl.program_id(0) == 0)
    def _():
        for half in range(halves):
            far_scrs[half][...] = ordered(table, part_refs[half])

    def write(weights):
        total = None
        for half in range(halves):
            units = d_refs[2 * half].shape[1]
            for kind in range(2):
                term = dot(
                    d_refs[2 * half + kind][...], weights[half][:, kind * units : (kind + 1) * units], 1, 1
                )
                total = term if total is None else total + term
        total_scr[...] = total
        rows = own_out_ref.shape[0]
        own_out_ref[...] = total_scr[pl.ds(pl.multiple_of(table[ROW] * rows, rows), rows)]
        other = pl.multiple_of((1 - table[ROW]) * rows, rows)
        for index, other_ref in enumerate(other_refs):

            @pl.when(pl.program_id(0) // share == index)
            def _():
                other_ref[...] = total_scr[pl.ds(other, rows)].astype(BF16)

    @pl.when(pl.program_id(0) < steps)
    def _():
        write(own_refs)

    @pl.when(pl.program_id(0) >= steps)
    def _():
        start = pl.multiple_of((pl.program_id(0) - steps) * tile, tile)
        write([scr.at[pl.ds(start, tile)] for scr in far_scrs])


def normed_grad(table, d_parts, own, far_parts):
    seq_len = d_parts[0].shape[0]
    units = [part.shape[1] for part in d_parts[::2]]
    features = own[0].shape[0]
    tile = 256
    steps = features // tile
    halves = len(own)
    parts = [piece for half in far_parts for piece in half]
    share = 2 * steps // 3

    def third(index):
        return pl.BlockSpec(
            (seq_len // 2, tile), lambda j, t: (0, jnp.clip(j - share * index, 0, share - 1))
        )

    own_specs = [
        pl.BlockSpec((tile, 2 * wide), lambda j, t: (jnp.minimum(j, steps - 1), 0)) for wide in units
    ]
    return pl.pallas_call(
        functools.partial(normed_grad_kernel, halves, steps, tile, [len(half) for half in far_parts]),
        grid_spec=pltpu.PrefetchScalarGridSpec(
            num_scalar_prefetch=1,
            grid=(2 * steps,),
            in_specs=[whole(part.shape) for part in d_parts]
            + own_specs
            + [whole(piece.shape) for piece in parts],
            out_specs=[pl.BlockSpec((seq_len // 2, tile), lambda j, t: (0, j))]
            + [third(index) for index in range(3)],
            scratch_shapes=[pltpu.VMEM((features, 2 * wide), BF16) for wide in units]
            + [pltpu.VMEM((seq_len, tile), F32)],
        ),
        out_shape=[
            jax.ShapeDtypeStruct((seq_len // 2, 2 * features), F32),
            *[jax.ShapeDtypeStruct((seq_len // 2, 2 * features // 3), BF16)] * 3,
        ],
        compiler_params=params("arbitrary"),
        cost_estimate=cost(
            8 * seq_len * features * sum(units), 8 * sum(units) * (seq_len + features)
        ),
        name="normed_grad",
    )(table, *d_parts, *own, *parts)


def chip_sum_kernel(own_ref, *refs):
    near_refs, (out_ref, *low_refs) = refs[:-3], refs[-3:]
    width = low_refs[0].shape[1]
    start = 0
    for near_ref in near_refs:
        columns = slice(start, start + near_ref.shape[1])
        total = own_ref[:, columns] + near_ref[...].astype(F32)
        out_ref[:, columns] = total
        start += near_ref.shape[1]
    for index, low_ref in enumerate(low_refs):
        low_ref[...] = out_ref[:, index * width : (index + 1) * width].astype(BF16)


def chip_sum(own, nears):
    rows, width = own.shape
    block = pl.BlockSpec((rows // 4, width), lambda i: (i, 0))
    return pl.pallas_call(
        chip_sum_kernel,
        grid=(4,),
        in_specs=[block] + [pl.BlockSpec((rows // 4, near.shape[1]), lambda i: (i, 0)) for near in nears],
        out_specs=[block] + [pl.BlockSpec((rows // 4, width // 2), lambda i: (i, 0))] * 2,
        out_shape=[jax.ShapeDtypeStruct(own.shape, F32)]
        + [jax.ShapeDtypeStruct((rows, width // 2), BF16)] * 2,
        compiler_params=params("arbitrary"),
        cost_estimate=cost(0, 12 * rows * width),
        name="chip_sum",
    )(own, *nears)


def norm_back_kernel(
    width, table, chip_ref, far_own_ref, far_other_ref, hidden_ref, scale_ref, grad_ref, gain_ref, out_ref, low0_ref, low1_ref, gain_grad_ref
):
    @pl.when(pl.program_id(0) == 0)
    def _():
        gain_grad_ref[...] = jnp.zeros_like(gain_grad_ref)

    d_left = chip_ref[:, :width] + far_other_ref[...].astype(F32)
    d_right = chip_ref[:, width:] + far_own_ref[...].astype(F32)
    left, right = hidden_ref[:, :width], hidden_ref[:, width:]
    scale = scale_ref[:, :1]
    gain_grad_ref[...] += jnp.sum(d_left * left * scale, axis=0, keepdims=True)
    left_weighted, right_weighted = d_left * gain_ref[:, :width], d_right * gain_ref[:, width:]
    inner = jnp.sum(left_weighted * left, axis=1, keepdims=True) + jnp.sum(
        right_weighted * right, axis=1, keepdims=True
    )
    factor = scale * scale * (inner / (2 * width))
    d_left = grad_ref[:, :width].astype(F32) + scale * (left_weighted - left * factor)
    d_right = grad_ref[:, width:].astype(F32) + scale * (right_weighted - right * factor)
    out_ref[...] = d_left
    low0_ref[...] = d_left.astype(BF16)
    low1_ref[...] = d_right.astype(BF16)


def norm_back(table, chip, far, hidden, scale, grad, gain):
    rows, width = chip.shape
    block = rows // 4

    def own(columns):
        return pl.BlockSpec((block, columns), lambda i, t: (i, 0))

    def tokens(columns):
        return pl.BlockSpec((block, columns), lambda i, t: (4 * t[ROW] + i, 0))

    return pl.pallas_call(
        functools.partial(norm_back_kernel, width // 2),
        grid_spec=pltpu.PrefetchScalarGridSpec(
            num_scalar_prefetch=1,
            grid=(4,),
            in_specs=[own(width), own(width // 2), own(width // 2), tokens(width), tokens(128), tokens(width), whole((1, width))],
            out_specs=[own(width // 2)] * 3 + [whole((1, width // 2))],
        ),
        out_shape=[
            jax.ShapeDtypeStruct((rows, width // 2), F32),
            jax.ShapeDtypeStruct((rows, width // 2), BF16),
            jax.ShapeDtypeStruct((rows, width // 2), BF16),
            jax.ShapeDtypeStruct((1, width // 2), F32),
        ],
        compiler_params=params("arbitrary"),
        cost_estimate=cost(0, 20 * rows * width),
        name="norm_back",
    )(table, chip, *far, hidden, scale, grad, gain)


def project_back_kernel(
    count, bit, table, query_ref, key_value_ref, arrived_query_ref, arrived_ref, normed_ref, weight_ref, group_ref,
    d_hidden_ref, d_hidden_near_ref, sent_ref, kept_ref, own_ref, other_ref, bias_ref, d_scr, total_scr, hidden_scr, out_scr,
):
    first = table[COL] == 0
    query_width = query_ref.shape[1]
    own, far = query_ref[...], arrived_query_ref[...]
    d_scr[:, :query_width] = jnp.where(first, own, far)
    d_scr[:, query_width : 2 * query_width] = jnp.where(first, far, own)
    d_key_value = key_value_ref[...] + arrived_ref[...].astype(F32)
    d_scr[:, 2 * query_width :] = d_key_value.astype(BF16)
    d_projected = d_scr[...]
    bias_ref[...] = jnp.sum(d_projected.astype(F32), axis=0, keepdims=True)
    total_scr[...] = dot(normed_ref[...], d_projected, 0, 0)
    tokens = own_ref.shape[0]
    hidden_scr[:tokens] = jnp.where(table[ROW] == 0, d_hidden_ref[...], d_hidden_near_ref[...])
    hidden_scr[tokens:] = jnp.where(table[ROW] == 0, d_hidden_near_ref[...], d_hidden_ref[...])
    out_scr[...] = dot(group_ref[...], hidden_scr[...], 0, 0)
    rows = sent_ref.shape[1]
    width = total_scr.shape[1]
    side = table[BITS + bit]
    for out_ref, value in ((sent_ref, 1 - side), (kept_ref, side)):
        for index in range(count // 2):
            start = with_bit(index, bit, value) * rows
            if rows % 8 == 0:
                start = pl.multiple_of(start, 8)
            out_ref[index, :, :width] = total_scr[pl.ds(start, rows)].astype(BF16)
            out_ref[index, :, width:] = out_scr[pl.ds(start, rows)].astype(BF16)
    for out_ref, half in ((own_ref, table[ROW]), (other_ref, 1 - table[ROW])):
        d_half = d_scr[pl.ds(pl.multiple_of(half * tokens, tokens), tokens)]
        out_ref[...] = dot(d_half, weight_ref[...], 1, 1).astype(out_ref.dtype)


def project_back(table, d_query, d_key_value, arrived_query, arrived, normed, weight, group, d_hidden, near, count, bit):
    seq_len = d_query.shape[0]
    width, columns = weight.shape
    rows = width // count
    arrays = (d_query, d_key_value, arrived_query, arrived, normed, weight, group, d_hidden, near)
    terms = (count // 2, rows, columns + d_hidden.shape[1])
    return pl.pallas_call(
        functools.partial(project_back_kernel, count, bit),
        grid_spec=pltpu.PrefetchScalarGridSpec(
            num_scalar_prefetch=1,
            grid=(1,),
            in_specs=[whole(array.shape) for array in arrays],
            out_specs=[
                whole(terms), whole(terms), whole((seq_len // 2, width)), whole((seq_len // 2, width)),
                whole((1, columns)),
            ],
            scratch_shapes=[
                pltpu.VMEM((seq_len, columns), BF16), pltpu.VMEM((width, columns), F32),
                pltpu.VMEM((seq_len, d_hidden.shape[1]), BF16), pltpu.VMEM((width, d_hidden.shape[1]), F32),
            ],
        ),
        out_shape=[
            jax.ShapeDtypeStruct(terms, BF16),
            jax.ShapeDtypeStruct(terms, BF16),
            jax.ShapeDtypeStruct((seq_len // 2, width), F32),
            jax.ShapeDtypeStruct((seq_len // 2, width), BF16),
            jax.ShapeDtypeStruct((1, columns), F32),
        ],
        compiler_params=params("arbitrary"),
        cost_estimate=cost(4 * seq_len * width * columns, 8 * seq_len * columns),
        name="project_back",
    )(table, *arrays)


def swap(part, axis_name):
    return lax.ppermute(part, axis_name, [(0, 1), (1, 0)])


def dp_swap(part, bit):
    count = lax.axis_size("dp")
    return lax.ppermute(part, "dp", [(i, i ^ (1 << bit)) for i in range(count)])


def after(value, *earlier):
    return lax.optimization_barrier((value,) + earlier)[0]


def pick(array, index, axis):
    return lax.dynamic_index_in_dim(array, index, axis, keepdims=False)


def in_order(index, own, other, axis):
    first = jnp.where(index == 0, own, other)
    second = jnp.where(index == 0, other, own)
    return jnp.concatenate([first, second], axis=axis)


def quad_slots(rank):
    low, high = rank % 2, rank // 2 % 2
    return jnp.stack([2 * high + low, 4 + 2 * low + high])


class Line:
    def __init__(self):
        self.last = ()

    def step(self, value):
        return after(value, *self.last) if self.last else value

    def mark(self, *values):
        self.last = values


class Quad:
    def __init__(self, part, rank):
        self.part = part
        self.low, self.high = rank % 2, rank // 2 % 2

    def first_round(self, line):
        part = line.step(self.part)
        self.sent = lax.optimization_barrier((part[0], part[1]))
        line.mark(*self.sent)
        self.arriving = dp_swap(self.sent[0], 0), dp_swap(self.sent[1], 1)

    def second_round(self, line):
        arrived = [line.step(value) for value in self.arriving]
        pairs = lax.optimization_barrier(
            (in_order(self.low, self.sent[0], arrived[0], 0), in_order(self.high, self.sent[1], arrived[1], 0))
        )
        line.mark(*pairs)
        self.parts = [*pairs, dp_swap(pairs[0], 1), dp_swap(pairs[1], 0)]
        return self.parts


def laid_out(parts, rank):
    low, high = rank % 2, rank // 2 % 2
    return [in_order(high, parts[0], parts[2], 0), in_order(low, parts[1], parts[3], 0)]


class Scatter:
    def __init__(self, table, sent, kept, order, line):
        self.table, self.kept = table, kept
        bits = lax.axis_size("dp").bit_length() - 1
        self.order = list(order) + [bit for bit in range(bits) if bit not in order]
        self.left = list(range(bits))
        self.pass_on(sent, line)

    def pass_on(self, sent, line):
        bit = self.order.pop(0)
        self.left.remove(bit)
        self.arriving = dp_swap(line.step(sent), bit)

    def relay(self, line):
        bit = self.order[0]
        sent, self.kept = relay(
            self.table, self.kept, line.step(self.arriving), self.left.index(bit), bit
        )
        line.mark(sent)
        self.pass_on(sent, line)

    def finish(self, line):
        while self.order:
            self.relay(line)
        total = self.kept.astype(F32) + line.step(self.arriving).astype(F32)
        total = lax.optimization_barrier(total)
        line.mark(total)
        return total


def shards(
    block_input,
    segment_ids,
    first_gain,
    qkv_weight,
    qkv_bias,
    output_weight,
    second_gain,
    gate_up_weight,
    down_weight,
    output_grad,
):
    count = lax.axis_size("dp")
    rank = lax.axis_index("dp")
    row = lax.axis_index("row")
    col = lax.axis_index("col")
    qkv_block = qkv_weight[0, 0]
    out_block = output_weight[0, 0]
    gate_up_block = gate_up_weight[0, 0]
    down_block = down_weight[0, 0]
    seq_len = segment_ids.shape[0]
    own_rows, half_width = block_input.shape
    model_width = 2 * half_width
    query_width = HEADS // 4 * HEAD_DIM
    own_units = down_block.shape[0] // 2
    segment = own_units // count
    step = max(16, 128 // count)
    padded = pl.cdiv(segment, 3 * step) * 3 * step
    feature_rows = half_width // count
    slot_rows = half_width // 8
    slots = quad_slots(rank)
    bits = count.bit_length() - 1

    def own_tokens(array):
        return lax.dynamic_slice_in_dim(array, row * own_rows, own_rows, 0)

    def slot_pair(array):
        parts = array.reshape((8, array.shape[0] // 8) + array.shape[1:])
        return jnp.stack([pick(parts, slots[0], 0), pick(parts, slots[1], 0)])

    table = jnp.stack([row, col] + [(rank >> bit) & 1 for bit in range(bits)]).astype(jnp.int32)
    line = Line()
    pair_first, line_first = [0, 1, 2], [1, 2, 0]

    def qkv_columns(side):
        heads = lax.dynamic_slice_in_dim(qkv_block, side * query_width, query_width, 1)
        return jnp.concatenate([heads, qkv_block[:, 2 * query_width :]], axis=1)

    gains = jnp.stack([first_gain, second_gain])
    gains = jnp.concatenate([gains, swap(gains, "col")], axis=1)
    early_send = slot_pair(jnp.concatenate([qkv_columns(1 - col), out_block], axis=1))
    early_quad = Quad(swap(early_send, "col"), rank)
    qkv_own = qkv_columns(col)
    qkv_width = qkv_own.shape[1]
    bias = qkv_bias[0]
    bias_own = jnp.concatenate(
        [lax.dynamic_slice_in_dim(bias, col * query_width, query_width, 0), bias[2 * query_width :]]
    )

    (send,) = unit_columns(
        after(gate_up_block, early_send, gains), 1 - col, slots, count, slot_rows, padded, (0,)
    )
    line.mark(send)

    near = swap(block_input, "row")
    far = swap(line.step(block_input), "col")

    position_index = jnp.arange(seq_len, dtype=jnp.int32)
    doc_first = jnp.concatenate([jnp.ones((1,), jnp.bool_), segment_ids[1:] != segment_ids[:-1]])
    positions = position_index - lax.cummax(jnp.where(doc_first, position_index, 0), axis=0)
    frequency = ROPE_BASE ** (-jnp.arange(0, HEAD_DIM, 2, dtype=F32) / HEAD_DIM)
    angles = positions.astype(F32)[:, None] * frequency[None, :]
    cosine, sine = jnp.cos(angles), jnp.sin(angles)
    cosine = jnp.concatenate([cosine, cosine], axis=1)
    sine = jnp.concatenate([-sine, sine], axis=1)
    seg_col, seg_row = segment_ids[:, None], segment_ids[None, :]

    low_slots, high_slots = jnp.arange(4), 4 + jnp.arange(4)
    gate_up_own = unit_columns(
        line.step(gate_up_block), col, low_slots, count, slot_rows, padded, (0, 1), low_slots, 8
    )
    line.mark(*gate_up_own)
    early_quad.first_round(line)
    gate_up_quad = Quad(swap(line.step(send), "col"), rank)
    early_far = early_quad.second_round(line)
    down_own = unit_rows(line.step(down_block), col, jnp.arange(count), count, padded)
    line.mark(*down_own)
    down_own = [part.reshape(-1, half_width) for part in down_own]
    far_halves = lax.optimization_barrier((far[: own_rows // 2], far[own_rows // 2 :]))
    far_near = [swap(half, "row") for half in far_halves]
    gate_up_own = unit_columns(
        line.step(gate_up_block), col, high_slots, count, slot_rows, padded, (0, 1), high_slots, 8, gate_up_own
    )
    line.mark(*gate_up_own)
    gate_up_own = [part.reshape(half_width, -1) for part in gate_up_own]
    out_near = swap(out_block, "row")
    stream, first_normed, first_scale, query, key, value = project(
        table, line.step(block_input), near, far, far_near, gains[:1], qkv_own, early_far,
        bias_own[None], cosine, sine,
    )
    line.mark(query)
    gate_up_quad.first_round(line)
    attended = attend(line.step(query), key, value, seg_col, seg_row)
    line.mark(*attended)
    attended_far = [swap(part, "col") for part in attended]
    attended_near = [swap(part, "row") for part in attended]
    gate_up_far = [gate_up_quad.second_round(line)]
    out_far = lax.optimization_barrier(
        laid_out([line.step(part)[:, qkv_width:] for part in early_far], rank)
    )
    line.mark(*out_far)
    out_far_near = [swap(part, "row") for part in out_far]
    share = count // 8
    send_ranks = (slots[:, None] * share + jnp.arange(share)[None, :]).reshape(-1)
    (down_send,) = unit_rows(line.step(down_block), 1 - col, send_ranks, count, padded, (0,))
    line.mark(down_send)
    (send,) = unit_columns(
        line.step(gate_up_block), 1 - col, jnp.arange(8), count, slot_rows, padded, (1,)
    )
    line.mark(send)
    attended_far = [line.step(part) for part in attended_far]
    line.mark(*attended_far)
    attended_far_near = [swap(part, "row") for part in attended_far]
    down_quad = Quad(swap(line.step(down_send).reshape(2, -1, half_width), "col"), rank)
    grad_far = swap(line.step(output_grad), "col")
    hidden_one, second_normed, second_scale, attended_group = residual(
        table, line.step(stream), (attended, attended_far, attended_near, attended_far_near),
        out_block, out_near, out_far, out_far_near, gains[1:],
    )
    line.mark(second_normed)
    gate_up_far[0] = [line.step(part) for part in gate_up_far[0]]
    line.mark(*gate_up_far[0])
    down_quad.first_round(line)

    act0, gate_factor0, up_factor0 = activate(
        table, line.step(second_normed), gate_up_own[0], gate_up_far[0]
    )
    line.mark(act0)
    grad_far = line.step(grad_far)
    line.mark(grad_far)
    down_far = [down_quad.second_round(line)]
    grad_near = swap(line.step(output_grad), "row")
    grad_far_near = swap(grad_far, "row")
    gate_up_far.append([swap(line.step(send).reshape(half_width, -1), "col")])
    grad_full = join(table, line.step(output_grad), grad_near, grad_far, grad_far_near)
    line.mark(grad_full)

    def down_terms(act, order):
        sent, kept = split_product(
            table, line.step(act), [(grad_full, 0, 2)], half_width, 1, count, [order[0]]
        )
        line.mark(sent)
        return sent, kept

    def gate_up_terms(d_gate, d_up, order, merge):
        tile = tile_of(d_gate.shape[1])
        rights = [(part, 0, part.shape[1] // tile) for part in (d_gate, d_up)]
        terms = split_product(
            table, line.step(second_normed), rights, tile, 2, count, [order[0]] * 2, merge
        )
        line.mark(terms[0])
        return terms

    terms = down_terms(act0, pair_first)
    down_far[0] = [line.step(part) for part in down_far[0]]
    line.mark(*down_far[0])
    down_sum0 = Scatter(table, *terms, pair_first, line)
    d_gate0, d_up0 = activate_back(
        table, line.step(grad_full), down_own[0], down_far[0], gate_factor0, up_factor0
    )
    line.mark(d_gate0)
    own_sent0, own_kept0, far_sent0, far_kept0 = gate_up_terms(d_gate0, d_up0, pair_first, False)
    far_sum0 = Scatter(table, far_sent0, far_kept0, pair_first, line)
    begin, width, full = halves_of(segment, padded)[1]
    down_send = pick(line.step(down_block).reshape(count, 2, segment, half_width), 1 - col, 1)
    down_send = jnp.pad(down_send[:, begin : begin + width], ((0, 0), (0, full - width), (0, 0)))
    down_send = lax.optimization_barrier(down_send.reshape(-1, half_width))
    line.mark(down_send)
    down_far.append([swap(down_send, "col")])
    act1, gate_factor1, up_factor1 = activate(
        table, line.step(second_normed), gate_up_own[1], gate_up_far[1]
    )
    line.mark(act1)
    down_sum0.relay(line)
    d_gate1, d_up1 = activate_back(
        table, line.step(grad_full), down_own[1], down_far[1], gate_factor1, up_factor1
    )
    line.mark(d_gate1)
    d_second_own, *d_second_other = normed_grad(
        table, [line.step(d_gate0), d_up0, d_gate1, d_up1], gate_up_own, gate_up_far
    )
    line.mark(*d_second_other)
    d_second_near = [swap(part, "row") for part in d_second_other]
    down_terms1 = down_terms(act1, pair_first)
    down_sum0.relay(line)
    d_second_chip, *d_second_low = chip_sum(line.step(d_second_own), d_second_near)
    line.mark(*d_second_low)
    d_second_far = [swap(part, "col") for part in d_second_low]
    far_sum0.relay(line)
    own_sum0 = Scatter(table, own_sent0, own_kept0, pair_first, line)
    gate_up_terms1 = gate_up_terms(d_gate1, d_up1, pair_first, True)
    mlp_own, mlp_other = down(table, [line.step(act0), act1], down_own, down_far)
    line.mark(mlp_other)
    far_sum0.relay(line)

    d_hidden, *d_hidden_low, second_gain_part = norm_back(
        table, line.step(d_second_chip), d_second_far, hidden_one, second_scale, grad_full, gains[1:]
    )
    line.mark(*d_hidden_low)
    d_hidden_near = [swap(part, "row") for part in d_hidden_low]
    down_sum0 = down_sum0.finish(line)[0]
    own_sum0.relay(line)
    gate_up_sum1 = Scatter(table, *gate_up_terms1, pair_first, line)

    d_query, d_key_value = attend_back(
        table, line.step(query), key, value, seg_col, seg_row, [*d_hidden_low, *d_hidden_near],
        out_block, out_far, cosine, sine,
    )
    d_key_value_low = lax.optimization_barrier(d_key_value.astype(BF16))
    line.mark(d_query, d_key_value_low)
    arrived = swap(d_query, "col"), swap(d_key_value_low, "col")
    far_sum0 = far_sum0.finish(line)[0]
    sent, kept, d_first_own, d_first_other, bias_part = project_back(
        table, line.step(d_query), d_key_value, *arrived, first_normed, qkv_block, attended_group,
        d_hidden_low[0], d_hidden_near[0], count, 0,
    )
    line.mark(sent)
    heads_sum = Scatter(table, sent, kept, pair_first, line)
    d_first_near = swap(d_first_other, "row")
    own_sum0.relay(line)

    d_first = line.step(d_first_own) + d_first_near.astype(F32)
    stream_own = block_input.astype(F32)
    first_scale_own = own_tokens(first_scale)[:, :1]
    first_gain_part = jnp.sum(d_first * stream_own * first_scale_own, axis=0)
    weighted = d_first * first_gain
    inner = jnp.sum(weighted * stream_own, axis=1)
    inner = (inner + swap(inner, "col"))[:, None]
    input_grad = d_hidden + first_scale_own * (
        weighted - stream_own * (first_scale_own * first_scale_own) * (inner / model_width)
    )

    gain_parts = jnp.concatenate([first_gain_part, second_gain_part[0]])
    gain_parts = lax.optimization_barrier(gain_parts + swap(gain_parts, "row"))
    line.mark(gain_parts)
    small = line.step(jnp.concatenate([gain_parts, bias_part[0]]))

    def dp_step(part, bit):
        part = lax.optimization_barrier(part + line.step(dp_swap(part, bit)))
        line.mark(part)
        return part

    gate_up_sum1.relay(line)
    down_sum1 = Scatter(table, *down_terms1, pair_first, line)
    mlp_chip = mlp_own + swap(line.step(mlp_other), "row").astype(F32)
    mlp_sent = lax.optimization_barrier(mlp_chip[:, half_width:].astype(BF16))
    line.mark(mlp_sent)
    mlp_far = swap(mlp_sent, "col").astype(F32)
    hidden_own = own_tokens(hidden_one)[:, :half_width]
    block_output = (hidden_own + (mlp_chip[:, :half_width] + mlp_far)).astype(BF16)
    down_sum0_far = swap(line.step(down_sum0[:, half_width:].astype(BF16)), "col")
    far_sum0 = swap(line.step(far_sum0.astype(BF16)), "col")
    heads_sum.relay(line)
    small = dp_step(small, 0)
    own_sum0 = own_sum0.finish(line)[0]
    gate_up_sum1.relay(line)
    heads_sum.relay(line)
    down_sum1.relay(line)
    small = dp_step(small, 1)
    own_sum1, far_sum1 = gate_up_sum1.finish(line)
    far_sum1 = swap(line.step(far_sum1.astype(BF16)), "col")
    down_sum1.relay(line)
    heads_sum = heads_sum.finish(line)[0]
    for bit in range(2, bits):
        small = dp_step(small, bit)
    qkv_sum, out_sum = heads_sum[:, : bias.shape[0]], heads_sum[:, bias.shape[0] :]
    down_sum1 = down_sum1.finish(line)[0]
    down_sum1_far = swap(line.step(down_sum1[:, half_width:].astype(BF16)), "col")
    bias_width = bias.shape[0] // count
    bias_grad = lax.dynamic_slice_in_dim(small[model_width:], rank * bias_width, bias_width, 0)

    widths = [width for _, width, _ in halves_of(segment, padded)]
    own_rows_sum = [
        part[:width, :half_width] for part, width in zip((down_sum0, down_sum1), widths)
    ]
    far_rows_sum = [
        part[:width].astype(F32) for part, width in zip((down_sum0_far, down_sum1_far), widths)
    ]
    down_grad = in_order(
        col, jnp.concatenate(own_rows_sum, axis=0), jnp.concatenate(far_rows_sum, axis=0), 0
    )
    gate_up_grad = spread_columns(
        table, (own_sum0, own_sum1), (far_sum0, far_sum1), count, segment, padded
    )

    return (
        block_output,
        input_grad,
        small[:half_width],
        qkv_sum[None, None],
        bias_grad[None],
        out_sum[None, None],
        small[half_width:model_width],
        gate_up_grad[None, None],
        down_grad[None, None],
    )


def solution(mesh):
    placed = (
        P(("dp", "row"), "col"),
        P("dp"),
        P("col"),
        P("col", "row", None, None),
        P("row", None),
        P("row", "col", None, None),
        P("col"),
        P("col", "row", None, None),
        P("row", "col", None, None),
        P(("dp", "row"), "col"),
    )
    return jax.shard_map(
        shards,
        mesh=mesh,
        in_specs=placed,
        out_specs=(
            P(("dp", "row"), "col"),
            P(("dp", "row"), "col"),
            P("col"),
            P("col", "row", "dp", None),
            P("row", "dp"),
            P("row", "col", "dp", None),
            P("col"),
            P("col", "row", "dp", None),
            P("row", "col", "dp", None),
        ),
        check_vma=False,
    )
```

```python
import functools
import jax
import jax.numpy as jnp
from jax import lax
from jax.experimental import pallas as pl
from jax.experimental.pallas import tpu as pltpu
from jax.sharding import PartitionSpec as P

HEADS = 12
KV_HEADS = 2
HEAD_DIM = 128
EPSILON = 1e-06
ROPE_BASE = 1000000.0
MASKED = -1e30
F32 = jnp.float32
BF16 = jnp.bfloat16
VMEM_LIMIT = 60 * 1024 * 1024


def dot(left, right, left_dim, right_dim):
    return lax.dot_general(
        left, right, (((left_dim,), (right_dim,)), ((), ())), preferred_element_type=F32
    )


def params(*semantics):
    return pltpu.CompilerParams(
        dimension_semantics=semantics or None, vmem_limit_bytes=VMEM_LIMIT
    )


def cost(flops, moved):
    return pl.CostEstimate(flops=1, bytes_accessed=1, transcendentals=0)


def whole(shape):
    return pl.BlockSpec(shape, lambda *_: (0,) * len(shape))


ROW, COL, LOW, HIGH = range(4)
BITS = 2


def with_bit(index, place, value):
    return ((index >> place) << (place + 1)) | (value << place) | (index & ((1 << place) - 1))


def ordered(table, parts, columns=slice(None)):
    if len(parts) == 1:
        return parts[0][:, columns]
    first, second, first_other, second_other = [part[:, columns] for part in parts]
    high, low = table[HIGH] == 0, table[LOW] == 0
    return jnp.concatenate(
        [
            jnp.where(high, first, first_other),
            jnp.where(high, first_other, first),
            jnp.where(low, second, second_other),
            jnp.where(low, second_other, second),
        ],
        axis=0,
    )


def halves_of(segment, padded):
    first = 2 * padded // 3
    return ((0, first, first), (first, segment - first, padded - first))


def units_kernel(count, segment, padded, outs, table, block_ref, *refs):
    rows = block_ref.shape[0]
    out_refs = refs[-len(outs) :]

    def write(side):
        for out_ref, (other, half) in zip(out_refs, outs):
            begin, width, full = halves_of(segment, padded)[half]
            parts = []
            for kind in range(2):
                for k in range(count):
                    start = ((kind * count + k) * 2 + (side ^ other)) * segment + begin
                    parts.append(block_ref[:, start : start + width])
                    if width < full:
                        parts.append(jnp.zeros((rows, full - width), block_ref.dtype))
            out_ref[0] = jnp.concatenate(parts, axis=1)

    @pl.when(table[0] == 0)
    def _():
        write(0)

    @pl.when(table[0] != 0)
    def _():
        write(1)


def unit_columns(block, side, slots, count, rows, padded, outs, places=None, depth=None, begun=None):
    columns = block.shape[1]
    segment = columns // (4 * count)
    units = [2 * count * halves_of(segment, padded)[half][2] for _, half in outs]
    steps = slots.shape[0]
    depth = steps if depth is None else depth
    places = jnp.arange(steps) if places is None else places
    begun = [] if begun is None else begun
    table = jnp.concatenate([side.reshape(1), slots, places]).astype(jnp.int32)
    return pl.pallas_call(
        functools.partial(units_kernel, count, segment, padded, outs),
        grid_spec=pltpu.PrefetchScalarGridSpec(
            num_scalar_prefetch=1,
            grid=(steps,),
            in_specs=[pl.BlockSpec((rows, columns), lambda i, t: (t[1 + i], 0))]
            + [pl.BlockSpec(memory_space=pl.ANY)] * len(begun),
            out_specs=[pl.BlockSpec((1, rows, wide), lambda i, t: (t[1 + steps + i], 0, 0)) for wide in units],
        ),
        out_shape=[jax.ShapeDtypeStruct((depth, rows, wide), block.dtype) for wide in units],
        input_output_aliases={2 + index: index for index in range(len(begun))},
        compiler_params=params("arbitrary"),
        cost_estimate=cost(0, 4 * steps * rows * sum(units)),
        name="unit_columns",
    )(table, block, *begun)


def unit_rows_kernel(parts, table, block_ref, *out_refs):
    for out_ref, (begin, width, full) in zip(out_refs, parts):
        if width == full and begin % 16 == 0 and full % 16 == 0:
            out_ref[0] = block_ref[0, 0, begin : begin + width]
        else:
            part = block_ref[0, 0].astype(F32)[begin : begin + width]
            part = jnp.concatenate([part, jnp.zeros((full - width, part.shape[1]), F32)], axis=0)
            out_ref[0] = part.astype(out_ref.dtype)


def unit_rows(block, side, ranks, count, padded, halves=(0, 1)):
    rows, width = block.shape
    segment = rows // (2 * count)
    parts = [halves_of(segment, padded)[half] for half in halves]
    steps = ranks.shape[0]
    table = jnp.concatenate([side.reshape(1), ranks]).astype(jnp.int32)
    return pl.pallas_call(
        functools.partial(unit_rows_kernel, parts),
        grid_spec=pltpu.PrefetchScalarGridSpec(
            num_scalar_prefetch=1,
            grid=(steps,),
            in_specs=[pl.BlockSpec((1, 1, segment, width), lambda i, t: (t[1 + i], t[0], 0, 0))],
            out_specs=[pl.BlockSpec((1, full, width), lambda i, t: (i, 0, 0)) for _, _, full in parts],
        ),
        out_shape=[jax.ShapeDtypeStruct((steps, full, width), block.dtype) for _, _, full in parts],
        compiler_params=params("arbitrary"),
        cost_estimate=cost(0, 4 * steps * segment * width),
        name="unit_rows",
    )(table, block.reshape(count, 2, segment, width))


def spread_kernel(count, segment, padded, table, own0_ref, own1_ref, far0_ref, far1_ref, out_ref):
    def write(sides):
        pieces = []
        for kind in range(2):
            for k in range(count):
                for side in sides:
                    for ref, (_, width, full) in zip(side, halves_of(segment, padded)):
                        start = (kind * count + k) * full
                        pieces.append(ref[:, start : start + width].astype(F32))
        out_ref[...] = jnp.concatenate(pieces, axis=1)

    own, far = (own0_ref, own1_ref), (far0_ref, far1_ref)

    @pl.when(table[COL] == 0)
    def _():
        write((own, far))

    @pl.when(table[COL] != 0)
    def _():
        write((far, own))


def spread_columns(table, own, far, count, segment, padded):
    rows = own[0].shape[0]
    step = rows // 3 if rows % 24 == 0 else rows
    parts = [pl.BlockSpec((step, part.shape[1]), lambda i, t: (i, 0)) for part in (*own, *far)]
    columns = 4 * count * segment
    return pl.pallas_call(
        functools.partial(spread_kernel, count, segment, padded),
        grid_spec=pltpu.PrefetchScalarGridSpec(
            num_scalar_prefetch=1,
            grid=(rows // step,),
            in_specs=parts,
            out_specs=pl.BlockSpec((step, columns), lambda i, t: (i, 0)),
        ),
        out_shape=jax.ShapeDtypeStruct((rows, columns), F32),
        compiler_params=params("arbitrary"),
        cost_estimate=cost(0, 7 * rows * columns),
        name="spread_columns",
    )(table, *own, *far)


def project_kernel(
    width, table, own_ref, near_ref, far_ref, far_near0_ref, far_near1_ref, gain_ref, weight_ref,
    part0_ref, part1_ref, part2_ref, part3_ref, bias_ref, cosine_ref, sine_ref, stream_ref, normed_ref, scale_ref, query_ref, key_ref, value_ref,
):
    half = pl.program_id(0) * 2 // pl.num_programs(0)
    mine = half == table[ROW]
    left = jnp.where(mine, own_ref[...], near_ref[...]).astype(F32)
    even = pl.program_id(0) % 2 == 0
    right = jnp.where(
        mine,
        far_ref[...],
        jnp.where(even, far_near0_ref[...], far_near1_ref[...]),
    ).astype(F32)
    squares = jnp.sum(left * left, axis=1, keepdims=True) + jnp.sum(
        right * right, axis=1, keepdims=True
    )
    scale = lax.rsqrt(squares / (2 * width) + EPSILON)
    left_normed = (left * scale * gain_ref[:, :width]).astype(BF16)
    right_normed = (right * scale * gain_ref[:, width:]).astype(BF16)
    stream_ref[:, :width] = left.astype(BF16)
    stream_ref[:, width:] = right.astype(BF16)
    normed_ref[...] = left_normed
    scale_ref[...] = jnp.broadcast_to(scale, scale_ref.shape)
    far_weight = ordered(table, (part0_ref, part1_ref, part2_ref, part3_ref))
    projected = (
        dot(left_normed, weight_ref[...], 1, 0) + dot(right_normed, far_weight, 1, 0) + bias_ref[...]
    )
    cosine, sine = cosine_ref[...], sine_ref[...]

    def rotated(values):
        return (values * cosine + pltpu.roll(values, HEAD_DIM // 2, 1) * sine).astype(BF16)

    query_width = query_ref.shape[1]
    for start in range(0, query_width, HEAD_DIM):
        query_ref[:, start : start + HEAD_DIM] = rotated(projected[:, start : start + HEAD_DIM])
    key_ref[...] = rotated(projected[:, query_width : query_width + HEAD_DIM])
    value_ref[...] = projected[:, query_width + HEAD_DIM :].astype(BF16)


def project(table, own, near, far, far_near, gain, weight, far_parts, bias, cosine, sine):
    rows, width = own.shape
    seq_len = 2 * rows
    block = rows // 2
    per_half = 2
    out_width = weight.shape[1]
    query_width = out_width - 2 * HEAD_DIM
    part = pl.BlockSpec((block, width), lambda i, t: (i % per_half, 0))

    def tokens(columns):
        return pl.BlockSpec((block, columns), lambda i, t: (i, 0))

    return pl.pallas_call(
        functools.partial(project_kernel, width),
        grid_spec=pltpu.PrefetchScalarGridSpec(
            num_scalar_prefetch=1,
            grid=(seq_len // block,),
            in_specs=[part, part, part]
            + [whole((block, width))] * 2
            + [whole((1, 2 * width)), whole(weight.shape)]
            + [whole((piece.shape[0], out_width)) for piece in far_parts]
            + [whole((1, out_width)), tokens(HEAD_DIM), tokens(HEAD_DIM)],
            out_specs=[
                tokens(2 * width), tokens(width), tokens(128),
                tokens(query_width), tokens(HEAD_DIM), tokens(HEAD_DIM),
            ],
        ),
        out_shape=[
            jax.ShapeDtypeStruct((seq_len, 2 * width), BF16),
            jax.ShapeDtypeStruct((seq_len, width), BF16),
            jax.ShapeDtypeStruct((seq_len, 128), F32),
            jax.ShapeDtypeStruct((seq_len, query_width), BF16),
            jax.ShapeDtypeStruct((seq_len, HEAD_DIM), BF16),
            jax.ShapeDtypeStruct((seq_len, HEAD_DIM), BF16),
        ],
        compiler_params=params("arbitrary"),
        cost_estimate=cost(4 * seq_len * width * out_width, 12 * seq_len * width),
        name="project",
    )(table, own, near, far, *far_near, gain, weight, *far_parts, bias, cosine, sine)


def join_kernel(width, table, own_ref, near_ref, far_ref, far_near_ref, out_ref):
    mine = pl.program_id(0) * 2 // pl.num_programs(0) == table[ROW]
    out_ref[:, :width] = jnp.where(mine, own_ref[...], near_ref[...])
    out_ref[:, width:] = jnp.where(mine, far_ref[...], far_near_ref[...])


def join(table, own, near, far, far_near):
    rows, width = own.shape
    block = min(256, rows)
    per_half = rows // block
    part = pl.BlockSpec((block, width), lambda i, t: (i % per_half, 0))
    return pl.pallas_call(
        functools.partial(join_kernel, width),
        grid_spec=pltpu.PrefetchScalarGridSpec(
            num_scalar_prefetch=1,
            grid=(2 * rows // block,),
            in_specs=[part] * 4,
            out_specs=pl.BlockSpec((block, 2 * width), lambda i, t: (i, 0)),
        ),
        out_shape=jax.ShapeDtypeStruct((2 * rows, 2 * width), own.dtype),
        compiler_params=params("arbitrary"),
        cost_estimate=cost(0, 16 * rows * width),
        name="join",
    )(table, own, near, far, far_near)


def block_probs(query, key, seg_col, seg_row, start, stop):
    scores = dot(query, key, 1, 1) * HEAD_DIM ** (-0.5)
    rows = stop - start
    query_index = start + lax.broadcasted_iota(jnp.int32, (rows, stop), 0)
    key_index = lax.broadcasted_iota(jnp.int32, (rows, stop), 1)
    allowed = (key_index <= query_index) & (seg_col == seg_row)
    scores = jnp.where(allowed, scores, MASKED)
    exponent = jnp.exp(scores - jnp.max(scores, axis=1, keepdims=True))
    return exponent / jnp.sum(exponent, axis=1, keepdims=True)


def attend_kernel(block, query_ref, key_ref, value_ref, seg_col_ref, seg_row_ref, all_ref, out_ref, last_ref):
    last = pl.program_id(0) == pl.num_programs(0) - 1
    for start in range(0, query_ref.shape[0], block):
        stop = start + block
        probs = block_probs(
            query_ref[start:stop], key_ref[:stop], seg_col_ref[start:stop], seg_row_ref[:, :stop], start, stop
        )
        out = dot(probs.astype(BF16), value_ref[:stop], 1, 0).astype(BF16)
        all_ref[start:stop] = out

        @pl.when(last)
        def _():
            last_ref[start:stop] = out

        @pl.when(jnp.logical_not(last))
        def _():
            out_ref[start:stop] = out


def attend(query, key, value, seg_col, seg_row):
    seq_len, width = query.shape
    heads = width // HEAD_DIM
    head = pl.BlockSpec((seq_len, HEAD_DIM), lambda h: (0, h))
    shared = whole((seq_len, HEAD_DIM))
    return pl.pallas_call(
        functools.partial(attend_kernel, 256),
        grid=(width // HEAD_DIM,),
        in_specs=[head, shared, shared, whole((seq_len, 1)), whole((1, seq_len))],
        out_specs=[head, pl.BlockSpec((seq_len, HEAD_DIM), lambda h: (0, jnp.minimum(h, heads - 2))), shared],
        out_shape=[
            jax.ShapeDtypeStruct((seq_len, width), BF16),
            jax.ShapeDtypeStruct((seq_len, width - HEAD_DIM), BF16),
            jax.ShapeDtypeStruct((seq_len, HEAD_DIM), BF16),
        ],
        compiler_params=params("arbitrary"),
        cost_estimate=cost(12 * seq_len * seq_len * width, 8 * seq_len * width),
        name="attend",
    )(query, key, value, seg_col, seg_row)


def attend_back_kernel(
    block, begun, ends, table, query_ref, key_ref, value_ref, seg_col_ref, seg_row_ref, own_ref, far_ref, near_ref, far_near_ref,
    weight_ref, far_top_ref, far_bottom_ref, cosine_ref, sine_ref, *refs
):
    sent_ref, key_value_ref = refs[-2:]
    scaling = HEAD_DIM ** (-0.5)
    own_rows = own_ref.shape[0]
    far_weight = jnp.where(table[COL] == 0, far_top_ref[...], far_bottom_ref[...])

    @pl.when(pl.program_id(0) == 0)
    def _():
        key_value_ref[...] = refs[0][...] if begun else jnp.zeros_like(key_value_ref)

    for start in range(0, query_ref.shape[0], block):
        stop = start + block
        mine = table[ROW] == start // own_rows
        place = slice(start % own_rows, start % own_rows + block)
        grad = (
            dot(jnp.where(mine, own_ref[place], near_ref[place]), weight_ref[...], 1, 1)
            + dot(jnp.where(mine, far_ref[place], far_near_ref[place]), far_weight, 1, 1)
        ).astype(BF16)
        query = query_ref[start:stop]
        key, value = key_ref[:stop], value_ref[:stop]
        probs = block_probs(
            query, key, seg_col_ref[start:stop], seg_row_ref[:, :stop], start, stop
        )
        d_probs = dot(grad, value, 1, 1)
        d_scores = probs * (d_probs - jnp.sum(d_probs * probs, axis=1, keepdims=True))
        d_scores = d_scores.astype(BF16)
        d_query = dot(d_scores, key, 1, 0) * scaling
        turned = pltpu.roll(d_query * sine_ref[start:stop], HEAD_DIM // 2, 1)
        sent_ref[start:stop] = (d_query * cosine_ref[start:stop] + turned).astype(BF16)
        key_value_ref[:stop, :HEAD_DIM] += dot(d_scores, query, 0, 0) * scaling
        key_value_ref[:stop, HEAD_DIM:] += dot(probs.astype(BF16), grad, 0, 0)

    if ends:

        @pl.when(pl.program_id(0) == pl.num_programs(0) - 1)
        def _():
            d_key = key_value_ref[:, :HEAD_DIM]
            turned = pltpu.roll(d_key * sine_ref[...], HEAD_DIM // 2, 1)
            key_value_ref[:, :HEAD_DIM] = d_key * cosine_ref[...] + turned


def attend_back(
    table, query, key, value, seg_col, seg_row, d_hidden, weight, far_weights, cosine, sine, first, count, begun=None
):
    seq_len, width = query.shape
    features = weight.shape[1]
    heads = width // HEAD_DIM
    head = pl.BlockSpec((seq_len, HEAD_DIM), lambda h, t: (0, first + h))
    rows = pl.BlockSpec((HEAD_DIM, features), lambda h, t: (heads * t[COL] + first + h, 0))
    far_rows = pl.BlockSpec((HEAD_DIM, features), lambda h, t: (first + h, 0))
    shared = whole((seq_len, HEAD_DIM))
    key_value = whole((seq_len, 2 * HEAD_DIM))
    more = [] if begun is None else [begun]
    return pl.pallas_call(
        functools.partial(attend_back_kernel, 256, begun is not None, first + count == heads),
        grid_spec=pltpu.PrefetchScalarGridSpec(
            num_scalar_prefetch=1,
            grid=(count,),
            in_specs=[
                head, shared, shared, whole((seq_len, 1)), whole((1, seq_len)),
                *[whole(part.shape) for part in d_hidden], rows, far_rows, far_rows, shared, shared,
                *[key_value] * len(more),
            ],
            out_specs=[pl.BlockSpec((seq_len, HEAD_DIM), lambda h, t: (0, h)), key_value],
        ),
        out_shape=[
            jax.ShapeDtypeStruct((seq_len, count * HEAD_DIM), BF16),
            jax.ShapeDtypeStruct((seq_len, 2 * HEAD_DIM), F32),
        ],
        compiler_params=params("arbitrary"),
        cost_estimate=cost(24 * seq_len * seq_len * count * HEAD_DIM, 12 * seq_len * width),
        name="attend_back",
    )(table, query, key, value, seg_col, seg_row, *d_hidden, weight, *far_weights, cosine, sine, *more)


def residual_kernel(table, stream_ref, *refs):
    pieces, weights, (gain_ref, hidden_ref, normed_ref, scale_ref, group_ref) = refs[:6], refs[6:12], refs[12:]
    first = table[COL] == 0
    own, near = pieces[0][...], pieces[1][...]
    far, near_far = (
        jnp.concatenate([pieces[index][...], pieces[index + 1][...]], axis=1) for index in (2, 4)
    )
    part = own.shape[1]
    group = [jnp.where(first, own, far), jnp.where(first, far, own)]
    other = [jnp.where(first, near, near_far), jnp.where(first, near_far, near)]
    group_ref[:, :part] = group[0]
    group_ref[:, part:] = group[1]
    own_w, near_w, *far_w = weights
    width = own_w.shape[1]
    halves = []
    for index in range(2):
        total = stream_ref[:, index * width : (index + 1) * width].astype(F32)
        for place in range(2):
            rows = slice(place * part, (place + 1) * part)
            mine, theirs = (own_w[rows], near_w[rows]) if index == 0 else (far_w[place][...], far_w[2 + place][...])
            total = total + dot(group[place], mine, 1, 0)
            total = total + dot(other[place], theirs, 1, 0)
        halves.append(total)
    squares = sum(jnp.sum(total * total, axis=1, keepdims=True) for total in halves)
    scale = lax.rsqrt(squares / (2 * width) + EPSILON)
    scale_ref[...] = jnp.broadcast_to(scale, scale_ref.shape)
    for index, total in enumerate(halves):
        columns = slice(index * width, (index + 1) * width)
        hidden_ref[:, columns] = total
        normed_ref[:, columns] = (total * scale * gain_ref[:, columns]).astype(BF16)


def residual(table, stream, attended, own_weight, near_weight, far_weights, near_far_weights, gain):
    seq_len, width = stream.shape
    pieces = attended
    part = attended[0].shape[1]
    weights = [own_weight, near_weight, *far_weights, *near_far_weights]
    block = min(256, seq_len)

    def tokens(columns):
        return pl.BlockSpec((block, columns), lambda i, t: (i, 0))

    return pl.pallas_call(
        residual_kernel,
        grid_spec=pltpu.PrefetchScalarGridSpec(
            num_scalar_prefetch=1,
            grid=(seq_len // block,),
            in_specs=[tokens(width)]
            + [tokens(piece.shape[1]) for piece in pieces]
            + [whole(weight.shape) for weight in weights]
            + [whole((1, width))],
            out_specs=[tokens(width), tokens(width), tokens(128), tokens(2 * part)],
        ),
        out_shape=[
            jax.ShapeDtypeStruct((seq_len, width), F32),
            jax.ShapeDtypeStruct((seq_len, width), BF16),
            jax.ShapeDtypeStruct((seq_len, 128), F32),
            jax.ShapeDtypeStruct((seq_len, 2 * part), BF16),
        ],
        compiler_params=params("arbitrary"),
        cost_estimate=cost(2 * seq_len * width * width, 14 * seq_len * width),
        name="residual",
    )(table, stream, *pieces, *weights, gain)


def activate_kernel(width, table, normed_ref, own_gate_ref, own_up_ref, *refs):
    (act_ref, gate_factor_ref, up_factor_ref), refs = refs[-3:], refs[:-3]
    gate_parts, up_parts = refs[: len(refs) // 2], refs[len(refs) // 2 :]
    left, right = normed_ref[:, :width], normed_ref[:, width:]
    gate = dot(left, own_gate_ref[...], 1, 0) + dot(right, ordered(table, gate_parts), 1, 0)
    up = dot(left, own_up_ref[...], 1, 0) + dot(right, ordered(table, up_parts), 1, 0)
    sigmoid = jax.nn.sigmoid(gate)
    silu = gate * sigmoid
    act_ref[...] = (silu * up).astype(BF16)
    gate_factor_ref[...] = (up * (sigmoid * (1.0 + gate * (1.0 - sigmoid)))).astype(BF16)
    up_factor_ref[...] = silu.astype(BF16)


def tile_of(units):
    return next(t for t in (384, 256, 128, units) if units % t == 0)


def activate(table, normed, own, far_parts):
    seq_len, width = normed.shape
    units = own.shape[1] // 2
    tile = tile_of(units)
    steps = units // tile

    def gate(rows):
        return pl.BlockSpec((rows, tile), lambda j, t: (0, j))

    def up(rows):
        return pl.BlockSpec((rows, tile), lambda j, t: (0, steps + j))

    rows = far_parts[0].shape[0]
    out = pl.BlockSpec((seq_len, tile), lambda j, t: (0, j))
    return pl.pallas_call(
        functools.partial(activate_kernel, width // 2),
        grid_spec=pltpu.PrefetchScalarGridSpec(
            num_scalar_prefetch=1,
            grid=(steps,),
            in_specs=[whole(normed.shape), gate(width // 2), up(width // 2)]
            + [gate(rows)] * len(far_parts)
            + [up(rows)] * len(far_parts),
            out_specs=[out] * 3,
        ),
        out_shape=[jax.ShapeDtypeStruct((seq_len, units), BF16)] * 3,
        compiler_params=params("arbitrary"),
        cost_estimate=cost(4 * seq_len * width * units, 6 * seq_len * units + 4 * width * units),
        name="activate",
    )(table, normed, own, own, *far_parts, *far_parts)


def activate_back_kernel(tile, width, table, grad_ref, own_ref, *refs):
    (gate_factor_ref, up_factor_ref, d_gate_ref, d_up_ref, far_scr), part_refs = refs[-5:], refs[:-5]

    @pl.when(pl.program_id(0) == 0)
    def _():
        far_scr[...] = ordered(table, part_refs)

    far = far_scr[pl.ds(pl.multiple_of(pl.program_id(0) * tile, tile), tile)]
    d_act = dot(grad_ref[:, :width], own_ref[...], 1, 1) + dot(grad_ref[:, width:], far, 1, 1)
    d_gate_ref[...] = (d_act * gate_factor_ref[...].astype(F32)).astype(BF16)
    d_up_ref[...] = (d_act * up_factor_ref[...].astype(F32)).astype(BF16)


def activate_back(table, grad, own, far_parts, gate_factor, up_factor):
    seq_len, width = grad.shape
    units = own.shape[0]
    tile = tile_of(units)
    out = pl.BlockSpec((seq_len, tile), lambda j, t: (0, j))
    return pl.pallas_call(
        functools.partial(activate_back_kernel, tile, width // 2),
        grid_spec=pltpu.PrefetchScalarGridSpec(
            num_scalar_prefetch=1,
            grid=(units // tile,),
            in_specs=[whole(grad.shape), pl.BlockSpec((tile, width // 2), lambda j, t: (j, 0))]
            + [whole(piece.shape) for piece in far_parts]
            + [out, out],
            out_specs=[out] * 2,
            scratch_shapes=[pltpu.VMEM((units, width // 2), BF16)],
        ),
        out_shape=[jax.ShapeDtypeStruct((seq_len, units), BF16)] * 2,
        compiler_params=params("arbitrary"),
        cost_estimate=cost(2 * seq_len * width * units, 8 * seq_len * units + 2 * width * units),
        name="activate_back",
    )(table, grad, own, *far_parts, gate_factor, up_factor)


def down_kernel(counts, table, *refs):
    halves = len(counts)
    act_refs, own_refs, refs = refs[:halves], refs[halves : 2 * halves], refs[2 * halves :]
    own_out_ref, *other_refs, total_scr = refs[-4:]
    part_refs = []
    for parts in counts:
        part_refs.append(refs[:parts])
        refs = refs[parts:]

    def write(weights, other_ref):
        total_scr[...] = sum(dot(act_ref[...], weight, 1, 0) for act_ref, weight in zip(act_refs, weights))
        rows = own_out_ref.shape[0]
        own_out_ref[...] = total_scr[pl.ds(pl.multiple_of(table[ROW] * rows, rows), rows)]
        other = pl.multiple_of((1 - table[ROW]) * rows, rows)
        other_ref[...] = total_scr[pl.ds(other, rows)].astype(BF16)

    @pl.when(pl.program_id(0) == 0)
    def _():
        write([own_ref[...] for own_ref in own_refs], other_refs[0])

    @pl.when(pl.program_id(0) == 1)
    def _():
        write([ordered(table, parts) for parts in part_refs], other_refs[1])


def down(table, acts, own, far_parts):
    seq_len = acts[0].shape[0]
    features = own[0].shape[1]
    units = sum(part.shape[0] for part in own)
    arrays = (*acts, *own, *[piece for parts in far_parts for piece in parts])
    return pl.pallas_call(
        functools.partial(down_kernel, [len(parts) for parts in far_parts]),
        grid_spec=pltpu.PrefetchScalarGridSpec(
            num_scalar_prefetch=1,
            grid=(2,),
            in_specs=[whole(array.shape) for array in arrays],
            out_specs=[pl.BlockSpec((seq_len // 2, features), lambda j, t: (0, j))]
            + [whole((seq_len // 2, features))] * 2,
            scratch_shapes=[pltpu.VMEM((seq_len, features), F32)],
        ),
        out_shape=[
            jax.ShapeDtypeStruct((seq_len // 2, 2 * features), F32),
            *[jax.ShapeDtypeStruct((seq_len // 2, features), BF16)] * 2,
        ],
        compiler_params=params("arbitrary"),
        cost_estimate=cost(4 * seq_len * units * features, 8 * seq_len * features + 8 * units * (seq_len + features)),
        name="down",
    )(table, *arrays)


def split_product(table, left, rights, tile, groups, count, bits, merge=False):
    seq_len, height = left.shape
    rows = height // (groups * count)
    place = [(0, group) if merge else (group, 0) for group in range(groups)]
    outs, depth = (1, groups * count // 2) if merge else (groups, count // 2)
    firsts = [first for _, first, _ in rights]
    steps = [length for _, _, length in rights]
    rights = [right for right, _, _ in rights]
    columns = sum(steps) * tile
    starts = [sum(steps[:index]) for index in range(len(rights))]

    def kernel(table, left_ref, *refs):
        right_refs, out_refs, total_scr = refs[: len(rights)], refs[len(rights) : -1], refs[-1]
        step = pl.program_id(0)
        for right_ref, start, length in zip(right_refs, starts, steps):

            @pl.when((step >= start) & (step < start + length))
            def _():
                total_scr[...] = dot(left_ref[...], right_ref[...], 0, 0)

        for group, bit in enumerate(bits):
            side = table[BITS + bit]
            sent_ref, kept_ref = out_refs[2 * place[group][0] : 2 * place[group][0] + 2]
            for out_ref, value in ((sent_ref, 1 - side), (kept_ref, side)):
                for index in range(count // 2):
                    begin = (group * count + with_bit(index, bit, value)) * rows
                    if rows % 8 == 0:
                        begin = pl.multiple_of(begin, 8)
                    out_ref[place[group][1] * (count // 2) + index] = total_scr[pl.ds(begin, rows)].astype(BF16)

    def right_spec(first, start, length):
        return pl.BlockSpec((seq_len, tile), lambda i, t: (0, first + jnp.clip(i - start, 0, length - 1)))

    return pl.pallas_call(
        kernel,
        grid_spec=pltpu.PrefetchScalarGridSpec(
            num_scalar_prefetch=1,
            grid=(sum(steps),),
            in_specs=[whole(left.shape)]
            + [right_spec(*place) for place in zip(firsts, starts, steps)],
            out_specs=[pl.BlockSpec((depth, rows, tile), lambda i, t: (0, 0, i))] * (2 * outs),
            scratch_shapes=[pltpu.VMEM((height, tile), F32)],
        ),
        out_shape=[jax.ShapeDtypeStruct((depth, rows, columns), BF16)] * (2 * outs),
        compiler_params=params("arbitrary"),
        cost_estimate=cost(
            2 * seq_len * height * columns, 2 * (seq_len * (height + columns) + height * columns)
        ),
        name="split_product",
    )(table, left, *rights)


def relay_kernel(table, kept_sent_ref, arrived_sent_ref, kept_ref, arrived_ref, sent_out_ref, kept_out_ref):
    sent_out_ref[...] = (kept_sent_ref[...].astype(F32) + arrived_sent_ref[...].astype(F32)).astype(BF16)
    kept_out_ref[...] = (kept_ref[...].astype(F32) + arrived_ref[...].astype(F32)).astype(BF16)


def relay(table, kept, arrived, place, bit):
    count, rows, columns = kept.shape

    def block(sent):
        def index(i, t):
            value = t[BITS + bit]
            return (with_bit(i, place, 1 - value if sent else value), 0, 0)

        return pl.BlockSpec((1, rows, columns), index)

    out = pl.BlockSpec((1, rows, columns), lambda i, t: (i, 0, 0))
    return pl.pallas_call(
        relay_kernel,
        grid_spec=pltpu.PrefetchScalarGridSpec(
            num_scalar_prefetch=1,
            grid=(count // 2,),
            in_specs=[block(True), block(True), block(False), block(False)],
            out_specs=[out, out],
        ),
        out_shape=[jax.ShapeDtypeStruct((count // 2, rows, columns), BF16)] * 2,
        compiler_params=params("arbitrary"),
        cost_estimate=cost(0, 6 * count * rows * columns),
        name="relay",
    )(table, kept, arrived, kept, arrived)


def normed_grad_kernel(halves, steps, tile, counts, table, *refs):
    d_refs, own_refs, refs = refs[: 2 * halves], refs[2 * halves : 3 * halves], refs[3 * halves :]
    part_refs = []
    for parts in counts:
        part_refs.append(refs[:parts])
        refs = refs[parts:]
    own_out_ref, other_refs, far_scrs, total_scr = refs[0], refs[1:3], refs[3:-1], refs[-1]

    @pl.when(pl.program_id(0) == 0)
    def _():
        for half in range(halves):
            far_scrs[half][...] = ordered(table, part_refs[half])

    def write(weights):
        total = None
        for half in range(halves):
            units = d_refs[2 * half].shape[1]
            for kind in range(2):
                term = dot(
                    d_refs[2 * half + kind][...], weights[half][:, kind * units : (kind + 1) * units], 1, 1
                )
                total = term if total is None else total + term
        total_scr[...] = total
        rows = own_out_ref.shape[0]
        own_out_ref[...] = total_scr[pl.ds(pl.multiple_of(table[ROW] * rows, rows), rows)]
        other = pl.multiple_of((1 - table[ROW]) * rows, rows)
        for index, other_ref in enumerate(other_refs):

            @pl.when(pl.program_id(0) // steps == index)
            def _():
                other_ref[...] = total_scr[pl.ds(other, rows)].astype(BF16)

    @pl.when(pl.program_id(0) < steps)
    def _():
        write(own_refs)

    @pl.when(pl.program_id(0) >= steps)
    def _():
        start = pl.multiple_of((pl.program_id(0) - steps) * tile, tile)
        write([scr.at[pl.ds(start, tile)] for scr in far_scrs])


def normed_grad(table, d_parts, own, far_parts):
    seq_len = d_parts[0].shape[0]
    units = [part.shape[1] for part in d_parts[::2]]
    features = own[0].shape[0]
    tile = 256
    steps = features // tile
    halves = len(own)
    parts = [piece for half in far_parts for piece in half]

    def side(index):
        return pl.BlockSpec(
            (seq_len // 2, tile), lambda j, t: (0, jnp.clip(j - steps * index, 0, steps - 1))
        )

    own_specs = [
        pl.BlockSpec((tile, 2 * wide), lambda j, t: (jnp.minimum(j, steps - 1), 0)) for wide in units
    ]
    return pl.pallas_call(
        functools.partial(normed_grad_kernel, halves, steps, tile, [len(half) for half in far_parts]),
        grid_spec=pltpu.PrefetchScalarGridSpec(
            num_scalar_prefetch=1,
            grid=(2 * steps,),
            in_specs=[whole(part.shape) for part in d_parts]
            + own_specs
            + [whole(piece.shape) for piece in parts],
            out_specs=[pl.BlockSpec((seq_len // 2, tile), lambda j, t: (0, j))]
            + [side(index) for index in range(2)],
            scratch_shapes=[pltpu.VMEM((features, 2 * wide), BF16) for wide in units]
            + [pltpu.VMEM((seq_len, tile), F32)],
        ),
        out_shape=[
            jax.ShapeDtypeStruct((seq_len // 2, 2 * features), F32),
            *[jax.ShapeDtypeStruct((seq_len // 2, features), BF16)] * 2,
        ],
        compiler_params=params("arbitrary"),
        cost_estimate=cost(
            8 * seq_len * features * sum(units), 8 * sum(units) * (seq_len + features)
        ),
        name="normed_grad",
    )(table, *d_parts, *own, *parts)


def chip_sum_kernel(own_ref, *refs):
    near_refs, (out_ref, *low_refs) = refs[:-3], refs[-3:]
    width = low_refs[0].shape[1]
    start = 0
    for near_ref in near_refs:
        columns = slice(start, start + near_ref.shape[1])
        total = own_ref[:, columns] + near_ref[...].astype(F32)
        out_ref[:, columns] = total
        start += near_ref.shape[1]
    for index, low_ref in enumerate(low_refs):
        low_ref[...] = out_ref[:, index * width : (index + 1) * width].astype(BF16)


def chip_sum(own, nears):
    rows, width = own.shape
    block = pl.BlockSpec((rows // 4, width), lambda i: (i, 0))
    return pl.pallas_call(
        chip_sum_kernel,
        grid=(4,),
        in_specs=[block] + [pl.BlockSpec((rows // 4, near.shape[1]), lambda i: (i, 0)) for near in nears],
        out_specs=[block] + [pl.BlockSpec((rows // 4, width // 2), lambda i: (i, 0))] * 2,
        out_shape=[jax.ShapeDtypeStruct(own.shape, F32)]
        + [jax.ShapeDtypeStruct((rows, width // 2), BF16)] * 2,
        compiler_params=params("arbitrary"),
        cost_estimate=cost(0, 12 * rows * width),
        name="chip_sum",
    )(own, *nears)


def norm_back_kernel(
    width, table, chip_ref, far_own_ref, far_other_ref, hidden_ref, scale_ref, grad_ref, gain_ref, out_ref, low0_ref, low1_ref, gain_grad_ref
):
    @pl.when(pl.program_id(0) == 0)
    def _():
        gain_grad_ref[...] = jnp.zeros_like(gain_grad_ref)

    d_left = chip_ref[:, :width] + far_other_ref[...].astype(F32)
    d_right = chip_ref[:, width:] + far_own_ref[...].astype(F32)
    left, right = hidden_ref[:, :width], hidden_ref[:, width:]
    scale = scale_ref[:, :1]
    gain_grad_ref[...] += jnp.sum(d_left * left * scale, axis=0, keepdims=True)
    left_weighted, right_weighted = d_left * gain_ref[:, :width], d_right * gain_ref[:, width:]
    inner = jnp.sum(left_weighted * left, axis=1, keepdims=True) + jnp.sum(
        right_weighted * right, axis=1, keepdims=True
    )
    factor = scale * scale * (inner / (2 * width))
    d_left = grad_ref[:, :width].astype(F32) + scale * (left_weighted - left * factor)
    d_right = grad_ref[:, width:].astype(F32) + scale * (right_weighted - right * factor)
    out_ref[...] = d_left
    low0_ref[...] = d_left.astype(BF16)
    low1_ref[...] = d_right.astype(BF16)


def norm_back(table, chip, far, hidden, scale, grad, gain):
    rows, width = chip.shape
    block = rows // 4

    def own(columns):
        return pl.BlockSpec((block, columns), lambda i, t: (i, 0))

    def tokens(columns):
        return pl.BlockSpec((block, columns), lambda i, t: (4 * t[ROW] + i, 0))

    return pl.pallas_call(
        functools.partial(norm_back_kernel, width // 2),
        grid_spec=pltpu.PrefetchScalarGridSpec(
            num_scalar_prefetch=1,
            grid=(4,),
            in_specs=[own(width), own(width // 2), own(width // 2), tokens(width), tokens(128), tokens(width), whole((1, width))],
            out_specs=[own(width // 2)] * 3 + [whole((1, width // 2))],
        ),
        out_shape=[
            jax.ShapeDtypeStruct((rows, width // 2), F32),
            jax.ShapeDtypeStruct((rows, width // 2), BF16),
            jax.ShapeDtypeStruct((rows, width // 2), BF16),
            jax.ShapeDtypeStruct((1, width // 2), F32),
        ],
        compiler_params=params("arbitrary"),
        cost_estimate=cost(0, 20 * rows * width),
        name="norm_back",
    )(table, chip, *far, hidden, scale, grad, gain)


def project_back_kernel(
    count, bit, table, query_ref, key_value_ref, arrived_ref, normed_ref, weight_ref, group_ref,
    d_hidden_ref, d_hidden_near_ref, sent_ref, kept_ref, own_ref, other_ref, bias_ref, d_scr, total_scr, hidden_scr, out_scr,
):
    first = table[COL] == 0
    query_width = query_ref.shape[1]
    own, far = query_ref[...], arrived_ref[:, :query_width]
    d_scr[:, :query_width] = jnp.where(first, own, far)
    d_scr[:, query_width : 2 * query_width] = jnp.where(first, far, own)
    d_key_value = key_value_ref[...] + arrived_ref[:, query_width:].astype(F32)
    d_scr[:, 2 * query_width :] = d_key_value.astype(BF16)
    d_projected = d_scr[...]
    bias_ref[...] = jnp.sum(d_projected.astype(F32), axis=0, keepdims=True)
    total_scr[...] = dot(normed_ref[...], d_projected, 0, 0)
    tokens = own_ref.shape[0]
    hidden_scr[:tokens] = jnp.where(table[ROW] == 0, d_hidden_ref[...], d_hidden_near_ref[...])
    hidden_scr[tokens:] = jnp.where(table[ROW] == 0, d_hidden_near_ref[...], d_hidden_ref[...])
    out_scr[...] = dot(group_ref[...], hidden_scr[...], 0, 0)
    rows = sent_ref.shape[1]
    width = total_scr.shape[1]
    side = table[BITS + bit]
    for out_ref, value in ((sent_ref, 1 - side), (kept_ref, side)):
        for index in range(count // 2):
            start = with_bit(index, bit, value) * rows
            if rows % 8 == 0:
                start = pl.multiple_of(start, 8)
            out_ref[index, :, :width] = total_scr[pl.ds(start, rows)].astype(BF16)
            out_ref[index, :, width:] = out_scr[pl.ds(start, rows)].astype(BF16)
    for out_ref, half in ((own_ref, table[ROW]), (other_ref, 1 - table[ROW])):
        d_half = d_scr[pl.ds(pl.multiple_of(half * tokens, tokens), tokens)]
        out_ref[...] = dot(d_half, weight_ref[...], 1, 1).astype(out_ref.dtype)


def project_back(table, d_query, d_key_value, arrived, normed, weight, group, d_hidden, near, count, bit):
    seq_len = d_query.shape[0]
    width, columns = weight.shape
    rows = width // count
    arrays = (d_query, d_key_value, arrived, normed, weight, group, d_hidden, near)
    terms = (count // 2, rows, columns + d_hidden.shape[1])
    return pl.pallas_call(
        functools.partial(project_back_kernel, count, bit),
        grid_spec=pltpu.PrefetchScalarGridSpec(
            num_scalar_prefetch=1,
            grid=(1,),
            in_specs=[whole(array.shape) for array in arrays],
            out_specs=[
                whole(terms), whole(terms), whole((seq_len // 2, width)), whole((seq_len // 2, width)),
                whole((1, columns)),
            ],
            scratch_shapes=[
                pltpu.VMEM((seq_len, columns), BF16), pltpu.VMEM((width, columns), F32),
                pltpu.VMEM((seq_len, d_hidden.shape[1]), BF16), pltpu.VMEM((width, d_hidden.shape[1]), F32),
            ],
        ),
        out_shape=[
            jax.ShapeDtypeStruct(terms, BF16),
            jax.ShapeDtypeStruct(terms, BF16),
            jax.ShapeDtypeStruct((seq_len // 2, width), F32),
            jax.ShapeDtypeStruct((seq_len // 2, width), BF16),
            jax.ShapeDtypeStruct((1, columns), F32),
        ],
        compiler_params=params("arbitrary"),
        cost_estimate=cost(4 * seq_len * width * columns, 8 * seq_len * columns),
        name="project_back",
    )(table, *arrays)


def swap(part, axis_name):
    return lax.ppermute(part, axis_name, [(0, 1), (1, 0)])


def dp_swap(part, bit):
    count = lax.axis_size("dp")
    return lax.ppermute(part, "dp", [(i, i ^ (1 << bit)) for i in range(count)])


def after(value, *earlier):
    return lax.optimization_barrier((value,) + earlier)[0]


def pick(array, index, axis):
    return lax.dynamic_index_in_dim(array, index, axis, keepdims=False)


def in_order(index, own, other, axis):
    first = jnp.where(index == 0, own, other)
    second = jnp.where(index == 0, other, own)
    return jnp.concatenate([first, second], axis=axis)


def quad_slots(rank):
    low, high = rank % 2, rank // 2 % 2
    return jnp.stack([2 * high + low, 4 + 2 * low + high])


class Line:
    def __init__(self):
        self.last = ()

    def step(self, value):
        return after(value, *self.last) if self.last else value

    def mark(self, *values):
        self.last = values


class Quad:
    def __init__(self, part, rank):
        self.part = part
        self.low, self.high = rank % 2, rank // 2 % 2

    def first_round(self, line):
        if isinstance(self.part, list):
            self.sent = [line.step(slot) for slot in self.part]
        else:
            part = line.step(self.part)
            self.sent = lax.optimization_barrier([part[0], part[1]])
        line.mark(*self.sent)
        self.arriving = dp_swap(self.sent[0], 0), dp_swap(self.sent[1], 1)

    def second_round(self, line):
        arrived = [line.step(value) for value in self.arriving]
        pairs = lax.optimization_barrier(
            (in_order(self.low, self.sent[0], arrived[0], 0), in_order(self.high, self.sent[1], arrived[1], 0))
        )
        line.mark(*pairs)
        self.parts = [*pairs, dp_swap(pairs[0], 1), dp_swap(pairs[1], 0)]
        return self.parts


def laid_out(parts, rank):
    low, high = rank % 2, rank // 2 % 2
    return [in_order(high, parts[0], parts[2], 0), in_order(low, parts[1], parts[3], 0)]


class Scatter:
    def __init__(self, table, sent, kept, order, line):
        self.table, self.kept = table, kept
        bits = lax.axis_size("dp").bit_length() - 1
        self.order = list(order) + [bit for bit in range(bits) if bit not in order]
        self.left = list(range(bits))
        self.pass_on(sent, line)

    def pass_on(self, sent, line):
        bit = self.order.pop(0)
        self.left.remove(bit)
        self.arriving = dp_swap(line.step(sent), bit)

    def relay(self, line):
        bit = self.order[0]
        sent, self.kept = relay(
            self.table, self.kept, line.step(self.arriving), self.left.index(bit), bit
        )
        line.mark(sent)
        self.pass_on(sent, line)

    def finish(self, line):
        while self.order:
            self.relay(line)
        total = self.kept.astype(F32) + line.step(self.arriving).astype(F32)
        total = lax.optimization_barrier(total)
        line.mark(total)
        return total


def shards(
    block_input,
    segment_ids,
    first_gain,
    qkv_weight,
    qkv_bias,
    output_weight,
    second_gain,
    gate_up_weight,
    down_weight,
    output_grad,
):
    count = lax.axis_size("dp")
    rank = lax.axis_index("dp")
    row = lax.axis_index("row")
    col = lax.axis_index("col")
    qkv_block = qkv_weight[0, 0]
    out_block = output_weight[0, 0]
    gate_up_block = gate_up_weight[0, 0]
    down_block = down_weight[0, 0]
    seq_len = segment_ids.shape[0]
    own_rows, half_width = block_input.shape
    model_width = 2 * half_width
    query_width = HEADS // 4 * HEAD_DIM
    own_units = down_block.shape[0] // 2
    segment = own_units // count
    step = max(16, 128 // count)
    padded = pl.cdiv(segment, 3 * step) * 3 * step
    feature_rows = half_width // count
    slot_rows = half_width // 8
    slots = quad_slots(rank)
    bits = count.bit_length() - 1

    def own_tokens(array):
        return lax.dynamic_slice_in_dim(array, row * own_rows, own_rows, 0)

    def slot_pair(array):
        parts = array.reshape((8, array.shape[0] // 8) + array.shape[1:])
        return [pick(parts, slot, 0) for slot in slots]

    def swap_pair(pair):
        return [swap(slot, "col") for slot in pair]

    table = jnp.stack([row, col] + [(rank >> bit) & 1 for bit in range(bits)]).astype(jnp.int32)
    line = Line()
    pair_first, line_first = [0, 1, 2], [1, 0, 2]

    def qkv_columns(side):
        heads = lax.dynamic_slice_in_dim(qkv_block, side * query_width, query_width, 1)
        return jnp.concatenate([heads, qkv_block[:, 2 * query_width :]], axis=1)

    gains = jnp.stack([first_gain, second_gain])
    gains = jnp.concatenate([gains, swap(gains, "col")], axis=1)
    early_send = slot_pair(jnp.concatenate([qkv_columns(1 - col), out_block], axis=1))
    early_send = lax.optimization_barrier(early_send)
    early_quad = Quad(swap_pair(early_send), rank)
    qkv_own = qkv_columns(col)
    qkv_width = qkv_own.shape[1]
    bias = qkv_bias[0]
    bias_own = jnp.concatenate(
        [lax.dynamic_slice_in_dim(bias, col * query_width, query_width, 0), bias[2 * query_width :]]
    )

    (send,) = unit_columns(
        after(gate_up_block, *early_send, gains), 1 - col, slots, count, slot_rows, padded, ((0, 0),)
    )
    line.mark(send)

    near = swap(block_input, "row")
    out_near = swap(out_block, "row")
    far = swap(after(block_input, *early_send), "col")

    position_index = jnp.arange(seq_len, dtype=jnp.int32)
    doc_first = jnp.concatenate([jnp.ones((1,), jnp.bool_), segment_ids[1:] != segment_ids[:-1]])
    positions = position_index - lax.cummax(jnp.where(doc_first, position_index, 0), axis=0)
    frequency = ROPE_BASE ** (-jnp.arange(0, HEAD_DIM, 2, dtype=F32) / HEAD_DIM)
    angles = positions.astype(F32)[:, None] * frequency[None, :]
    cosine, sine = jnp.cos(angles), jnp.sin(angles)
    cosine = jnp.concatenate([cosine, cosine], axis=1)
    sine = jnp.concatenate([-sine, sine], axis=1)
    seg_col, seg_row = segment_ids[:, None], segment_ids[None, :]

    low_slots, high_slots = jnp.arange(4), 4 + jnp.arange(4)
    early_quad.first_round(line)
    gate_up_quad = Quad(swap(line.step(send), "col"), rank)
    outs = ((0, 0), (0, 1), (1, 1))
    gate_up_own = unit_columns(
        line.step(gate_up_block), col, low_slots, count, slot_rows, padded, outs, low_slots, 8
    )
    line.mark(*gate_up_own)
    early_far = early_quad.second_round(line)
    far_halves = lax.optimization_barrier((far[: own_rows // 2], far[own_rows // 2 :]))
    far_near = [swap(half, "row") for half in far_halves]
    gate_up_own = unit_columns(
        line.step(gate_up_block), col, high_slots, count, slot_rows, padded, outs, high_slots, 8, gate_up_own
    )
    line.mark(*gate_up_own)
    *gate_up_own, send = [part.reshape(half_width, -1) for part in gate_up_own]
    out_near = line.step(out_near)
    line.mark(out_near)
    stream, first_normed, first_scale, query, key, value = project(
        table, line.step(block_input), near, far, far_near, gains[:1], qkv_own, early_far,
        bias_own[None], cosine, sine,
    )
    line.mark(query)
    gate_up_quad.first_round(line)
    attended, *attended_parts = attend(line.step(query), key, value, seg_col, seg_row)
    line.mark(attended)
    attended_far = [swap(part, "col") for part in attended_parts]
    attended_near = swap(attended, "row")
    gate_up_far = [gate_up_quad.second_round(line)]
    out_far = lax.optimization_barrier(
        laid_out([line.step(part)[:, qkv_width:] for part in early_far], rank)
    )
    line.mark(*out_far)
    out_far_near = [swap(part, "row") for part in out_far]
    share = count // 8
    send_ranks = (slots[:, None] * share + jnp.arange(share)[None, :]).reshape(-1)
    (down_send,) = unit_rows(line.step(down_block), 1 - col, send_ranks, count, padded, (0,))
    line.mark(down_send)
    down_own = unit_rows(line.step(down_block), col, jnp.arange(count), count, padded)
    line.mark(*down_own)
    down_own = [part.reshape(-1, half_width) for part in down_own]
    attended_far = [line.step(part) for part in attended_far]
    line.mark(*attended_far)
    attended_far_near = [swap(part, "row") for part in attended_far]
    down_quad = Quad(swap(line.step(down_send).reshape(2, -1, half_width), "col"), rank)
    grad_far = swap(line.step(output_grad), "col")
    hidden_one, second_normed, second_scale, attended_group = residual(
        table, line.step(stream), [attended, attended_near, *attended_far, *attended_far_near],
        out_block, out_near, out_far, out_far_near, gains[1:],
    )
    line.mark(second_normed)
    gate_up_far[0] = [line.step(part) for part in gate_up_far[0]]
    line.mark(*gate_up_far[0])
    down_quad.first_round(line)

    act0, gate_factor0, up_factor0 = activate(
        table, line.step(second_normed), gate_up_own[0], gate_up_far[0]
    )
    line.mark(act0)
    grad_far = line.step(grad_far)
    line.mark(grad_far)
    down_far = [down_quad.second_round(line)]
    grad_near = swap(line.step(output_grad), "row")
    grad_far_near = swap(grad_far, "row")
    gate_up_far.append([swap(line.step(send), "col")])
    grad_full = join(table, line.step(output_grad), grad_near, grad_far, grad_far_near)
    line.mark(grad_full)

    def down_terms(act, order):
        sent, kept = split_product(
            table, line.step(act), [(grad_full, 0, 2)], half_width, 1, count, [order[0]]
        )
        line.mark(sent)
        return sent, kept

    def gate_up_terms(d_gate, d_up, order, merge):
        tile = tile_of(d_gate.shape[1])
        rights = [(part, 0, part.shape[1] // tile) for part in (d_gate, d_up)]
        terms = split_product(
            table, line.step(second_normed), rights, tile, 2, count, [order[0]] * 2, merge
        )
        line.mark(terms[0])
        return terms

    terms = down_terms(act0, pair_first)
    down_far[0] = [line.step(part) for part in down_far[0]]
    line.mark(*down_far[0])
    down_sum0 = Scatter(table, *terms, pair_first, line)
    begin, width, full = halves_of(segment, padded)[1]
    down_send = pick(line.step(down_block).reshape(count, 2, segment, half_width), 1 - col, 1)
    down_send = jnp.pad(down_send[:, begin : begin + width], ((0, 0), (0, full - width), (0, 0)))
    down_send = lax.optimization_barrier(down_send.reshape(-1, half_width))
    line.mark(down_send)
    down_far.append([swap(down_send, "col")])
    d_gate0, d_up0 = activate_back(
        table, line.step(grad_full), down_own[0], down_far[0], gate_factor0, up_factor0
    )
    line.mark(d_gate0)
    own_sent0, own_kept0, far_sent0, far_kept0 = gate_up_terms(d_gate0, d_up0, pair_first, False)
    far_sum0 = Scatter(table, far_sent0, far_kept0, pair_first, line)
    act1, gate_factor1, up_factor1 = activate(
        table, line.step(second_normed), gate_up_own[1], gate_up_far[1]
    )
    line.mark(act1)
    down_far[1] = [line.step(down_far[1][0])]
    line.mark(*down_far[1])
    down_sum0.relay(line)
    own_sum0 = Scatter(table, own_sent0, own_kept0, pair_first, line)
    d_gate1, d_up1 = activate_back(
        table, line.step(grad_full), down_own[1], down_far[1], gate_factor1, up_factor1
    )
    line.mark(d_gate1)
    d_second_own, *d_second_other = normed_grad(
        table, [line.step(d_gate0), d_up0, d_gate1, d_up1], gate_up_own, gate_up_far
    )
    line.mark(*d_second_other)
    d_second_near = [swap(part, "row") for part in d_second_other]
    down_terms1 = down_terms(act1, pair_first)
    down_sum0.relay(line)
    far_sum0.relay(line)
    d_second_chip, *d_second_low = chip_sum(line.step(d_second_own), d_second_near)
    line.mark(*d_second_low)
    d_second_far = [swap(part, "col") for part in d_second_low]
    gate_up_terms1 = gate_up_terms(d_gate1, d_up1, pair_first, True)
    mlp_own, mlp_other, mlp_other_far = down(table, [line.step(act0), act1], down_own, down_far)
    line.mark(mlp_other)
    far_sum0.relay(line)
    own_sum0.relay(line)
    down_sum0 = down_sum0.finish(line)[0]
    down_sum1 = Scatter(table, *down_terms1, pair_first, line)
    mlp_near = swap(line.step(mlp_other_far), "row")

    d_hidden, *d_hidden_low, second_gain_part = norm_back(
        table, line.step(d_second_chip), d_second_far, hidden_one, second_scale, grad_full, gains[1:]
    )
    line.mark(*d_hidden_low)
    d_hidden_near = [swap(part, "row") for part in d_hidden_low]
    mlp_sent = mlp_own[:, half_width:] + line.step(mlp_near).astype(F32)
    mlp_sent = lax.optimization_barrier(mlp_sent.astype(BF16))
    line.mark(mlp_sent)

    attend_inputs = [key, value, seg_col, seg_row, [*d_hidden_low, *d_hidden_near], out_block, out_far, cosine, sine]
    d_query, d_key_value = attend_back(table, line.step(query), *attend_inputs, 0, HEADS // 4)
    d_projected_sent = jnp.concatenate([d_query, d_key_value.astype(BF16)], axis=1)
    d_projected_sent = lax.optimization_barrier(d_projected_sent)
    line.mark(d_projected_sent)
    arrived = swap(d_projected_sent, "col")
    down_sum1.relay(line)
    gate_up_sum1 = Scatter(table, *gate_up_terms1, pair_first, line)
    sent, kept, d_first_own, d_first_other, bias_part = project_back(
        table, line.step(d_query), d_key_value, arrived, first_normed, qkv_block, attended_group,
        d_hidden_low[0], d_hidden_near[0], count, 0,
    )
    line.mark(sent)
    heads_sum = Scatter(table, sent, kept, pair_first, line)
    d_first_near = swap(d_first_other, "row")
    own_sum0.relay(line)
    down_sum1.relay(line)
    far_sum0 = far_sum0.finish(line)[0]
    gate_up_sum1.relay(line)

    d_first = line.step(d_first_own) + d_first_near.astype(F32)
    stream_own = block_input.astype(F32)
    first_scale_own = own_tokens(first_scale)[:, :1]
    first_gain_part = jnp.sum(d_first * stream_own * first_scale_own, axis=0)
    weighted = d_first * first_gain
    inner = jnp.sum(weighted * stream_own, axis=1)
    inner = (inner + swap(inner, "col"))[:, None]
    input_grad = d_hidden + first_scale_own * (
        weighted - stream_own * (first_scale_own * first_scale_own) * (inner / model_width)
    )

    gain_parts = line.step(jnp.concatenate([first_gain_part, second_gain_part[0]]))
    gain_parts = lax.optimization_barrier(gain_parts + swap(gain_parts, "row"))
    line.mark(gain_parts)
    small = line.step(jnp.concatenate([gain_parts, bias_part[0]]))

    def dp_step(part, bit):
        part = lax.optimization_barrier(part + line.step(dp_swap(part, bit)))
        line.mark(part)
        return part

    heads_sum.relay(line)
    far_sum0 = swap(line.step(far_sum0.astype(BF16)), "col")
    down_sum0_far = swap(line.step(down_sum0[:, half_width:].astype(BF16)), "col")
    own_sum0 = own_sum0.finish(line)[0]
    down_sum1 = down_sum1.finish(line)[0]
    mlp_far = swap(line.step(mlp_sent), "col")
    down_sum1_far = swap(line.step(down_sum1[:, half_width:].astype(BF16)), "col")
    gate_up_sum1.relay(line)
    small = dp_step(small, 0)
    heads_sum.relay(line)
    hidden_own = own_tokens(hidden_one)[:, :half_width]
    mlp_near = swap(line.step(mlp_other), "row")
    mlp_chip = mlp_own[:, :half_width] + mlp_near.astype(F32)
    block_output = (hidden_own + (mlp_chip + line.step(mlp_far).astype(F32))).astype(BF16)
    small = dp_step(small, 1)
    own_sum1, far_sum1 = gate_up_sum1.finish(line)
    far_sum1 = swap(line.step(far_sum1.astype(BF16)), "col")
    for bit in range(2, bits):
        small = dp_step(small, bit)
    heads_sum = heads_sum.finish(line)[0]
    qkv_sum, out_sum = heads_sum[:, : bias.shape[0]], heads_sum[:, bias.shape[0] :]
    bias_width = bias.shape[0] // count
    bias_grad = lax.dynamic_slice_in_dim(small[model_width:], rank * bias_width, bias_width, 0)

    widths = [width for _, width, _ in halves_of(segment, padded)]
    own_rows_sum = [
        part[:width, :half_width] for part, width in zip((down_sum0, down_sum1), widths)
    ]
    far_rows_sum = [
        part[:width].astype(F32) for part, width in zip((down_sum0_far, down_sum1_far), widths)
    ]
    down_grad = in_order(
        col, jnp.concatenate(own_rows_sum, axis=0), jnp.concatenate(far_rows_sum, axis=0), 0
    )
    gate_up_grad = spread_columns(
        table, (own_sum0, own_sum1), (far_sum0, far_sum1), count, segment, padded
    )

    return (
        block_output,
        input_grad,
        small[:half_width],
        qkv_sum[None, None],
        bias_grad[None],
        out_sum[None, None],
        small[half_width:model_width],
        gate_up_grad[None, None],
        down_grad[None, None],
    )


def solution(mesh):
    placed = (
        P(("dp", "row"), "col"),
        P("dp"),
        P("col"),
        P("col", "row", None, None),
        P("row", None),
        P("row", "col", None, None),
        P("col"),
        P("col", "row", None, None),
        P("row", "col", None, None),
        P(("dp", "row"), "col"),
    )
    return jax.shard_map(
        shards,
        mesh=mesh,
        in_specs=placed,
        out_specs=(
            P(("dp", "row"), "col"),
            P(("dp", "row"), "col"),
            P("col"),
            P("col", "row", "dp", None),
            P("row", "dp"),
            P("row", "col", "dp", None),
            P("col"),
            P("col", "row", "dp", None),
            P("row", "col", "dp", None),
        ),
        check_vma=False,
    )
```

```python
import functools
import jax
import jax.numpy as jnp
from jax import lax
from jax.experimental import pallas as pl
from jax.experimental.pallas import tpu as pltpu
from jax.sharding import PartitionSpec as P

HEADS = 12
KV_HEADS = 2
HEAD_DIM = 128
EPSILON = 1e-06
ROPE_BASE = 1000000.0
MASKED = -1e30
F32 = jnp.float32
BF16 = jnp.bfloat16
VMEM_LIMIT = 60 * 1024 * 1024


def dot(left, right, left_dim, right_dim):
    return lax.dot_general(
        left, right, (((left_dim,), (right_dim,)), ((), ())), preferred_element_type=F32
    )


def params(*semantics):
    return pltpu.CompilerParams(
        dimension_semantics=semantics or None, vmem_limit_bytes=VMEM_LIMIT
    )


def cost(flops, moved):
    return pl.CostEstimate(flops=1, bytes_accessed=1, transcendentals=0)


def whole(shape):
    return pl.BlockSpec(shape, lambda *_: (0,) * len(shape))


ROW, COL, LOW, HIGH = range(4)
BITS = 2


def with_bit(index, place, value):
    return ((index >> place) << (place + 1)) | (value << place) | (index & ((1 << place) - 1))


def ordered(table, parts, columns=slice(None)):
    if len(parts) == 1:
        return parts[0][:, columns]
    first, second, first_other, second_other = [part[:, columns] for part in parts]
    high, low = table[HIGH] == 0, table[LOW] == 0
    return jnp.concatenate(
        [
            jnp.where(high, first, first_other),
            jnp.where(high, first_other, first),
            jnp.where(low, second, second_other),
            jnp.where(low, second_other, second),
        ],
        axis=0,
    )


def halves_of(segment, padded):
    first = 2 * padded // 3
    return ((0, first, first), (first, segment - first, padded - first))


def units_kernel(count, segment, padded, outs, table, block_ref, *refs):
    rows = block_ref.shape[0]
    out_refs = refs[-len(outs) :]

    def write(side):
        for out_ref, (other, half) in zip(out_refs, outs):
            begin, width, full = halves_of(segment, padded)[half]
            parts = []
            for kind in range(2):
                for k in range(count):
                    start = ((kind * count + k) * 2 + (side ^ other)) * segment + begin
                    parts.append(block_ref[:, start : start + width])
                    if width < full:
                        parts.append(jnp.zeros((rows, full - width), block_ref.dtype))
            out_ref[0] = jnp.concatenate(parts, axis=1)

    @pl.when(table[0] == 0)
    def _():
        write(0)

    @pl.when(table[0] != 0)
    def _():
        write(1)


def unit_columns(block, side, slots, count, rows, padded, outs, places=None, depth=None, begun=None):
    columns = block.shape[1]
    segment = columns // (4 * count)
    units = [2 * count * halves_of(segment, padded)[half][2] for _, half in outs]
    steps = slots.shape[0]
    depth = steps if depth is None else depth
    places = jnp.arange(steps) if places is None else places
    begun = [] if begun is None else begun
    table = jnp.concatenate([side.reshape(1), slots, places]).astype(jnp.int32)
    return pl.pallas_call(
        functools.partial(units_kernel, count, segment, padded, outs),
        grid_spec=pltpu.PrefetchScalarGridSpec(
            num_scalar_prefetch=1,
            grid=(steps,),
            in_specs=[pl.BlockSpec((rows, columns), lambda i, t: (t[1 + i], 0))]
            + [pl.BlockSpec(memory_space=pl.ANY)] * len(begun),
            out_specs=[pl.BlockSpec((1, rows, wide), lambda i, t: (t[1 + steps + i], 0, 0)) for wide in units],
        ),
        out_shape=[jax.ShapeDtypeStruct((depth, rows, wide), block.dtype) for wide in units],
        input_output_aliases={2 + index: index for index in range(len(begun))},
        compiler_params=params("arbitrary"),
        cost_estimate=cost(0, 4 * steps * rows * sum(units)),
        name="unit_columns",
    )(table, block, *begun)


def unit_rows_kernel(parts, table, block_ref, *out_refs):
    for out_ref, (begin, width, full) in zip(out_refs, parts):
        if width == full and begin % 16 == 0 and full % 16 == 0:
            out_ref[0] = block_ref[0, 0, begin : begin + width]
        else:
            part = block_ref[0, 0].astype(F32)[begin : begin + width]
            part = jnp.concatenate([part, jnp.zeros((full - width, part.shape[1]), F32)], axis=0)
            out_ref[0] = part.astype(out_ref.dtype)


def unit_rows(block, side, ranks, count, padded, halves=(0, 1)):
    rows, width = block.shape
    segment = rows // (2 * count)
    parts = [halves_of(segment, padded)[half] for half in halves]
    steps = ranks.shape[0]
    table = jnp.concatenate([side.reshape(1), ranks]).astype(jnp.int32)
    return pl.pallas_call(
        functools.partial(unit_rows_kernel, parts),
        grid_spec=pltpu.PrefetchScalarGridSpec(
            num_scalar_prefetch=1,
            grid=(steps,),
            in_specs=[pl.BlockSpec((1, 1, segment, width), lambda i, t: (t[1 + i], t[0], 0, 0))],
            out_specs=[pl.BlockSpec((1, full, width), lambda i, t: (i, 0, 0)) for _, _, full in parts],
        ),
        out_shape=[jax.ShapeDtypeStruct((steps, full, width), block.dtype) for _, _, full in parts],
        compiler_params=params("arbitrary"),
        cost_estimate=cost(0, 4 * steps * segment * width),
        name="unit_rows",
    )(table, block.reshape(count, 2, segment, width))


def spread_kernel(count, segment, padded, table, own0_ref, own1_ref, far0_ref, far1_ref, out_ref):
    def write(sides):
        pieces = []
        for kind in range(2):
            for k in range(count):
                for side in sides:
                    for ref, (_, width, full) in zip(side, halves_of(segment, padded)):
                        start = (kind * count + k) * full
                        pieces.append(ref[:, start : start + width].astype(F32))
        out_ref[...] = jnp.concatenate(pieces, axis=1)

    own, far = (own0_ref, own1_ref), (far0_ref, far1_ref)

    @pl.when(table[COL] == 0)
    def _():
        write((own, far))

    @pl.when(table[COL] != 0)
    def _():
        write((far, own))


def spread_columns(table, own, far, count, segment, padded):
    rows = own[0].shape[0]
    step = rows // 3 if rows % 24 == 0 else rows
    parts = [pl.BlockSpec((step, part.shape[1]), lambda i, t: (i, 0)) for part in (*own, *far)]
    columns = 4 * count * segment
    return pl.pallas_call(
        functools.partial(spread_kernel, count, segment, padded),
        grid_spec=pltpu.PrefetchScalarGridSpec(
            num_scalar_prefetch=1,
            grid=(rows // step,),
            in_specs=parts,
            out_specs=pl.BlockSpec((step, columns), lambda i, t: (i, 0)),
        ),
        out_shape=jax.ShapeDtypeStruct((rows, columns), F32),
        compiler_params=params("arbitrary"),
        cost_estimate=cost(0, 7 * rows * columns),
        name="spread_columns",
    )(table, *own, *far)


def project_kernel(
    width, table, own_ref, near_ref, far_ref, far_near0_ref, far_near1_ref, gain_ref, weight_ref,
    part0_ref, part1_ref, part2_ref, part3_ref, bias_ref, cosine_ref, sine_ref, stream_ref, normed_ref, scale_ref, query_ref, key_ref, value_ref,
):
    half = pl.program_id(0) * 2 // pl.num_programs(0)
    mine = half == table[ROW]
    left = jnp.where(mine, own_ref[...], near_ref[...]).astype(F32)
    even = pl.program_id(0) % 2 == 0
    right = jnp.where(
        mine,
        far_ref[...],
        jnp.where(even, far_near0_ref[...], far_near1_ref[...]),
    ).astype(F32)
    squares = jnp.sum(left * left, axis=1, keepdims=True) + jnp.sum(
        right * right, axis=1, keepdims=True
    )
    scale = lax.rsqrt(squares / (2 * width) + EPSILON)
    left_normed = (left * scale * gain_ref[:, :width]).astype(BF16)
    right_normed = (right * scale * gain_ref[:, width:]).astype(BF16)
    stream_ref[:, :width] = left.astype(BF16)
    stream_ref[:, width:] = right.astype(BF16)
    normed_ref[...] = left_normed
    scale_ref[...] = jnp.broadcast_to(scale, scale_ref.shape)
    far_weight = ordered(table, (part0_ref, part1_ref, part2_ref, part3_ref))
    projected = (
        dot(left_normed, weight_ref[...], 1, 0) + dot(right_normed, far_weight, 1, 0) + bias_ref[...]
    )
    cosine, sine = cosine_ref[...], sine_ref[...]

    def rotated(values):
        return (values * cosine + pltpu.roll(values, HEAD_DIM // 2, 1) * sine).astype(BF16)

    query_width = query_ref.shape[1]
    for start in range(0, query_width, HEAD_DIM):
        query_ref[:, start : start + HEAD_DIM] = rotated(projected[:, start : start + HEAD_DIM])
    key_ref[...] = rotated(projected[:, query_width : query_width + HEAD_DIM])
    value_ref[...] = projected[:, query_width + HEAD_DIM :].astype(BF16)


def project(table, own, near, far, far_near, gain, weight, far_parts, bias, cosine, sine):
    rows, width = own.shape
    seq_len = 2 * rows
    block = rows // 2
    per_half = 2
    out_width = weight.shape[1]
    query_width = out_width - 2 * HEAD_DIM
    part = pl.BlockSpec((block, width), lambda i, t: (i % per_half, 0))

    def tokens(columns):
        return pl.BlockSpec((block, columns), lambda i, t: (i, 0))

    return pl.pallas_call(
        functools.partial(project_kernel, width),
        grid_spec=pltpu.PrefetchScalarGridSpec(
            num_scalar_prefetch=1,
            grid=(seq_len // block,),
            in_specs=[part, part, part]
            + [whole((block, width))] * 2
            + [whole((1, 2 * width)), whole(weight.shape)]
            + [whole((piece.shape[0], out_width)) for piece in far_parts]
            + [whole((1, out_width)), tokens(HEAD_DIM), tokens(HEAD_DIM)],
            out_specs=[
                tokens(2 * width), tokens(width), tokens(128),
                tokens(query_width), tokens(HEAD_DIM), tokens(HEAD_DIM),
            ],
        ),
        out_shape=[
            jax.ShapeDtypeStruct((seq_len, 2 * width), BF16),
            jax.ShapeDtypeStruct((seq_len, width), BF16),
            jax.ShapeDtypeStruct((seq_len, 128), F32),
            jax.ShapeDtypeStruct((seq_len, query_width), BF16),
            jax.ShapeDtypeStruct((seq_len, HEAD_DIM), BF16),
            jax.ShapeDtypeStruct((seq_len, HEAD_DIM), BF16),
        ],
        compiler_params=params("arbitrary"),
        cost_estimate=cost(4 * seq_len * width * out_width, 12 * seq_len * width),
        name="project",
    )(table, own, near, far, *far_near, gain, weight, *far_parts, bias, cosine, sine)


def join_kernel(width, table, own_ref, near_ref, far_ref, far_near_ref, out_ref):
    mine = pl.program_id(0) * 2 // pl.num_programs(0) == table[ROW]
    out_ref[:, :width] = jnp.where(mine, own_ref[...], near_ref[...])
    out_ref[:, width:] = jnp.where(mine, far_ref[...], far_near_ref[...])


def join(table, own, near, far, far_near):
    rows, width = own.shape
    block = min(256, rows)
    per_half = rows // block
    part = pl.BlockSpec((block, width), lambda i, t: (i % per_half, 0))
    return pl.pallas_call(
        functools.partial(join_kernel, width),
        grid_spec=pltpu.PrefetchScalarGridSpec(
            num_scalar_prefetch=1,
            grid=(2 * rows // block,),
            in_specs=[part] * 4,
            out_specs=pl.BlockSpec((block, 2 * width), lambda i, t: (i, 0)),
        ),
        out_shape=jax.ShapeDtypeStruct((2 * rows, 2 * width), own.dtype),
        compiler_params=params("arbitrary"),
        cost_estimate=cost(0, 16 * rows * width),
        name="join",
    )(table, own, near, far, far_near)


def block_probs(query, key, seg_col, seg_row, start, stop):
    scores = dot(query, key, 1, 1) * HEAD_DIM ** (-0.5)
    rows = stop - start
    query_index = start + lax.broadcasted_iota(jnp.int32, (rows, stop), 0)
    key_index = lax.broadcasted_iota(jnp.int32, (rows, stop), 1)
    allowed = (key_index <= query_index) & (seg_col == seg_row)
    scores = jnp.where(allowed, scores, MASKED)
    exponent = jnp.exp(scores - jnp.max(scores, axis=1, keepdims=True))
    return exponent / jnp.sum(exponent, axis=1, keepdims=True)


def attend_kernel(block, query_ref, key_ref, value_ref, seg_col_ref, seg_row_ref, all_ref, out_ref, last_ref):
    last = pl.program_id(0) == pl.num_programs(0) - 1
    for start in range(0, query_ref.shape[0], block):
        stop = start + block
        probs = block_probs(
            query_ref[start:stop], key_ref[:stop], seg_col_ref[start:stop], seg_row_ref[:, :stop], start, stop
        )
        out = dot(probs.astype(BF16), value_ref[:stop], 1, 0).astype(BF16)
        all_ref[start:stop] = out

        @pl.when(last)
        def _():
            last_ref[start:stop] = out

        @pl.when(jnp.logical_not(last))
        def _():
            out_ref[start:stop] = out


def attend(query, key, value, seg_col, seg_row):
    seq_len, width = query.shape
    heads = width // HEAD_DIM
    head = pl.BlockSpec((seq_len, HEAD_DIM), lambda h: (0, h))
    shared = whole((seq_len, HEAD_DIM))
    return pl.pallas_call(
        functools.partial(attend_kernel, 256),
        grid=(width // HEAD_DIM,),
        in_specs=[head, shared, shared, whole((seq_len, 1)), whole((1, seq_len))],
        out_specs=[head, pl.BlockSpec((seq_len, HEAD_DIM), lambda h: (0, jnp.minimum(h, heads - 2))), shared],
        out_shape=[
            jax.ShapeDtypeStruct((seq_len, width), BF16),
            jax.ShapeDtypeStruct((seq_len, width - HEAD_DIM), BF16),
            jax.ShapeDtypeStruct((seq_len, HEAD_DIM), BF16),
        ],
        compiler_params=params("arbitrary"),
        cost_estimate=cost(12 * seq_len * seq_len * width, 8 * seq_len * width),
        name="attend",
    )(query, key, value, seg_col, seg_row)


def attend_back_kernel(
    block, table, query_ref, key_ref, value_ref, seg_col_ref, seg_row_ref, own_ref, far_ref, near_ref, far_near_ref,
    weight_ref, far_top_ref, far_bottom_ref, cosine_ref, sine_ref, *refs
):
    sent_ref, key_value_ref = refs
    head = pl.ds(pl.multiple_of(pl.program_id(0) * HEAD_DIM, HEAD_DIM), HEAD_DIM)
    width = sent_ref.shape[1] - 2 * HEAD_DIM
    scaling = HEAD_DIM ** (-0.5)
    own_rows = own_ref.shape[0]
    far_weight = jnp.where(table[COL] == 0, far_top_ref[...], far_bottom_ref[...])

    @pl.when(pl.program_id(0) == 0)
    def _():
        key_value_ref[...] = jnp.zeros_like(key_value_ref)

    for start in range(0, query_ref.shape[0], block):
        stop = start + block
        mine = table[ROW] == start // own_rows
        place = slice(start % own_rows, start % own_rows + block)
        grad = (
            dot(jnp.where(mine, own_ref[place], near_ref[place]), weight_ref[...], 1, 1)
            + dot(jnp.where(mine, far_ref[place], far_near_ref[place]), far_weight, 1, 1)
        ).astype(BF16)
        query = query_ref[start:stop]
        key, value = key_ref[:stop], value_ref[:stop]
        probs = block_probs(
            query, key, seg_col_ref[start:stop], seg_row_ref[:, :stop], start, stop
        )
        d_probs = dot(grad, value, 1, 1)
        d_scores = probs * (d_probs - jnp.sum(d_probs * probs, axis=1, keepdims=True))
        d_scores = d_scores.astype(BF16)
        d_query = dot(d_scores, key, 1, 0) * scaling
        turned = pltpu.roll(d_query * sine_ref[start:stop], HEAD_DIM // 2, 1)
        sent_ref[start:stop, head] = (d_query * cosine_ref[start:stop] + turned).astype(BF16)
        key_value_ref[:stop, :HEAD_DIM] += dot(d_scores, query, 0, 0) * scaling
        key_value_ref[:stop, HEAD_DIM:] += dot(probs.astype(BF16), grad, 0, 0)

    @pl.when(pl.program_id(0) == pl.num_programs(0) - 1)
    def _():
        d_key = key_value_ref[:, :HEAD_DIM]
        turned = pltpu.roll(d_key * sine_ref[...], HEAD_DIM // 2, 1)
        key_value_ref[:, :HEAD_DIM] = d_key * cosine_ref[...] + turned
        sent_ref[:, width:] = key_value_ref[...].astype(BF16)


def attend_back(table, query, key, value, seg_col, seg_row, d_hidden, weight, far_weights, cosine, sine):
    seq_len, width = query.shape
    features = weight.shape[1]
    heads = width // HEAD_DIM
    head = pl.BlockSpec((seq_len, HEAD_DIM), lambda h, t: (0, h))
    rows = pl.BlockSpec((HEAD_DIM, features), lambda h, t: (heads * t[COL] + h, 0))
    far_rows = pl.BlockSpec((HEAD_DIM, features), lambda h, t: (h, 0))
    shared = whole((seq_len, HEAD_DIM))
    key_value = whole((seq_len, 2 * HEAD_DIM))
    return pl.pallas_call(
        functools.partial(attend_back_kernel, 256),
        grid_spec=pltpu.PrefetchScalarGridSpec(
            num_scalar_prefetch=1,
            grid=(heads,),
            in_specs=[
                head, shared, shared, whole((seq_len, 1)), whole((1, seq_len)),
                *[whole(part.shape) for part in d_hidden], rows, far_rows, far_rows, shared, shared,
            ],
            out_specs=[whole((seq_len, width + 2 * HEAD_DIM)), key_value],
        ),
        out_shape=[
            jax.ShapeDtypeStruct((seq_len, width + 2 * HEAD_DIM), BF16),
            jax.ShapeDtypeStruct((seq_len, 2 * HEAD_DIM), F32),
        ],
        compiler_params=params("arbitrary"),
        cost_estimate=cost(24 * seq_len * seq_len * width, 12 * seq_len * width),
        name="attend_back",
    )(table, query, key, value, seg_col, seg_row, *d_hidden, weight, *far_weights, cosine, sine)


def residual_kernel(table, stream_ref, *refs):
    pieces, weights, (gain_ref, hidden_ref, normed_ref, scale_ref, group_ref) = refs[:6], refs[6:12], refs[12:]
    first = table[COL] == 0
    own, near = pieces[0][...], pieces[1][...]
    far, near_far = (
        jnp.concatenate([pieces[index][...], pieces[index + 1][...]], axis=1) for index in (2, 4)
    )
    part = own.shape[1]
    group = [jnp.where(first, own, far), jnp.where(first, far, own)]
    other = [jnp.where(first, near, near_far), jnp.where(first, near_far, near)]
    group_ref[:, :part] = group[0]
    group_ref[:, part:] = group[1]
    own_w, near_w, *far_w = weights
    width = own_w.shape[1]
    halves = []
    for index in range(2):
        total = stream_ref[:, index * width : (index + 1) * width].astype(F32)
        for place in range(2):
            rows = slice(place * part, (place + 1) * part)
            mine, theirs = (own_w[rows], near_w[rows]) if index == 0 else (far_w[place][...], far_w[2 + place][...])
            total = total + dot(group[place], mine, 1, 0)
            total = total + dot(other[place], theirs, 1, 0)
        halves.append(total)
    squares = sum(jnp.sum(total * total, axis=1, keepdims=True) for total in halves)
    scale = lax.rsqrt(squares / (2 * width) + EPSILON)
    scale_ref[...] = jnp.broadcast_to(scale, scale_ref.shape)
    for index, total in enumerate(halves):
        columns = slice(index * width, (index + 1) * width)
        hidden_ref[:, columns] = total
        normed_ref[:, columns] = (total * scale * gain_ref[:, columns]).astype(BF16)


def residual(table, stream, attended, own_weight, near_weight, far_weights, near_far_weights, gain):
    seq_len, width = stream.shape
    pieces = attended
    part = attended[0].shape[1]
    weights = [own_weight, near_weight, *far_weights, *near_far_weights]
    block = min(256, seq_len)

    def tokens(columns):
        return pl.BlockSpec((block, columns), lambda i, t: (i, 0))

    return pl.pallas_call(
        residual_kernel,
        grid_spec=pltpu.PrefetchScalarGridSpec(
            num_scalar_prefetch=1,
            grid=(seq_len // block,),
            in_specs=[tokens(width)]
            + [tokens(piece.shape[1]) for piece in pieces]
            + [whole(weight.shape) for weight in weights]
            + [whole((1, width))],
            out_specs=[tokens(width), tokens(width), tokens(128), tokens(2 * part)],
        ),
        out_shape=[
            jax.ShapeDtypeStruct((seq_len, width), F32),
            jax.ShapeDtypeStruct((seq_len, width), BF16),
            jax.ShapeDtypeStruct((seq_len, 128), F32),
            jax.ShapeDtypeStruct((seq_len, 2 * part), BF16),
        ],
        compiler_params=params("arbitrary"),
        cost_estimate=cost(2 * seq_len * width * width, 14 * seq_len * width),
        name="residual",
    )(table, stream, *pieces, *weights, gain)


def activate_kernel(width, table, normed_ref, own_gate_ref, own_up_ref, *refs):
    (act_ref, gate_factor_ref, up_factor_ref), refs = refs[-3:], refs[:-3]
    gate_parts, up_parts = refs[: len(refs) // 2], refs[len(refs) // 2 :]
    left, right = normed_ref[:, :width], normed_ref[:, width:]
    gate = dot(left, own_gate_ref[...], 1, 0) + dot(right, ordered(table, gate_parts), 1, 0)
    up = dot(left, own_up_ref[...], 1, 0) + dot(right, ordered(table, up_parts), 1, 0)
    sigmoid = jax.nn.sigmoid(gate)
    silu = gate * sigmoid
    act_ref[...] = (silu * up).astype(BF16)
    gate_factor_ref[...] = (up * (sigmoid * (1.0 + gate * (1.0 - sigmoid)))).astype(BF16)
    up_factor_ref[...] = silu.astype(BF16)


def tile_of(units, most=384):
    return next(t for t in (768, 512, 384, 256, 128, units) if units % t == 0 and (t <= most or t == units))


def activate(table, normed, own, far_parts):
    seq_len, width = normed.shape
    units = own.shape[1] // 2
    tile = tile_of(units)
    steps = units // tile

    def gate(rows):
        return pl.BlockSpec((rows, tile), lambda j, t: (0, j))

    def up(rows):
        return pl.BlockSpec((rows, tile), lambda j, t: (0, steps + j))

    rows = far_parts[0].shape[0]
    out = pl.BlockSpec((seq_len, tile), lambda j, t: (0, j))
    return pl.pallas_call(
        functools.partial(activate_kernel, width // 2),
        grid_spec=pltpu.PrefetchScalarGridSpec(
            num_scalar_prefetch=1,
            grid=(steps,),
            in_specs=[whole(normed.shape), gate(width // 2), up(width // 2)]
            + [gate(rows)] * len(far_parts)
            + [up(rows)] * len(far_parts),
            out_specs=[out] * 3,
        ),
        out_shape=[jax.ShapeDtypeStruct((seq_len, units), BF16)] * 3,
        compiler_params=params("arbitrary"),
        cost_estimate=cost(4 * seq_len * width * units, 6 * seq_len * units + 4 * width * units),
        name="activate",
    )(table, normed, own, own, *far_parts, *far_parts)


def activate_back_kernel(tile, width, table, grad_ref, own_ref, *refs):
    (gate_factor_ref, up_factor_ref, d_gate_ref, d_up_ref, far_scr), part_refs = refs[-5:], refs[:-5]

    @pl.when(pl.program_id(0) == 0)
    def _():
        far_scr[...] = ordered(table, part_refs)

    far = far_scr[pl.ds(pl.multiple_of(pl.program_id(0) * tile, tile), tile)]
    d_act = dot(grad_ref[:, :width], own_ref[...], 1, 1) + dot(grad_ref[:, width:], far, 1, 1)
    d_gate_ref[...] = (d_act * gate_factor_ref[...].astype(F32)).astype(BF16)
    d_up_ref[...] = (d_act * up_factor_ref[...].astype(F32)).astype(BF16)


def activate_back(table, grad, own, far_parts, gate_factor, up_factor):
    seq_len, width = grad.shape
    units = own.shape[0]
    tile = tile_of(units)
    out = pl.BlockSpec((seq_len, tile), lambda j, t: (0, j))
    return pl.pallas_call(
        functools.partial(activate_back_kernel, tile, width // 2),
        grid_spec=pltpu.PrefetchScalarGridSpec(
            num_scalar_prefetch=1,
            grid=(units // tile,),
            in_specs=[whole(grad.shape), pl.BlockSpec((tile, width // 2), lambda j, t: (j, 0))]
            + [whole(piece.shape) for piece in far_parts]
            + [out, out],
            out_specs=[out] * 2,
            scratch_shapes=[pltpu.VMEM((units, width // 2), BF16)],
        ),
        out_shape=[jax.ShapeDtypeStruct((seq_len, units), BF16)] * 2,
        compiler_params=params("arbitrary"),
        cost_estimate=cost(2 * seq_len * width * units, 8 * seq_len * units + 2 * width * units),
        name="activate_back",
    )(table, grad, own, *far_parts, gate_factor, up_factor)


def down_kernel(counts, table, *refs):
    halves = len(counts)
    act_refs, own_refs, refs = refs[:halves], refs[halves : 2 * halves], refs[2 * halves :]
    own_out_ref, *other_refs, total_scr = refs[-4:]
    part_refs = []
    for parts in counts:
        part_refs.append(refs[:parts])
        refs = refs[parts:]

    def write(weights, other_ref):
        total_scr[...] = sum(dot(act_ref[...], weight, 1, 0) for act_ref, weight in zip(act_refs, weights))
        rows = own_out_ref.shape[0]
        own_out_ref[...] = total_scr[pl.ds(pl.multiple_of(table[ROW] * rows, rows), rows)]
        other = pl.multiple_of((1 - table[ROW]) * rows, rows)
        other_ref[...] = total_scr[pl.ds(other, rows)].astype(BF16)

    @pl.when(pl.program_id(0) == 0)
    def _():
        write([own_ref[...] for own_ref in own_refs], other_refs[0])

    @pl.when(pl.program_id(0) == 1)
    def _():
        write([ordered(table, parts) for parts in part_refs], other_refs[1])


def down(table, acts, own, far_parts):
    seq_len = acts[0].shape[0]
    features = own[0].shape[1]
    units = sum(part.shape[0] for part in own)
    arrays = (*acts, *own, *[piece for parts in far_parts for piece in parts])
    return pl.pallas_call(
        functools.partial(down_kernel, [len(parts) for parts in far_parts]),
        grid_spec=pltpu.PrefetchScalarGridSpec(
            num_scalar_prefetch=1,
            grid=(2,),
            in_specs=[whole(array.shape) for array in arrays],
            out_specs=[pl.BlockSpec((seq_len // 2, features), lambda j, t: (0, j))]
            + [whole((seq_len // 2, features))] * 2,
            scratch_shapes=[pltpu.VMEM((seq_len, features), F32)],
        ),
        out_shape=[
            jax.ShapeDtypeStruct((seq_len // 2, 2 * features), F32),
            *[jax.ShapeDtypeStruct((seq_len // 2, features), BF16)] * 2,
        ],
        compiler_params=params("arbitrary"),
        cost_estimate=cost(4 * seq_len * units * features, 8 * seq_len * features + 8 * units * (seq_len + features)),
        name="down",
    )(table, *arrays)


def split_product(table, left, rights, tile, groups, count, bits, merge=False):
    seq_len, height = left.shape
    rows = height // (groups * count)
    place = [(0, group) if merge else (group, 0) for group in range(groups)]
    outs, depth = (1, groups * count // 2) if merge else (groups, count // 2)
    firsts = [first for _, first, _ in rights]
    steps = [length for _, _, length in rights]
    rights = [right for right, _, _ in rights]
    columns = sum(steps) * tile
    starts = [sum(steps[:index]) for index in range(len(rights))]

    def kernel(table, left_ref, *refs):
        right_refs, out_refs, total_scr = refs[: len(rights)], refs[len(rights) : -1], refs[-1]
        step = pl.program_id(0)
        for right_ref, start, length in zip(right_refs, starts, steps):

            @pl.when((step >= start) & (step < start + length))
            def _():
                total_scr[...] = dot(left_ref[...], right_ref[...], 0, 0)

        for group, bit in enumerate(bits):
            side = table[BITS + bit]
            sent_ref, kept_ref = out_refs[2 * place[group][0] : 2 * place[group][0] + 2]
            for out_ref, value in ((sent_ref, 1 - side), (kept_ref, side)):
                for index in range(count // 2):
                    begin = (group * count + with_bit(index, bit, value)) * rows
                    if rows % 8 == 0:
                        begin = pl.multiple_of(begin, 8)
                    out_ref[place[group][1] * (count // 2) + index] = total_scr[pl.ds(begin, rows)].astype(BF16)

    def right_spec(first, start, length):
        return pl.BlockSpec((seq_len, tile), lambda i, t: (0, first + jnp.clip(i - start, 0, length - 1)))

    return pl.pallas_call(
        kernel,
        grid_spec=pltpu.PrefetchScalarGridSpec(
            num_scalar_prefetch=1,
            grid=(sum(steps),),
            in_specs=[whole(left.shape)]
            + [right_spec(*place) for place in zip(firsts, starts, steps)],
            out_specs=[pl.BlockSpec((depth, rows, tile), lambda i, t: (0, 0, i))] * (2 * outs),
            scratch_shapes=[pltpu.VMEM((height, tile), F32)],
        ),
        out_shape=[jax.ShapeDtypeStruct((depth, rows, columns), BF16)] * (2 * outs),
        compiler_params=params("arbitrary"),
        cost_estimate=cost(
            2 * seq_len * height * columns, 2 * (seq_len * (height + columns) + height * columns)
        ),
        name="split_product",
    )(table, left, *rights)


def relay_kernel(table, kept_sent_ref, arrived_sent_ref, kept_ref, arrived_ref, sent_out_ref, kept_out_ref):
    sent_out_ref[...] = (kept_sent_ref[...].astype(F32) + arrived_sent_ref[...].astype(F32)).astype(BF16)
    kept_out_ref[...] = (kept_ref[...].astype(F32) + arrived_ref[...].astype(F32)).astype(BF16)


def relay(table, kept, arrived, place, bit):
    count, rows, columns = kept.shape

    def block(sent):
        def index(i, t):
            value = t[BITS + bit]
            return (with_bit(i, place, 1 - value if sent else value), 0, 0)

        return pl.BlockSpec((1, rows, columns), index)

    out = pl.BlockSpec((1, rows, columns), lambda i, t: (i, 0, 0))
    return pl.pallas_call(
        relay_kernel,
        grid_spec=pltpu.PrefetchScalarGridSpec(
            num_scalar_prefetch=1,
            grid=(count // 2,),
            in_specs=[block(True), block(True), block(False), block(False)],
            out_specs=[out, out],
        ),
        out_shape=[jax.ShapeDtypeStruct((count // 2, rows, columns), BF16)] * 2,
        compiler_params=params("arbitrary"),
        cost_estimate=cost(0, 6 * count * rows * columns),
        name="relay",
    )(table, kept, arrived, kept, arrived)


def normed_grad_kernel(halves, steps, tile, counts, table, *refs):
    d_refs, own_refs, refs = refs[: 2 * halves], refs[2 * halves : 3 * halves], refs[3 * halves :]
    part_refs = []
    for parts in counts:
        part_refs.append(refs[:parts])
        refs = refs[parts:]
    own_out_ref, other_refs, far_scrs, total_scr = refs[0], refs[1:3], refs[3:-1], refs[-1]

    @pl.when(pl.program_id(0) == 0)
    def _():
        for half in range(halves):
            far_scrs[half][...] = ordered(table, part_refs[half])

    def write(weights):
        total = None
        for half in range(halves):
            units = d_refs[2 * half].shape[1]
            for kind in range(2):
                term = dot(
                    d_refs[2 * half + kind][...], weights[half][:, kind * units : (kind + 1) * units], 1, 1
                )
                total = term if total is None else total + term
        total_scr[...] = total
        rows = own_out_ref.shape[0]
        own_out_ref[...] = total_scr[pl.ds(pl.multiple_of(table[ROW] * rows, rows), rows)]
        other = pl.multiple_of((1 - table[ROW]) * rows, rows)
        for index, other_ref in enumerate(other_refs):

            @pl.when(pl.program_id(0) // steps == index)
            def _():
                other_ref[...] = total_scr[pl.ds(other, rows)].astype(BF16)

    @pl.when(pl.program_id(0) < steps)
    def _():
        write(own_refs)

    @pl.when(pl.program_id(0) >= steps)
    def _():
        start = pl.multiple_of((pl.program_id(0) - steps) * tile, tile)
        write([scr.at[pl.ds(start, tile)] for scr in far_scrs])


def normed_grad(table, d_parts, own, far_parts):
    seq_len = d_parts[0].shape[0]
    units = [part.shape[1] for part in d_parts[::2]]
    features = own[0].shape[0]
    tile = 256
    steps = features // tile
    halves = len(own)
    parts = [piece for half in far_parts for piece in half]

    def side(index):
        return pl.BlockSpec(
            (seq_len // 2, tile), lambda j, t: (0, jnp.clip(j - steps * index, 0, steps - 1))
        )

    own_specs = [
        pl.BlockSpec((tile, 2 * wide), lambda j, t: (jnp.minimum(j, steps - 1), 0)) for wide in units
    ]
    return pl.pallas_call(
        functools.partial(normed_grad_kernel, halves, steps, tile, [len(half) for half in far_parts]),
        grid_spec=pltpu.PrefetchScalarGridSpec(
            num_scalar_prefetch=1,
            grid=(2 * steps,),
            in_specs=[whole(part.shape) for part in d_parts]
            + own_specs
            + [whole(piece.shape) for piece in parts],
            out_specs=[pl.BlockSpec((seq_len // 2, tile), lambda j, t: (0, j))]
            + [side(index) for index in range(2)],
            scratch_shapes=[pltpu.VMEM((features, 2 * wide), BF16) for wide in units]
            + [pltpu.VMEM((seq_len, tile), F32)],
        ),
        out_shape=[
            jax.ShapeDtypeStruct((seq_len // 2, 2 * features), F32),
            *[jax.ShapeDtypeStruct((seq_len // 2, features), BF16)] * 2,
        ],
        compiler_params=params("arbitrary"),
        cost_estimate=cost(
            8 * seq_len * features * sum(units), 8 * sum(units) * (seq_len + features)
        ),
        name="normed_grad",
    )(table, *d_parts, *own, *parts)


def chip_sum_kernel(own_ref, *refs):
    near_refs, (out_ref, *low_refs) = refs[:-3], refs[-3:]
    width = low_refs[0].shape[1]
    start = 0
    for near_ref in near_refs:
        columns = slice(start, start + near_ref.shape[1])
        total = own_ref[:, columns] + near_ref[...].astype(F32)
        out_ref[:, columns] = total
        start += near_ref.shape[1]
    for index, low_ref in enumerate(low_refs):
        low_ref[...] = out_ref[:, index * width : (index + 1) * width].astype(BF16)


def chip_sum(own, nears):
    rows, width = own.shape
    block = pl.BlockSpec((rows // 4, width), lambda i: (i, 0))
    return pl.pallas_call(
        chip_sum_kernel,
        grid=(4,),
        in_specs=[block] + [pl.BlockSpec((rows // 4, near.shape[1]), lambda i: (i, 0)) for near in nears],
        out_specs=[block] + [pl.BlockSpec((rows // 4, width // 2), lambda i: (i, 0))] * 2,
        out_shape=[jax.ShapeDtypeStruct(own.shape, F32)]
        + [jax.ShapeDtypeStruct((rows, width // 2), BF16)] * 2,
        compiler_params=params("arbitrary"),
        cost_estimate=cost(0, 12 * rows * width),
        name="chip_sum",
    )(own, *nears)


def norm_back_kernel(
    width, table, chip_ref, far_own_ref, far_other_ref, hidden_ref, scale_ref, grad_ref, gain_ref, out_ref, low0_ref, low1_ref, gain_grad_ref
):
    @pl.when(pl.program_id(0) == 0)
    def _():
        gain_grad_ref[...] = jnp.zeros_like(gain_grad_ref)

    d_left = chip_ref[:, :width] + far_other_ref[...].astype(F32)
    d_right = chip_ref[:, width:] + far_own_ref[...].astype(F32)
    left, right = hidden_ref[:, :width], hidden_ref[:, width:]
    scale = scale_ref[:, :1]
    gain_grad_ref[...] += jnp.sum(d_left * left * scale, axis=0, keepdims=True)
    left_weighted, right_weighted = d_left * gain_ref[:, :width], d_right * gain_ref[:, width:]
    inner = jnp.sum(left_weighted * left, axis=1, keepdims=True) + jnp.sum(
        right_weighted * right, axis=1, keepdims=True
    )
    factor = scale * scale * (inner / (2 * width))
    d_left = grad_ref[:, :width].astype(F32) + scale * (left_weighted - left * factor)
    d_right = grad_ref[:, width:].astype(F32) + scale * (right_weighted - right * factor)
    out_ref[...] = d_left
    low0_ref[...] = d_left.astype(BF16)
    low1_ref[...] = d_right.astype(BF16)


def norm_back(table, chip, far, hidden, scale, grad, gain):
    rows, width = chip.shape
    block = rows // 4

    def own(columns):
        return pl.BlockSpec((block, columns), lambda i, t: (i, 0))

    def tokens(columns):
        return pl.BlockSpec((block, columns), lambda i, t: (4 * t[ROW] + i, 0))

    return pl.pallas_call(
        functools.partial(norm_back_kernel, width // 2),
        grid_spec=pltpu.PrefetchScalarGridSpec(
            num_scalar_prefetch=1,
            grid=(4,),
            in_specs=[own(width), own(width // 2), own(width // 2), tokens(width), tokens(128), tokens(width), whole((1, width))],
            out_specs=[own(width // 2)] * 3 + [whole((1, width // 2))],
        ),
        out_shape=[
            jax.ShapeDtypeStruct((rows, width // 2), F32),
            jax.ShapeDtypeStruct((rows, width // 2), BF16),
            jax.ShapeDtypeStruct((rows, width // 2), BF16),
            jax.ShapeDtypeStruct((1, width // 2), F32),
        ],
        compiler_params=params("arbitrary"),
        cost_estimate=cost(0, 20 * rows * width),
        name="norm_back",
    )(table, chip, *far, hidden, scale, grad, gain)


def project_back_kernel(
    count, bit, table, query_ref, key_value_ref, arrived_ref, normed_ref, weight_ref, group_ref,
    d_hidden_ref, d_hidden_near_ref, sent_ref, kept_ref, own_ref, other_ref, bias_ref, d_scr, total_scr, hidden_scr, out_scr,
):
    first = table[COL] == 0
    query_width = query_ref.shape[1] - 2 * HEAD_DIM
    own, far = query_ref[:, :query_width], arrived_ref[:, :query_width]
    d_scr[:, :query_width] = jnp.where(first, own, far)
    d_scr[:, query_width : 2 * query_width] = jnp.where(first, far, own)
    d_key_value = key_value_ref[...] + arrived_ref[:, query_width:].astype(F32)
    d_scr[:, 2 * query_width :] = d_key_value.astype(BF16)
    d_projected = d_scr[...]
    bias_ref[...] = jnp.sum(d_projected.astype(F32), axis=0, keepdims=True)
    total_scr[...] = dot(normed_ref[...], d_projected, 0, 0)
    tokens = own_ref.shape[0]
    hidden_scr[:tokens] = jnp.where(table[ROW] == 0, d_hidden_ref[...], d_hidden_near_ref[...])
    hidden_scr[tokens:] = jnp.where(table[ROW] == 0, d_hidden_near_ref[...], d_hidden_ref[...])
    out_scr[...] = dot(group_ref[...], hidden_scr[...], 0, 0)
    rows = sent_ref.shape[1]
    width = total_scr.shape[1]
    side = table[BITS + bit]
    for out_ref, value in ((sent_ref, 1 - side), (kept_ref, side)):
        for index in range(count // 2):
            start = with_bit(index, bit, value) * rows
            if rows % 8 == 0:
                start = pl.multiple_of(start, 8)
            out_ref[index, :, :width] = total_scr[pl.ds(start, rows)].astype(BF16)
            out_ref[index, :, width:] = out_scr[pl.ds(start, rows)].astype(BF16)
    for out_ref, half in ((own_ref, table[ROW]), (other_ref, 1 - table[ROW])):
        d_half = d_scr[pl.ds(pl.multiple_of(half * tokens, tokens), tokens)]
        out_ref[...] = dot(d_half, weight_ref[...], 1, 1).astype(out_ref.dtype)


def project_back(table, d_query, d_key_value, arrived, normed, weight, group, d_hidden, near, count, bit):
    seq_len = d_query.shape[0]
    width, columns = weight.shape
    rows = width // count
    arrays = (d_query, d_key_value, arrived, normed, weight, group, d_hidden, near)
    terms = (count // 2, rows, columns + d_hidden.shape[1])
    return pl.pallas_call(
        functools.partial(project_back_kernel, count, bit),
        grid_spec=pltpu.PrefetchScalarGridSpec(
            num_scalar_prefetch=1,
            grid=(1,),
            in_specs=[whole(array.shape) for array in arrays],
            out_specs=[
                whole(terms), whole(terms), whole((seq_len // 2, width)), whole((seq_len // 2, width)),
                whole((1, columns)),
            ],
            scratch_shapes=[
                pltpu.VMEM((seq_len, columns), BF16), pltpu.VMEM((width, columns), F32),
                pltpu.VMEM((seq_len, d_hidden.shape[1]), BF16), pltpu.VMEM((width, d_hidden.shape[1]), F32),
            ],
        ),
        out_shape=[
            jax.ShapeDtypeStruct(terms, BF16),
            jax.ShapeDtypeStruct(terms, BF16),
            jax.ShapeDtypeStruct((seq_len // 2, width), F32),
            jax.ShapeDtypeStruct((seq_len // 2, width), BF16),
            jax.ShapeDtypeStruct((1, columns), F32),
        ],
        compiler_params=params("arbitrary"),
        cost_estimate=cost(4 * seq_len * width * columns, 8 * seq_len * columns),
        name="project_back",
    )(table, *arrays)


def swap(part, axis_name):
    return lax.ppermute(part, axis_name, [(0, 1), (1, 0)])


def dp_swap(part, bit):
    count = lax.axis_size("dp")
    return lax.ppermute(part, "dp", [(i, i ^ (1 << bit)) for i in range(count)])


def after(value, *earlier):
    return lax.optimization_barrier((value,) + earlier)[0]


def pick(array, index, axis):
    return lax.dynamic_index_in_dim(array, index, axis, keepdims=False)


def in_order(index, own, other, axis):
    first = jnp.where(index == 0, own, other)
    second = jnp.where(index == 0, other, own)
    return jnp.concatenate([first, second], axis=axis)


def quad_slots(rank):
    low, high = rank % 2, rank // 2 % 2
    return jnp.stack([2 * high + low, 4 + 2 * low + high])


class Line:
    def __init__(self):
        self.last = ()

    def step(self, value):
        return after(value, *self.last) if self.last else value

    def mark(self, *values):
        self.last = values


class Quad:
    def __init__(self, part, rank):
        self.part = part
        self.low, self.high = rank % 2, rank // 2 % 2

    def first_round(self, line):
        if isinstance(self.part, list):
            self.sent = [line.step(slot) for slot in self.part]
        else:
            part = line.step(self.part)
            self.sent = lax.optimization_barrier([part[0], part[1]])
        line.mark(*self.sent)
        self.arriving = dp_swap(self.sent[0], 0), dp_swap(self.sent[1], 1)

    def second_round(self, line):
        arrived = [line.step(value) for value in self.arriving]
        pairs = lax.optimization_barrier(
            (in_order(self.low, self.sent[0], arrived[0], 0), in_order(self.high, self.sent[1], arrived[1], 0))
        )
        line.mark(*pairs)
        self.parts = [*pairs, dp_swap(pairs[0], 1), dp_swap(pairs[1], 0)]
        return self.parts


def laid_out(parts, rank):
    low, high = rank % 2, rank // 2 % 2
    return [in_order(high, parts[0], parts[2], 0), in_order(low, parts[1], parts[3], 0)]


class Scatter:
    def __init__(self, table, sent, kept, order, line):
        self.table, self.kept = table, kept
        bits = lax.axis_size("dp").bit_length() - 1
        self.order = list(order) + [bit for bit in range(bits) if bit not in order]
        self.left = list(range(bits))
        self.pass_on(sent, line)

    def pass_on(self, sent, line):
        bit = self.order.pop(0)
        self.left.remove(bit)
        self.arriving = dp_swap(line.step(sent), bit)

    def relay(self, line):
        bit = self.order[0]
        sent, self.kept = relay(
            self.table, self.kept, line.step(self.arriving), self.left.index(bit), bit
        )
        line.mark(sent)
        self.pass_on(sent, line)

    def finish(self, line):
        while self.order:
            self.relay(line)
        total = self.kept.astype(F32) + line.step(self.arriving).astype(F32)
        total = lax.optimization_barrier(total)
        line.mark(total)
        return total


def shards(
    block_input,
    segment_ids,
    first_gain,
    qkv_weight,
    qkv_bias,
    output_weight,
    second_gain,
    gate_up_weight,
    down_weight,
    output_grad,
):
    count = lax.axis_size("dp")
    rank = lax.axis_index("dp")
    row = lax.axis_index("row")
    col = lax.axis_index("col")
    qkv_block = qkv_weight[0, 0]
    out_block = output_weight[0, 0]
    gate_up_block = gate_up_weight[0, 0]
    down_block = down_weight[0, 0]
    seq_len = segment_ids.shape[0]
    own_rows, half_width = block_input.shape
    model_width = 2 * half_width
    query_width = HEADS // 4 * HEAD_DIM
    own_units = down_block.shape[0] // 2
    segment = own_units // count
    step = max(16, 128 // count)
    padded = pl.cdiv(segment, 3 * step) * 3 * step
    feature_rows = half_width // count
    slot_rows = half_width // 8
    slots = quad_slots(rank)
    bits = count.bit_length() - 1

    def own_tokens(array):
        return lax.dynamic_slice_in_dim(array, row * own_rows, own_rows, 0)

    def slot_pair(array):
        parts = array.reshape((8, array.shape[0] // 8) + array.shape[1:])
        return [pick(parts, slot, 0) for slot in slots]

    def swap_pair(pair):
        return [swap(slot, "col") for slot in pair]

    table = jnp.stack([row, col] + [(rank >> bit) & 1 for bit in range(bits)]).astype(jnp.int32)
    line = Line()
    pair_first, line_first = [0, 1, 2], [1, 0, 2]

    def qkv_columns(side):
        heads = lax.dynamic_slice_in_dim(qkv_block, side * query_width, query_width, 1)
        return jnp.concatenate([heads, qkv_block[:, 2 * query_width :]], axis=1)

    gains = jnp.stack([first_gain, second_gain])
    gains = jnp.concatenate([gains, swap(gains, "col")], axis=1)
    early_send = slot_pair(jnp.concatenate([qkv_columns(1 - col), out_block], axis=1))
    early_send = lax.optimization_barrier(early_send)
    early_quad = Quad(swap_pair(early_send), rank)
    qkv_own = qkv_columns(col)
    qkv_width = qkv_own.shape[1]
    bias = qkv_bias[0]
    bias_own = jnp.concatenate(
        [lax.dynamic_slice_in_dim(bias, col * query_width, query_width, 0), bias[2 * query_width :]]
    )

    (send,) = unit_columns(
        after(gate_up_block, *early_send, gains), 1 - col, slots, count, slot_rows, padded, ((0, 0),)
    )
    line.mark(send)

    near = swap(block_input, "row")
    out_near = swap(out_block, "row")
    far = swap(after(block_input, *early_send), "col")

    position_index = jnp.arange(seq_len, dtype=jnp.int32)
    doc_first = jnp.concatenate([jnp.ones((1,), jnp.bool_), segment_ids[1:] != segment_ids[:-1]])
    positions = position_index - lax.cummax(jnp.where(doc_first, position_index, 0), axis=0)
    frequency = ROPE_BASE ** (-jnp.arange(0, HEAD_DIM, 2, dtype=F32) / HEAD_DIM)
    angles = positions.astype(F32)[:, None] * frequency[None, :]
    cosine, sine = jnp.cos(angles), jnp.sin(angles)
    cosine = jnp.concatenate([cosine, cosine], axis=1)
    sine = jnp.concatenate([-sine, sine], axis=1)
    seg_col, seg_row = segment_ids[:, None], segment_ids[None, :]

    low_slots, high_slots = jnp.arange(4), 4 + jnp.arange(4)
    early_quad.first_round(line)
    gate_up_quad = Quad(swap(line.step(send), "col"), rank)
    outs = ((0, 0), (0, 1), (1, 1))
    gate_up_own = unit_columns(
        line.step(gate_up_block), col, low_slots, count, slot_rows, padded, outs, low_slots, 8
    )
    line.mark(*gate_up_own)
    early_far = early_quad.second_round(line)
    far_halves = lax.optimization_barrier((far[: own_rows // 2], far[own_rows // 2 :]))
    far_near = [swap(half, "row") for half in far_halves]
    gate_up_own = unit_columns(
        line.step(gate_up_block), col, high_slots, count, slot_rows, padded, outs, high_slots, 8, gate_up_own
    )
    line.mark(*gate_up_own)
    *gate_up_own, send = [part.reshape(half_width, -1) for part in gate_up_own]
    out_near = line.step(out_near)
    line.mark(out_near)
    stream, first_normed, first_scale, query, key, value = project(
        table, line.step(block_input), near, far, far_near, gains[:1], qkv_own, early_far,
        bias_own[None], cosine, sine,
    )
    line.mark(query)
    gate_up_quad.first_round(line)
    attended, *attended_parts = attend(line.step(query), key, value, seg_col, seg_row)
    line.mark(attended)
    attended_far = [swap(part, "col") for part in attended_parts]
    attended_near = swap(attended, "row")
    gate_up_far = [gate_up_quad.second_round(line)]
    out_far = lax.optimization_barrier(
        laid_out([line.step(part)[:, qkv_width:] for part in early_far], rank)
    )
    line.mark(*out_far)
    out_far_near = [swap(part, "row") for part in out_far]
    share = count // 8
    send_ranks = (slots[:, None] * share + jnp.arange(share)[None, :]).reshape(-1)
    (down_send,) = unit_rows(line.step(down_block), 1 - col, send_ranks, count, padded, (0,))
    line.mark(down_send)
    down_own = unit_rows(line.step(down_block), col, jnp.arange(count), count, padded)
    line.mark(*down_own)
    down_own = [part.reshape(-1, half_width) for part in down_own]
    attended_far = [line.step(part) for part in attended_far]
    line.mark(*attended_far)
    attended_far_near = [swap(part, "row") for part in attended_far]
    down_quad = Quad(swap(line.step(down_send).reshape(2, -1, half_width), "col"), rank)
    grad_far = swap(line.step(output_grad), "col")
    hidden_one, second_normed, second_scale, attended_group = residual(
        table, line.step(stream), [attended, attended_near, *attended_far, *attended_far_near],
        out_block, out_near, out_far, out_far_near, gains[1:],
    )
    line.mark(second_normed)
    gate_up_far[0] = [line.step(part) for part in gate_up_far[0]]
    line.mark(*gate_up_far[0])
    down_quad.first_round(line)

    act0, gate_factor0, up_factor0 = activate(
        table, line.step(second_normed), gate_up_own[0], gate_up_far[0]
    )
    line.mark(act0)
    grad_far = line.step(grad_far)
    line.mark(grad_far)
    down_far = [down_quad.second_round(line)]
    grad_near = swap(line.step(output_grad), "row")
    grad_far_near = swap(grad_far, "row")
    gate_up_far.append([swap(line.step(send), "col")])
    grad_full = join(table, line.step(output_grad), grad_near, grad_far, grad_far_near)
    line.mark(grad_full)

    def down_terms(act, order):
        sent, kept = split_product(
            table, line.step(act), [(grad_full, 0, 2)], half_width, 1, count, [order[0]]
        )
        line.mark(sent)
        return sent, kept

    def gate_up_terms(d_gate, d_up, order, merge):
        tile = tile_of(d_gate.shape[1], 768)
        rights = [(part, 0, part.shape[1] // tile) for part in (d_gate, d_up)]
        terms = split_product(
            table, line.step(second_normed), rights, tile, 2, count, [order[0]] * 2, merge
        )
        line.mark(terms[0])
        return terms

    terms = down_terms(act0, pair_first)
    down_far[0] = [line.step(part) for part in down_far[0]]
    line.mark(*down_far[0])
    down_sum0 = Scatter(table, *terms, pair_first, line)
    begin, width, full = halves_of(segment, padded)[1]
    down_send = pick(line.step(down_block).reshape(count, 2, segment, half_width), 1 - col, 1)
    down_send = jnp.pad(down_send[:, begin : begin + width], ((0, 0), (0, full - width), (0, 0)))
    down_send = lax.optimization_barrier(down_send.reshape(-1, half_width))
    line.mark(down_send)
    down_far.append([swap(down_send, "col")])
    d_gate0, d_up0 = activate_back(
        table, line.step(grad_full), down_own[0], down_far[0], gate_factor0, up_factor0
    )
    line.mark(d_gate0)
    own_sent0, own_kept0, far_sent0, far_kept0 = gate_up_terms(d_gate0, d_up0, pair_first, False)
    far_sum0 = Scatter(table, far_sent0, far_kept0, pair_first, line)
    act1, gate_factor1, up_factor1 = activate(
        table, line.step(second_normed), gate_up_own[1], gate_up_far[1]
    )
    line.mark(act1)
    down_far[1] = [line.step(down_far[1][0])]
    line.mark(*down_far[1])
    down_sum0.relay(line)
    own_sum0 = Scatter(table, own_sent0, own_kept0, pair_first, line)
    d_gate1, d_up1 = activate_back(
        table, line.step(grad_full), down_own[1], down_far[1], gate_factor1, up_factor1
    )
    line.mark(d_gate1)
    d_second_own, *d_second_other = normed_grad(
        table, [line.step(d_gate0), d_up0, d_gate1, d_up1], gate_up_own, gate_up_far
    )
    line.mark(*d_second_other)
    d_second_near = [swap(part, "row") for part in d_second_other]
    down_terms1 = down_terms(act1, pair_first)
    down_sum0.relay(line)
    far_sum0.relay(line)
    d_second_chip, *d_second_low = chip_sum(line.step(d_second_own), d_second_near)
    line.mark(*d_second_low)
    d_second_far = [swap(part, "col") for part in d_second_low]
    gate_up_terms1 = gate_up_terms(d_gate1, d_up1, pair_first, True)
    mlp_own, mlp_other, mlp_other_far = down(table, [line.step(act0), act1], down_own, down_far)
    line.mark(mlp_other)
    far_sum0.relay(line)
    own_sum0.relay(line)
    down_sum0 = down_sum0.finish(line)[0]
    down_sum1 = Scatter(table, *down_terms1, pair_first, line)
    mlp_near = swap(line.step(mlp_other_far), "row")

    d_hidden, *d_hidden_low, second_gain_part = norm_back(
        table, line.step(d_second_chip), d_second_far, hidden_one, second_scale, grad_full, gains[1:]
    )
    line.mark(*d_hidden_low)
    d_hidden_near = [swap(part, "row") for part in d_hidden_low]
    mlp_sent = mlp_own[:, half_width:] + line.step(mlp_near).astype(F32)
    mlp_sent = lax.optimization_barrier(mlp_sent.astype(BF16))
    line.mark(mlp_sent)

    d_projected_sent, d_key_value = attend_back(
        table, line.step(query), key, value, seg_col, seg_row, [*d_hidden_low, *d_hidden_near], out_block, out_far,
        cosine, sine,
    )
    line.mark(d_projected_sent)
    arrived = swap(d_projected_sent, "col")
    down_sum1.relay(line)
    gate_up_sum1 = Scatter(table, *gate_up_terms1, pair_first, line)
    sent, kept, d_first_own, d_first_other, bias_part = project_back(
        table, line.step(d_projected_sent), d_key_value, arrived, first_normed, qkv_block, attended_group,
        d_hidden_low[0], d_hidden_near[0], count, 0,
    )
    line.mark(sent)
    heads_sum = Scatter(table, sent, kept, pair_first, line)
    d_first_near = swap(d_first_other, "row")
    own_sum0.relay(line)
    down_sum1.relay(line)
    far_sum0 = far_sum0.finish(line)[0]
    gate_up_sum1.relay(line)

    d_first = line.step(d_first_own) + d_first_near.astype(F32)
    stream_own = block_input.astype(F32)
    first_scale_own = own_tokens(first_scale)[:, :1]
    first_gain_part = jnp.sum(d_first * stream_own * first_scale_own, axis=0)
    weighted = d_first * first_gain
    inner = jnp.sum(weighted * stream_own, axis=1)
    inner = (inner + swap(inner, "col"))[:, None]
    input_grad = d_hidden + first_scale_own * (
        weighted - stream_own * (first_scale_own * first_scale_own) * (inner / model_width)
    )

    gain_parts = line.step(jnp.concatenate([first_gain_part, second_gain_part[0]]))
    gain_parts = lax.optimization_barrier(gain_parts + swap(gain_parts, "row"))
    line.mark(gain_parts)
    small = line.step(jnp.concatenate([gain_parts, bias_part[0]]))

    def dp_step(part, bit):
        part = lax.optimization_barrier(part + line.step(dp_swap(part, bit)))
        line.mark(part)
        return part

    heads_sum.relay(line)
    far_sum0 = swap(line.step(far_sum0.astype(BF16)), "col")
    down_sum0_far = swap(line.step(down_sum0[:, half_width:].astype(BF16)), "col")
    own_sum0 = own_sum0.finish(line)[0]
    down_sum1 = down_sum1.finish(line)[0]
    mlp_far = swap(line.step(mlp_sent), "col")
    down_sum1_far = swap(line.step(down_sum1[:, half_width:].astype(BF16)), "col")
    gate_up_sum1.relay(line)
    small = dp_step(small, 0)
    heads_sum.relay(line)
    hidden_own = own_tokens(hidden_one)[:, :half_width]
    mlp_near = swap(line.step(mlp_other), "row")
    mlp_chip = mlp_own[:, :half_width] + mlp_near.astype(F32)
    block_output = (hidden_own + (mlp_chip + line.step(mlp_far).astype(F32))).astype(BF16)
    small = dp_step(small, 1)
    own_sum1, far_sum1 = gate_up_sum1.finish(line)
    far_sum1 = swap(line.step(far_sum1.astype(BF16)), "col")
    far_sum1 = line.step(far_sum1)
    line.mark(far_sum1)
    for bit in range(2, bits):
        small = dp_step(small, bit)
    heads_sum = heads_sum.finish(line)[0]
    qkv_sum, out_sum = heads_sum[:, : bias.shape[0]], heads_sum[:, bias.shape[0] :]
    bias_width = bias.shape[0] // count
    bias_grad = lax.dynamic_slice_in_dim(small[model_width:], rank * bias_width, bias_width, 0)

    widths = [width for _, width, _ in halves_of(segment, padded)]
    own_rows_sum = [
        part[:width, :half_width] for part, width in zip((down_sum0, down_sum1), widths)
    ]
    far_rows_sum = [
        part[:width].astype(F32) for part, width in zip((down_sum0_far, down_sum1_far), widths)
    ]
    down_grad = in_order(
        col, jnp.concatenate(own_rows_sum, axis=0), jnp.concatenate(far_rows_sum, axis=0), 0
    )
    gate_up_grad = spread_columns(
        table, (own_sum0, own_sum1), (far_sum0, far_sum1), count, segment, padded
    )

    return (
        block_output,
        input_grad,
        small[:half_width],
        qkv_sum[None, None],
        bias_grad[None],
        out_sum[None, None],
        small[half_width:model_width],
        gate_up_grad[None, None],
        down_grad[None, None],
    )


def solution(mesh):
    placed = (
        P(("dp", "row"), "col"),
        P("dp"),
        P("col"),
        P("col", "row", None, None),
        P("row", None),
        P("row", "col", None, None),
        P("col"),
        P("col", "row", None, None),
        P("row", "col", None, None),
        P(("dp", "row"), "col"),
    )
    return jax.shard_map(
        shards,
        mesh=mesh,
        in_specs=placed,
        out_specs=(
            P(("dp", "row"), "col"),
            P(("dp", "row"), "col"),
            P("col"),
            P("col", "row", "dp", None),
            P("row", "dp"),
            P("row", "col", "dp", None),
            P("col"),
            P("col", "row", "dp", None),
            P("row", "col", "dp", None),
        ),
        check_vma=False,
    )
```

```python
import functools
import jax
import jax.numpy as jnp
from jax import lax
from jax.experimental import pallas as pl
from jax.experimental.pallas import tpu as pltpu
from jax.sharding import PartitionSpec as P

HEADS = 12
KV_HEADS = 2
HEAD_DIM = 128
EPSILON = 1e-06
ROPE_BASE = 1000000.0
MASKED = -1e30
F32 = jnp.float32
BF16 = jnp.bfloat16
VMEM_LIMIT = 60 * 1024 * 1024


def dot(left, right, left_dim, right_dim):
    return lax.dot_general(
        left, right, (((left_dim,), (right_dim,)), ((), ())), preferred_element_type=F32
    )


def params(*semantics):
    return pltpu.CompilerParams(
        dimension_semantics=semantics or None, vmem_limit_bytes=VMEM_LIMIT
    )


def cost(flops, moved):
    return pl.CostEstimate(flops=1, bytes_accessed=1, transcendentals=0)


def whole(shape):
    return pl.BlockSpec(shape, lambda *_: (0,) * len(shape))


ROW, COL, LOW, HIGH = range(4)
BITS = 2


def with_bit(index, place, value):
    return ((index >> place) << (place + 1)) | (value << place) | (index & ((1 << place) - 1))


def ordered(table, parts, columns=slice(None)):
    if len(parts) == 1:
        return parts[0][:, columns]
    first, second, first_other, second_other = [part[:, columns] for part in parts]
    high, low = table[HIGH] == 0, table[LOW] == 0
    return jnp.concatenate(
        [
            jnp.where(high, first, first_other),
            jnp.where(high, first_other, first),
            jnp.where(low, second, second_other),
            jnp.where(low, second_other, second),
        ],
        axis=0,
    )


def halves_of(segment, padded):
    first = 2 * padded // 3
    return ((0, first, first), (first, segment - first, padded - first))


def units_kernel(count, segment, padded, outs, table, block_ref, *refs):
    rows = block_ref.shape[0]
    out_refs = refs[-len(outs) :]

    def write(side):
        for out_ref, (other, half) in zip(out_refs, outs):
            begin, width, full = halves_of(segment, padded)[half]
            parts = []
            for kind in range(2):
                for k in range(count):
                    start = ((kind * count + k) * 2 + (side ^ other)) * segment + begin
                    parts.append(block_ref[:, start : start + width])
                    if width < full:
                        parts.append(jnp.zeros((rows, full - width), block_ref.dtype))
            out_ref[0] = jnp.concatenate(parts, axis=1)

    @pl.when(table[0] == 0)
    def _():
        write(0)

    @pl.when(table[0] != 0)
    def _():
        write(1)


def unit_columns(block, side, slots, count, rows, padded, outs, places=None, depth=None, begun=None):
    columns = block.shape[1]
    segment = columns // (4 * count)
    units = [2 * count * halves_of(segment, padded)[half][2] for _, half in outs]
    steps = slots.shape[0]
    depth = steps if depth is None else depth
    places = jnp.arange(steps) if places is None else places
    begun = [] if begun is None else begun
    table = jnp.concatenate([side.reshape(1), slots, places]).astype(jnp.int32)
    return pl.pallas_call(
        functools.partial(units_kernel, count, segment, padded, outs),
        grid_spec=pltpu.PrefetchScalarGridSpec(
            num_scalar_prefetch=1,
            grid=(steps,),
            in_specs=[pl.BlockSpec((rows, columns), lambda i, t: (t[1 + i], 0))]
            + [pl.BlockSpec(memory_space=pl.ANY)] * len(begun),
            out_specs=[pl.BlockSpec((1, rows, wide), lambda i, t: (t[1 + steps + i], 0, 0)) for wide in units],
        ),
        out_shape=[jax.ShapeDtypeStruct((depth, rows, wide), block.dtype) for wide in units],
        input_output_aliases={2 + index: index for index in range(len(begun))},
        compiler_params=params("arbitrary"),
        cost_estimate=cost(0, 4 * steps * rows * sum(units)),
        name="unit_columns",
    )(table, block, *begun)


def unit_rows_kernel(parts, table, block_ref, *out_refs):
    for out_ref, (begin, width, full) in zip(out_refs, parts):
        if width == full and begin % 16 == 0 and full % 16 == 0:
            out_ref[0] = block_ref[0, 0, begin : begin + width]
        else:
            part = block_ref[0, 0].astype(F32)[begin : begin + width]
            part = jnp.concatenate([part, jnp.zeros((full - width, part.shape[1]), F32)], axis=0)
            out_ref[0] = part.astype(out_ref.dtype)


def unit_rows(block, side, ranks, count, padded, halves=(0, 1)):
    rows, width = block.shape
    segment = rows // (2 * count)
    parts = [halves_of(segment, padded)[half] for half in halves]
    steps = ranks.shape[0]
    table = jnp.concatenate([side.reshape(1), ranks]).astype(jnp.int32)
    return pl.pallas_call(
        functools.partial(unit_rows_kernel, parts),
        grid_spec=pltpu.PrefetchScalarGridSpec(
            num_scalar_prefetch=1,
            grid=(steps,),
            in_specs=[pl.BlockSpec((1, 1, segment, width), lambda i, t: (t[1 + i], t[0], 0, 0))],
            out_specs=[pl.BlockSpec((1, full, width), lambda i, t: (i, 0, 0)) for _, _, full in parts],
        ),
        out_shape=[jax.ShapeDtypeStruct((steps, full, width), block.dtype) for _, _, full in parts],
        compiler_params=params("arbitrary"),
        cost_estimate=cost(0, 4 * steps * segment * width),
        name="unit_rows",
    )(table, block.reshape(count, 2, segment, width))


def spread_kernel(count, segment, padded, table, own0_ref, own1_ref, far0_ref, far1_ref, out_ref):
    def write(sides):
        pieces = []
        for kind in range(2):
            for k in range(count):
                for side in sides:
                    for ref, (_, width, full) in zip(side, halves_of(segment, padded)):
                        start = (kind * count + k) * full
                        pieces.append(ref[:, start : start + width].astype(F32))
        out_ref[...] = jnp.concatenate(pieces, axis=1)

    own, far = (own0_ref, own1_ref), (far0_ref, far1_ref)

    @pl.when(table[COL] == 0)
    def _():
        write((own, far))

    @pl.when(table[COL] != 0)
    def _():
        write((far, own))


def spread_columns(table, own, far, count, segment, padded):
    rows = own[0].shape[0]
    step = rows // 3 if rows % 24 == 0 else rows
    parts = [pl.BlockSpec((step, part.shape[1]), lambda i, t: (i, 0)) for part in (*own, *far)]
    columns = 4 * count * segment
    return pl.pallas_call(
        functools.partial(spread_kernel, count, segment, padded),
        grid_spec=pltpu.PrefetchScalarGridSpec(
            num_scalar_prefetch=1,
            grid=(rows // step,),
            in_specs=parts,
            out_specs=pl.BlockSpec((step, columns), lambda i, t: (i, 0)),
        ),
        out_shape=jax.ShapeDtypeStruct((rows, columns), F32),
        compiler_params=params("arbitrary"),
        cost_estimate=cost(0, 7 * rows * columns),
        name="spread_columns",
    )(table, *own, *far)


def project_kernel(
    width, table, own_ref, near_ref, far_ref, far_near0_ref, far_near1_ref, gain_ref, weight_ref,
    part0_ref, part1_ref, part2_ref, part3_ref, bias_ref, cosine_ref, sine_ref, stream_ref, normed_ref, scale_ref, query_ref, key_ref, value_ref,
):
    half = pl.program_id(0) * 2 // pl.num_programs(0)
    mine = half == table[ROW]
    left = jnp.where(mine, own_ref[...], near_ref[...]).astype(F32)
    even = pl.program_id(0) % 2 == 0
    right = jnp.where(
        mine,
        far_ref[...],
        jnp.where(even, far_near0_ref[...], far_near1_ref[...]),
    ).astype(F32)
    squares = jnp.sum(left * left, axis=1, keepdims=True) + jnp.sum(
        right * right, axis=1, keepdims=True
    )
    scale = lax.rsqrt(squares / (2 * width) + EPSILON)
    left_normed = (left * scale * gain_ref[:, :width]).astype(BF16)
    right_normed = (right * scale * gain_ref[:, width:]).astype(BF16)
    stream_ref[:, :width] = left.astype(BF16)
    stream_ref[:, width:] = right.astype(BF16)
    normed_ref[...] = left_normed
    scale_ref[...] = jnp.broadcast_to(scale, scale_ref.shape)
    far_weight = ordered(table, (part0_ref, part1_ref, part2_ref, part3_ref))
    projected = (
        dot(left_normed, weight_ref[...], 1, 0) + dot(right_normed, far_weight, 1, 0) + bias_ref[...]
    )
    cosine, sine = cosine_ref[...], sine_ref[...]

    def rotated(values):
        return (values * cosine + pltpu.roll(values, HEAD_DIM // 2, 1) * sine).astype(BF16)

    query_width = query_ref.shape[1]
    for start in range(0, query_width, HEAD_DIM):
        query_ref[:, start : start + HEAD_DIM] = rotated(projected[:, start : start + HEAD_DIM])
    key_ref[...] = rotated(projected[:, query_width : query_width + HEAD_DIM])
    value_ref[...] = projected[:, query_width + HEAD_DIM :].astype(BF16)


def project(table, own, near, far, far_near, gain, weight, far_parts, bias, cosine, sine):
    rows, width = own.shape
    seq_len = 2 * rows
    block = rows // 2
    per_half = 2
    out_width = weight.shape[1]
    query_width = out_width - 2 * HEAD_DIM
    part = pl.BlockSpec((block, width), lambda i, t: (i % per_half, 0))

    def tokens(columns):
        return pl.BlockSpec((block, columns), lambda i, t: (i, 0))

    return pl.pallas_call(
        functools.partial(project_kernel, width),
        grid_spec=pltpu.PrefetchScalarGridSpec(
            num_scalar_prefetch=1,
            grid=(seq_len // block,),
            in_specs=[part, part, part]
            + [whole((block, width))] * 2
            + [whole((1, 2 * width)), whole(weight.shape)]
            + [whole((piece.shape[0], out_width)) for piece in far_parts]
            + [whole((1, out_width)), tokens(HEAD_DIM), tokens(HEAD_DIM)],
            out_specs=[
                tokens(2 * width), tokens(width), tokens(128),
                tokens(query_width), tokens(HEAD_DIM), tokens(HEAD_DIM),
            ],
        ),
        out_shape=[
            jax.ShapeDtypeStruct((seq_len, 2 * width), BF16),
            jax.ShapeDtypeStruct((seq_len, width), BF16),
            jax.ShapeDtypeStruct((seq_len, 128), F32),
            jax.ShapeDtypeStruct((seq_len, query_width), BF16),
            jax.ShapeDtypeStruct((seq_len, HEAD_DIM), BF16),
            jax.ShapeDtypeStruct((seq_len, HEAD_DIM), BF16),
        ],
        compiler_params=params("arbitrary"),
        cost_estimate=cost(4 * seq_len * width * out_width, 12 * seq_len * width),
        name="project",
    )(table, own, near, far, *far_near, gain, weight, *far_parts, bias, cosine, sine)


def join_kernel(width, table, own_ref, near_ref, far_ref, far_near_ref, out_ref):
    mine = pl.program_id(0) * 2 // pl.num_programs(0) == table[ROW]
    out_ref[:, :width] = jnp.where(mine, own_ref[...], near_ref[...])
    out_ref[:, width:] = jnp.where(mine, far_ref[...], far_near_ref[...])


def join(table, own, near, far, far_near):
    rows, width = own.shape
    block = min(256, rows)
    per_half = rows // block
    part = pl.BlockSpec((block, width), lambda i, t: (i % per_half, 0))
    return pl.pallas_call(
        functools.partial(join_kernel, width),
        grid_spec=pltpu.PrefetchScalarGridSpec(
            num_scalar_prefetch=1,
            grid=(2 * rows // block,),
            in_specs=[part] * 4,
            out_specs=pl.BlockSpec((block, 2 * width), lambda i, t: (i, 0)),
        ),
        out_shape=jax.ShapeDtypeStruct((2 * rows, 2 * width), own.dtype),
        compiler_params=params("arbitrary"),
        cost_estimate=cost(0, 16 * rows * width),
        name="join",
    )(table, own, near, far, far_near)


def block_probs(query, key, seg_col, seg_row, start, stop):
    scores = dot(query, key, 1, 1) * HEAD_DIM ** (-0.5)
    rows = stop - start
    query_index = start + lax.broadcasted_iota(jnp.int32, (rows, stop), 0)
    key_index = lax.broadcasted_iota(jnp.int32, (rows, stop), 1)
    allowed = (key_index <= query_index) & (seg_col == seg_row)
    scores = jnp.where(allowed, scores, MASKED)
    exponent = jnp.exp(scores - jnp.max(scores, axis=1, keepdims=True))
    return exponent / jnp.sum(exponent, axis=1, keepdims=True)


def attend_kernel(block, query_ref, key_ref, value_ref, seg_col_ref, seg_row_ref, all_ref, out_ref, last_ref):
    last = pl.program_id(0) == pl.num_programs(0) - 1
    for start in range(0, query_ref.shape[0], block):
        stop = start + block
        probs = block_probs(
            query_ref[start:stop], key_ref[:stop], seg_col_ref[start:stop], seg_row_ref[:, :stop], start, stop
        )
        out = dot(probs.astype(BF16), value_ref[:stop], 1, 0).astype(BF16)
        all_ref[start:stop] = out

        @pl.when(last)
        def _():
            last_ref[start:stop] = out

        @pl.when(jnp.logical_not(last))
        def _():
            out_ref[start:stop] = out


def attend(query, key, value, seg_col, seg_row):
    seq_len, width = query.shape
    heads = width // HEAD_DIM
    head = pl.BlockSpec((seq_len, HEAD_DIM), lambda h: (0, h))
    shared = whole((seq_len, HEAD_DIM))
    return pl.pallas_call(
        functools.partial(attend_kernel, 256),
        grid=(width // HEAD_DIM,),
        in_specs=[head, shared, shared, whole((seq_len, 1)), whole((1, seq_len))],
        out_specs=[head, pl.BlockSpec((seq_len, HEAD_DIM), lambda h: (0, jnp.minimum(h, heads - 2))), shared],
        out_shape=[
            jax.ShapeDtypeStruct((seq_len, width), BF16),
            jax.ShapeDtypeStruct((seq_len, width - HEAD_DIM), BF16),
            jax.ShapeDtypeStruct((seq_len, HEAD_DIM), BF16),
        ],
        compiler_params=params("arbitrary"),
        cost_estimate=cost(12 * seq_len * seq_len * width, 8 * seq_len * width),
        name="attend",
    )(query, key, value, seg_col, seg_row)


def attend_back_kernel(
    block, table, query_ref, key_ref, value_ref, seg_col_ref, seg_row_ref, own_ref, far_ref, near_ref, far_near_ref,
    weight_ref, far_top_ref, far_bottom_ref, cosine_ref, sine_ref, *refs
):
    sent_ref, key_value_ref = refs
    head = pl.ds(pl.multiple_of(pl.program_id(0) * HEAD_DIM, HEAD_DIM), HEAD_DIM)
    width = sent_ref.shape[1] - 2 * HEAD_DIM
    scaling = HEAD_DIM ** (-0.5)
    own_rows = own_ref.shape[0]
    far_weight = jnp.where(table[COL] == 0, far_top_ref[...], far_bottom_ref[...])

    @pl.when(pl.program_id(0) == 0)
    def _():
        key_value_ref[...] = jnp.zeros_like(key_value_ref)

    for start in range(0, query_ref.shape[0], block):
        stop = start + block
        mine = table[ROW] == start // own_rows
        place = slice(start % own_rows, start % own_rows + block)
        grad = (
            dot(jnp.where(mine, own_ref[place], near_ref[place]), weight_ref[...], 1, 1)
            + dot(jnp.where(mine, far_ref[place], far_near_ref[place]), far_weight, 1, 1)
        ).astype(BF16)
        query = query_ref[start:stop]
        key, value = key_ref[:stop], value_ref[:stop]
        probs = block_probs(
            query, key, seg_col_ref[start:stop], seg_row_ref[:, :stop], start, stop
        )
        d_probs = dot(grad, value, 1, 1)
        d_scores = probs * (d_probs - jnp.sum(d_probs * probs, axis=1, keepdims=True))
        d_scores = d_scores.astype(BF16)
        d_query = dot(d_scores, key, 1, 0) * scaling
        turned = pltpu.roll(d_query * sine_ref[start:stop], HEAD_DIM // 2, 1)
        sent_ref[start:stop, head] = (d_query * cosine_ref[start:stop] + turned).astype(BF16)
        key_value_ref[:stop, :HEAD_DIM] += dot(d_scores, query, 0, 0) * scaling
        key_value_ref[:stop, HEAD_DIM:] += dot(probs.astype(BF16), grad, 0, 0)

    @pl.when(pl.program_id(0) == pl.num_programs(0) - 1)
    def _():
        d_key = key_value_ref[:, :HEAD_DIM]
        turned = pltpu.roll(d_key * sine_ref[...], HEAD_DIM // 2, 1)
        key_value_ref[:, :HEAD_DIM] = d_key * cosine_ref[...] + turned
        sent_ref[:, width:] = key_value_ref[...].astype(BF16)


def attend_back(table, query, key, value, seg_col, seg_row, d_hidden, weight, far_weights, cosine, sine):
    seq_len, width = query.shape
    features = weight.shape[1]
    heads = width // HEAD_DIM
    head = pl.BlockSpec((seq_len, HEAD_DIM), lambda h, t: (0, h))
    rows = pl.BlockSpec((HEAD_DIM, features), lambda h, t: (heads * t[COL] + h, 0))
    far_rows = pl.BlockSpec((HEAD_DIM, features), lambda h, t: (h, 0))
    shared = whole((seq_len, HEAD_DIM))
    key_value = whole((seq_len, 2 * HEAD_DIM))
    return pl.pallas_call(
        functools.partial(attend_back_kernel, 256),
        grid_spec=pltpu.PrefetchScalarGridSpec(
            num_scalar_prefetch=1,
            grid=(heads,),
            in_specs=[
                head, shared, shared, whole((seq_len, 1)), whole((1, seq_len)),
                *[whole(part.shape) for part in d_hidden], rows, far_rows, far_rows, shared, shared,
            ],
            out_specs=[whole((seq_len, width + 2 * HEAD_DIM)), key_value],
        ),
        out_shape=[
            jax.ShapeDtypeStruct((seq_len, width + 2 * HEAD_DIM), BF16),
            jax.ShapeDtypeStruct((seq_len, 2 * HEAD_DIM), F32),
        ],
        compiler_params=params("arbitrary"),
        cost_estimate=cost(24 * seq_len * seq_len * width, 12 * seq_len * width),
        name="attend_back",
    )(table, query, key, value, seg_col, seg_row, *d_hidden, weight, *far_weights, cosine, sine)


def residual_kernel(table, stream_ref, *refs):
    pieces, weights, (gain_ref, hidden_ref, normed_ref, scale_ref, group_ref) = refs[:6], refs[6:12], refs[12:]
    first = table[COL] == 0
    own, near = pieces[0][...], pieces[1][...]
    far, near_far = (
        jnp.concatenate([pieces[index][...], pieces[index + 1][...]], axis=1) for index in (2, 4)
    )
    part = own.shape[1]
    group = [jnp.where(first, own, far), jnp.where(first, far, own)]
    other = [jnp.where(first, near, near_far), jnp.where(first, near_far, near)]
    group_ref[:, :part] = group[0]
    group_ref[:, part:] = group[1]
    own_w, near_w, *far_w = weights
    width = own_w.shape[1]
    halves = []
    for index in range(2):
        total = stream_ref[:, index * width : (index + 1) * width].astype(F32)
        for place in range(2):
            rows = slice(place * part, (place + 1) * part)
            mine, theirs = (own_w[rows], near_w[rows]) if index == 0 else (far_w[place][...], far_w[2 + place][...])
            total = total + dot(group[place], mine, 1, 0)
            total = total + dot(other[place], theirs, 1, 0)
        halves.append(total)
    squares = sum(jnp.sum(total * total, axis=1, keepdims=True) for total in halves)
    scale = lax.rsqrt(squares / (2 * width) + EPSILON)
    scale_ref[...] = jnp.broadcast_to(scale, scale_ref.shape)
    for index, total in enumerate(halves):
        columns = slice(index * width, (index + 1) * width)
        hidden_ref[:, columns] = total
        normed_ref[:, columns] = (total * scale * gain_ref[:, columns]).astype(BF16)


def residual(table, stream, attended, own_weight, near_weight, far_weights, near_far_weights, gain):
    seq_len, width = stream.shape
    pieces = attended
    part = attended[0].shape[1]
    weights = [own_weight, near_weight, *far_weights, *near_far_weights]
    block = min(256, seq_len)

    def tokens(columns):
        return pl.BlockSpec((block, columns), lambda i, t: (i, 0))

    return pl.pallas_call(
        residual_kernel,
        grid_spec=pltpu.PrefetchScalarGridSpec(
            num_scalar_prefetch=1,
            grid=(seq_len // block,),
            in_specs=[tokens(width)]
            + [tokens(piece.shape[1]) for piece in pieces]
            + [whole(weight.shape) for weight in weights]
            + [whole((1, width))],
            out_specs=[tokens(width), tokens(width), tokens(128), tokens(2 * part)],
        ),
        out_shape=[
            jax.ShapeDtypeStruct((seq_len, width), F32),
            jax.ShapeDtypeStruct((seq_len, width), BF16),
            jax.ShapeDtypeStruct((seq_len, 128), F32),
            jax.ShapeDtypeStruct((seq_len, 2 * part), BF16),
        ],
        compiler_params=params("arbitrary"),
        cost_estimate=cost(2 * seq_len * width * width, 14 * seq_len * width),
        name="residual",
    )(table, stream, *pieces, *weights, gain)


def activate_kernel(width, table, normed_ref, own_gate_ref, own_up_ref, *refs):
    (act_ref, gate_factor_ref, up_factor_ref), refs = refs[-3:], refs[:-3]
    gate_parts, up_parts = refs[: len(refs) // 2], refs[len(refs) // 2 :]
    left, right = normed_ref[:, :width], normed_ref[:, width:]
    gate = dot(left, own_gate_ref[...], 1, 0) + dot(right, ordered(table, gate_parts), 1, 0)
    up = dot(left, own_up_ref[...], 1, 0) + dot(right, ordered(table, up_parts), 1, 0)
    sigmoid = jax.nn.sigmoid(gate)
    silu = gate * sigmoid
    act_ref[...] = (silu * up).astype(BF16)
    gate_factor_ref[...] = (up * (sigmoid * (1.0 + gate * (1.0 - sigmoid)))).astype(BF16)
    up_factor_ref[...] = silu.astype(BF16)


def tile_of(units, most=384):
    return next(t for t in (768, 512, 384, 256, 128, units) if units % t == 0 and (t <= most or t == units))


def activate(table, normed, own, far_parts):
    seq_len, width = normed.shape
    units = own.shape[1] // 2
    tile = tile_of(units)
    steps = units // tile

    def gate(rows):
        return pl.BlockSpec((rows, tile), lambda j, t: (0, j))

    def up(rows):
        return pl.BlockSpec((rows, tile), lambda j, t: (0, steps + j))

    rows = far_parts[0].shape[0]
    out = pl.BlockSpec((seq_len, tile), lambda j, t: (0, j))
    return pl.pallas_call(
        functools.partial(activate_kernel, width // 2),
        grid_spec=pltpu.PrefetchScalarGridSpec(
            num_scalar_prefetch=1,
            grid=(steps,),
            in_specs=[whole(normed.shape), gate(width // 2), up(width // 2)]
            + [gate(rows)] * len(far_parts)
            + [up(rows)] * len(far_parts),
            out_specs=[out] * 3,
        ),
        out_shape=[jax.ShapeDtypeStruct((seq_len, units), BF16)] * 3,
        compiler_params=params("arbitrary"),
        cost_estimate=cost(4 * seq_len * width * units, 6 * seq_len * units + 4 * width * units),
        name="activate",
    )(table, normed, own, own, *far_parts, *far_parts)


def activate_back_kernel(tile, width, table, grad_ref, own_ref, *refs):
    (gate_factor_ref, up_factor_ref, d_gate_ref, d_up_ref, far_scr), part_refs = refs[-5:], refs[:-5]

    @pl.when(pl.program_id(0) == 0)
    def _():
        far_scr[...] = ordered(table, part_refs)

    far = far_scr[pl.ds(pl.multiple_of(pl.program_id(0) * tile, tile), tile)]
    d_act = dot(grad_ref[:, :width], own_ref[...], 1, 1) + dot(grad_ref[:, width:], far, 1, 1)
    d_gate_ref[...] = (d_act * gate_factor_ref[...].astype(F32)).astype(BF16)
    d_up_ref[...] = (d_act * up_factor_ref[...].astype(F32)).astype(BF16)


def activate_back(table, grad, own, far_parts, gate_factor, up_factor):
    seq_len, width = grad.shape
    units = own.shape[0]
    tile = tile_of(units)
    out = pl.BlockSpec((seq_len, tile), lambda j, t: (0, j))
    return pl.pallas_call(
        functools.partial(activate_back_kernel, tile, width // 2),
        grid_spec=pltpu.PrefetchScalarGridSpec(
            num_scalar_prefetch=1,
            grid=(units // tile,),
            in_specs=[whole(grad.shape), pl.BlockSpec((tile, width // 2), lambda j, t: (j, 0))]
            + [whole(piece.shape) for piece in far_parts]
            + [out, out],
            out_specs=[out] * 2,
            scratch_shapes=[pltpu.VMEM((units, width // 2), BF16)],
        ),
        out_shape=[jax.ShapeDtypeStruct((seq_len, units), BF16)] * 2,
        compiler_params=params("arbitrary"),
        cost_estimate=cost(2 * seq_len * width * units, 8 * seq_len * units + 2 * width * units),
        name="activate_back",
    )(table, grad, own, *far_parts, gate_factor, up_factor)


def down_kernel(counts, table, *refs):
    halves = len(counts)
    act_refs, own_refs, refs = refs[:halves], refs[halves : 2 * halves], refs[2 * halves :]
    own_out_ref, *other_refs, total_scr = refs[-4:]
    part_refs = []
    for parts in counts:
        part_refs.append(refs[:parts])
        refs = refs[parts:]

    def write(weights, other_ref):
        total_scr[...] = sum(dot(act_ref[...], weight, 1, 0) for act_ref, weight in zip(act_refs, weights))
        rows = own_out_ref.shape[0]
        own_out_ref[...] = total_scr[pl.ds(pl.multiple_of(table[ROW] * rows, rows), rows)]
        other = pl.multiple_of((1 - table[ROW]) * rows, rows)
        other_ref[...] = total_scr[pl.ds(other, rows)].astype(BF16)

    @pl.when(pl.program_id(0) == 0)
    def _():
        write([own_ref[...] for own_ref in own_refs], other_refs[0])

    @pl.when(pl.program_id(0) == 1)
    def _():
        write([ordered(table, parts) for parts in part_refs], other_refs[1])


def down(table, acts, own, far_parts):
    seq_len = acts[0].shape[0]
    features = own[0].shape[1]
    units = sum(part.shape[0] for part in own)
    arrays = (*acts, *own, *[piece for parts in far_parts for piece in parts])
    return pl.pallas_call(
        functools.partial(down_kernel, [len(parts) for parts in far_parts]),
        grid_spec=pltpu.PrefetchScalarGridSpec(
            num_scalar_prefetch=1,
            grid=(2,),
            in_specs=[whole(array.shape) for array in arrays],
            out_specs=[pl.BlockSpec((seq_len // 2, features), lambda j, t: (0, j))]
            + [whole((seq_len // 2, features))] * 2,
            scratch_shapes=[pltpu.VMEM((seq_len, features), F32)],
        ),
        out_shape=[
            jax.ShapeDtypeStruct((seq_len // 2, 2 * features), F32),
            *[jax.ShapeDtypeStruct((seq_len // 2, features), BF16)] * 2,
        ],
        compiler_params=params("arbitrary"),
        cost_estimate=cost(4 * seq_len * units * features, 8 * seq_len * features + 8 * units * (seq_len + features)),
        name="down",
    )(table, *arrays)


def split_product(table, left, rights, tile, groups, count, bits, merge=False):
    seq_len, height = left.shape
    rows = height // (groups * count)
    place = [(0, group) if merge else (group, 0) for group in range(groups)]
    outs, depth = (1, groups * count // 2) if merge else (groups, count // 2)
    firsts = [first for _, first, _ in rights]
    steps = [length for _, _, length in rights]
    rights = [right for right, _, _ in rights]
    columns = sum(steps) * tile
    starts = [sum(steps[:index]) for index in range(len(rights))]

    def kernel(table, left_ref, *refs):
        right_refs, out_refs, total_scr = refs[: len(rights)], refs[len(rights) : -1], refs[-1]
        step = pl.program_id(0)
        for right_ref, start, length in zip(right_refs, starts, steps):

            @pl.when((step >= start) & (step < start + length))
            def _():
                total_scr[...] = dot(left_ref[...], right_ref[...], 0, 0)

        for group, bit in enumerate(bits):
            side = table[BITS + bit]
            sent_ref, kept_ref = out_refs[2 * place[group][0] : 2 * place[group][0] + 2]
            for out_ref, value in ((sent_ref, 1 - side), (kept_ref, side)):
                for index in range(count // 2):
                    begin = (group * count + with_bit(index, bit, value)) * rows
                    if rows % 8 == 0:
                        begin = pl.multiple_of(begin, 8)
                    out_ref[place[group][1] * (count // 2) + index] = total_scr[pl.ds(begin, rows)].astype(BF16)

    def right_spec(first, start, length):
        return pl.BlockSpec((seq_len, tile), lambda i, t: (0, first + jnp.clip(i - start, 0, length - 1)))

    return pl.pallas_call(
        kernel,
        grid_spec=pltpu.PrefetchScalarGridSpec(
            num_scalar_prefetch=1,
            grid=(sum(steps),),
            in_specs=[whole(left.shape)]
            + [right_spec(*place) for place in zip(firsts, starts, steps)],
            out_specs=[pl.BlockSpec((depth, rows, tile), lambda i, t: (0, 0, i))] * (2 * outs),
            scratch_shapes=[pltpu.VMEM((height, tile), F32)],
        ),
        out_shape=[jax.ShapeDtypeStruct((depth, rows, columns), BF16)] * (2 * outs),
        compiler_params=params("arbitrary"),
        cost_estimate=cost(
            2 * seq_len * height * columns, 2 * (seq_len * (height + columns) + height * columns)
        ),
        name="split_product",
    )(table, left, *rights)


def relay_kernel(table, kept_sent_ref, arrived_sent_ref, kept_ref, arrived_ref, sent_out_ref, kept_out_ref):
    sent_out_ref[...] = (kept_sent_ref[...].astype(F32) + arrived_sent_ref[...].astype(F32)).astype(BF16)
    kept_out_ref[...] = (kept_ref[...].astype(F32) + arrived_ref[...].astype(F32)).astype(BF16)


def relay(table, kept, arrived, place, bit):
    count, rows, columns = kept.shape

    def block(sent):
        def index(i, t):
            value = t[BITS + bit]
            return (with_bit(i, place, 1 - value if sent else value), 0, 0)

        return pl.BlockSpec((1, rows, columns), index)

    out = pl.BlockSpec((1, rows, columns), lambda i, t: (i, 0, 0))
    return pl.pallas_call(
        relay_kernel,
        grid_spec=pltpu.PrefetchScalarGridSpec(
            num_scalar_prefetch=1,
            grid=(count // 2,),
            in_specs=[block(True), block(True), block(False), block(False)],
            out_specs=[out, out],
        ),
        out_shape=[jax.ShapeDtypeStruct((count // 2, rows, columns), BF16)] * 2,
        compiler_params=params("arbitrary"),
        cost_estimate=cost(0, 6 * count * rows * columns),
        name="relay",
    )(table, kept, arrived, kept, arrived)


def normed_grad_kernel(halves, steps, tile, counts, table, *refs):
    d_refs, own_refs, refs = refs[: 2 * halves], refs[2 * halves : 3 * halves], refs[3 * halves :]
    part_refs = []
    for parts in counts:
        part_refs.append(refs[:parts])
        refs = refs[parts:]
    own_out_ref, other_refs, far_scrs, total_scr = refs[0], refs[1:3], refs[3:-1], refs[-1]

    @pl.when(pl.program_id(0) == 0)
    def _():
        for half in range(halves):
            far_scrs[half][...] = ordered(table, part_refs[half])

    def write(weights):
        total = None
        for half in range(halves):
            units = d_refs[2 * half].shape[1]
            for kind in range(2):
                term = dot(
                    d_refs[2 * half + kind][...], weights[half][:, kind * units : (kind + 1) * units], 1, 1
                )
                total = term if total is None else total + term
        total_scr[...] = total
        rows = own_out_ref.shape[0]
        own_out_ref[...] = total_scr[pl.ds(pl.multiple_of(table[ROW] * rows, rows), rows)]
        other = pl.multiple_of((1 - table[ROW]) * rows, rows)
        for index, other_ref in enumerate(other_refs):

            @pl.when(pl.program_id(0) // steps == index)
            def _():
                other_ref[...] = total_scr[pl.ds(other, rows)].astype(BF16)

    @pl.when(pl.program_id(0) < steps)
    def _():
        write(own_refs)

    @pl.when(pl.program_id(0) >= steps)
    def _():
        start = pl.multiple_of((pl.program_id(0) - steps) * tile, tile)
        write([scr.at[pl.ds(start, tile)] for scr in far_scrs])


def normed_grad(table, d_parts, own, far_parts):
    seq_len = d_parts[0].shape[0]
    units = [part.shape[1] for part in d_parts[::2]]
    features = own[0].shape[0]
    tile = 256
    steps = features // tile
    halves = len(own)
    parts = [piece for half in far_parts for piece in half]

    def side(index):
        return pl.BlockSpec(
            (seq_len // 2, tile), lambda j, t: (0, jnp.clip(j - steps * index, 0, steps - 1))
        )

    own_specs = [
        pl.BlockSpec((tile, 2 * wide), lambda j, t: (jnp.minimum(j, steps - 1), 0)) for wide in units
    ]
    return pl.pallas_call(
        functools.partial(normed_grad_kernel, halves, steps, tile, [len(half) for half in far_parts]),
        grid_spec=pltpu.PrefetchScalarGridSpec(
            num_scalar_prefetch=1,
            grid=(2 * steps,),
            in_specs=[whole(part.shape) for part in d_parts]
            + own_specs
            + [whole(piece.shape) for piece in parts],
            out_specs=[pl.BlockSpec((seq_len // 2, tile), lambda j, t: (0, j))]
            + [side(index) for index in range(2)],
            scratch_shapes=[pltpu.VMEM((features, 2 * wide), BF16) for wide in units]
            + [pltpu.VMEM((seq_len, tile), F32)],
        ),
        out_shape=[
            jax.ShapeDtypeStruct((seq_len // 2, 2 * features), F32),
            *[jax.ShapeDtypeStruct((seq_len // 2, features), BF16)] * 2,
        ],
        compiler_params=params("arbitrary"),
        cost_estimate=cost(
            8 * seq_len * features * sum(units), 8 * sum(units) * (seq_len + features)
        ),
        name="normed_grad",
    )(table, *d_parts, *own, *parts)


def chip_sum_kernel(own_ref, *refs):
    near_refs, (out_ref, *low_refs) = refs[:-3], refs[-3:]
    width = low_refs[0].shape[1]
    start = 0
    for near_ref in near_refs:
        columns = slice(start, start + near_ref.shape[1])
        total = own_ref[:, columns] + near_ref[...].astype(F32)
        out_ref[:, columns] = total
        start += near_ref.shape[1]
    for index, low_ref in enumerate(low_refs):
        low_ref[...] = out_ref[:, index * width : (index + 1) * width].astype(BF16)


def chip_sum(own, nears):
    rows, width = own.shape
    block = pl.BlockSpec((rows // 4, width), lambda i: (i, 0))
    return pl.pallas_call(
        chip_sum_kernel,
        grid=(4,),
        in_specs=[block] + [pl.BlockSpec((rows // 4, near.shape[1]), lambda i: (i, 0)) for near in nears],
        out_specs=[block] + [pl.BlockSpec((rows // 4, width // 2), lambda i: (i, 0))] * 2,
        out_shape=[jax.ShapeDtypeStruct(own.shape, F32)]
        + [jax.ShapeDtypeStruct((rows, width // 2), BF16)] * 2,
        compiler_params=params("arbitrary"),
        cost_estimate=cost(0, 12 * rows * width),
        name="chip_sum",
    )(own, *nears)


def norm_back_kernel(
    width, table, chip_ref, far_own_ref, far_other_ref, hidden_ref, scale_ref, grad_ref, gain_ref, out_ref, low0_ref, low1_ref, gain_grad_ref
):
    @pl.when(pl.program_id(0) == 0)
    def _():
        gain_grad_ref[...] = jnp.zeros_like(gain_grad_ref)

    d_left = chip_ref[:, :width] + far_other_ref[...].astype(F32)
    d_right = chip_ref[:, width:] + far_own_ref[...].astype(F32)
    left, right = hidden_ref[:, :width], hidden_ref[:, width:]
    scale = scale_ref[:, :1]
    gain_grad_ref[...] += jnp.sum(d_left * left * scale, axis=0, keepdims=True)
    left_weighted, right_weighted = d_left * gain_ref[:, :width], d_right * gain_ref[:, width:]
    inner = jnp.sum(left_weighted * left, axis=1, keepdims=True) + jnp.sum(
        right_weighted * right, axis=1, keepdims=True
    )
    factor = scale * scale * (inner / (2 * width))
    d_left = grad_ref[:, :width].astype(F32) + scale * (left_weighted - left * factor)
    d_right = grad_ref[:, width:].astype(F32) + scale * (right_weighted - right * factor)
    out_ref[...] = d_left
    low0_ref[...] = d_left.astype(BF16)
    low1_ref[...] = d_right.astype(BF16)


def norm_back(table, chip, far, hidden, scale, grad, gain):
    rows, width = chip.shape
    block = rows // 4

    def own(columns):
        return pl.BlockSpec((block, columns), lambda i, t: (i, 0))

    def tokens(columns):
        return pl.BlockSpec((block, columns), lambda i, t: (4 * t[ROW] + i, 0))

    return pl.pallas_call(
        functools.partial(norm_back_kernel, width // 2),
        grid_spec=pltpu.PrefetchScalarGridSpec(
            num_scalar_prefetch=1,
            grid=(4,),
            in_specs=[own(width), own(width // 2), own(width // 2), tokens(width), tokens(128), tokens(width), whole((1, width))],
            out_specs=[own(width // 2)] * 3 + [whole((1, width // 2))],
        ),
        out_shape=[
            jax.ShapeDtypeStruct((rows, width // 2), F32),
            jax.ShapeDtypeStruct((rows, width // 2), BF16),
            jax.ShapeDtypeStruct((rows, width // 2), BF16),
            jax.ShapeDtypeStruct((1, width // 2), F32),
        ],
        compiler_params=params("arbitrary"),
        cost_estimate=cost(0, 20 * rows * width),
        name="norm_back",
    )(table, chip, *far, hidden, scale, grad, gain)


def project_back_kernel(
    count, bit, table, query_ref, key_value_ref, arrived_ref, normed_ref, weight_ref, group_ref,
    d_hidden_ref, d_hidden_near_ref, sent_ref, kept_ref, own_ref, other_ref, bias_ref, d_scr, total_scr, hidden_scr, out_scr,
):
    first = table[COL] == 0
    query_width = query_ref.shape[1] - 2 * HEAD_DIM
    own, far = query_ref[:, :query_width], arrived_ref[:, :query_width]
    d_scr[:, :query_width] = jnp.where(first, own, far)
    d_scr[:, query_width : 2 * query_width] = jnp.where(first, far, own)
    d_key_value = key_value_ref[...] + arrived_ref[:, query_width:].astype(F32)
    d_scr[:, 2 * query_width :] = d_key_value.astype(BF16)
    d_projected = d_scr[...]
    bias_ref[...] = jnp.sum(d_projected.astype(F32), axis=0, keepdims=True)
    total_scr[...] = dot(normed_ref[...], d_projected, 0, 0)
    tokens = own_ref.shape[0]
    hidden_scr[:tokens] = jnp.where(table[ROW] == 0, d_hidden_ref[...], d_hidden_near_ref[...])
    hidden_scr[tokens:] = jnp.where(table[ROW] == 0, d_hidden_near_ref[...], d_hidden_ref[...])
    out_scr[...] = dot(group_ref[...], hidden_scr[...], 0, 0)
    rows = sent_ref.shape[1]
    width = total_scr.shape[1]
    side = table[BITS + bit]
    for out_ref, value in ((sent_ref, 1 - side), (kept_ref, side)):
        for index in range(count // 2):
            start = with_bit(index, bit, value) * rows
            if rows % 8 == 0:
                start = pl.multiple_of(start, 8)
            out_ref[index, :, :width] = total_scr[pl.ds(start, rows)].astype(BF16)
            out_ref[index, :, width:] = out_scr[pl.ds(start, rows)].astype(BF16)
    for out_ref, half in ((own_ref, table[ROW]), (other_ref, 1 - table[ROW])):
        d_half = d_scr[pl.ds(pl.multiple_of(half * tokens, tokens), tokens)]
        out_ref[...] = dot(d_half, weight_ref[...], 1, 1).astype(out_ref.dtype)


def project_back(table, d_query, d_key_value, arrived, normed, weight, group, d_hidden, near, count, bit):
    seq_len = d_query.shape[0]
    width, columns = weight.shape
    rows = width // count
    arrays = (d_query, d_key_value, arrived, normed, weight, group, d_hidden, near)
    terms = (count // 2, rows, columns + d_hidden.shape[1])
    return pl.pallas_call(
        functools.partial(project_back_kernel, count, bit),
        grid_spec=pltpu.PrefetchScalarGridSpec(
            num_scalar_prefetch=1,
            grid=(1,),
            in_specs=[whole(array.shape) for array in arrays],
            out_specs=[
                whole(terms), whole(terms), whole((seq_len // 2, width)), whole((seq_len // 2, width)),
                whole((1, columns)),
            ],
            scratch_shapes=[
                pltpu.VMEM((seq_len, columns), BF16), pltpu.VMEM((width, columns), F32),
                pltpu.VMEM((seq_len, d_hidden.shape[1]), BF16), pltpu.VMEM((width, d_hidden.shape[1]), F32),
            ],
        ),
        out_shape=[
            jax.ShapeDtypeStruct(terms, BF16),
            jax.ShapeDtypeStruct(terms, BF16),
            jax.ShapeDtypeStruct((seq_len // 2, width), F32),
            jax.ShapeDtypeStruct((seq_len // 2, width), BF16),
            jax.ShapeDtypeStruct((1, columns), F32),
        ],
        compiler_params=params("arbitrary"),
        cost_estimate=cost(4 * seq_len * width * columns, 8 * seq_len * columns),
        name="project_back",
    )(table, *arrays)


def swap(part, axis_name):
    return lax.ppermute(part, axis_name, [(0, 1), (1, 0)])


def dp_swap(part, bit):
    count = lax.axis_size("dp")
    return lax.ppermute(part, "dp", [(i, i ^ (1 << bit)) for i in range(count)])


def after(value, *earlier):
    return lax.optimization_barrier((value,) + earlier)[0]


def pick(array, index, axis):
    return lax.dynamic_index_in_dim(array, index, axis, keepdims=False)


def in_order(index, own, other, axis):
    first = jnp.where(index == 0, own, other)
    second = jnp.where(index == 0, other, own)
    return jnp.concatenate([first, second], axis=axis)


def quad_slots(rank):
    low, high = rank % 2, rank // 2 % 2
    return jnp.stack([2 * high + low, 4 + 2 * low + high])


class Line:
    def __init__(self):
        self.last = ()

    def step(self, value):
        return after(value, *self.last) if self.last else value

    def mark(self, *values):
        self.last = values


class Quad:
    def __init__(self, part, rank):
        self.part = part
        self.low, self.high = rank % 2, rank // 2 % 2

    def first_round(self, line):
        if isinstance(self.part, list):
            self.sent = [line.step(slot) for slot in self.part]
        else:
            part = line.step(self.part)
            self.sent = lax.optimization_barrier([part[0], part[1]])
        line.mark(*self.sent)
        self.arriving = dp_swap(self.sent[0], 0), dp_swap(self.sent[1], 1)

    def second_round(self, line):
        arrived = [line.step(value) for value in self.arriving]
        pairs = lax.optimization_barrier(
            (in_order(self.low, self.sent[0], arrived[0], 0), in_order(self.high, self.sent[1], arrived[1], 0))
        )
        line.mark(*pairs)
        self.parts = [*pairs, dp_swap(pairs[0], 1), dp_swap(pairs[1], 0)]
        return self.parts


def laid_out(parts, rank):
    low, high = rank % 2, rank // 2 % 2
    return [in_order(high, parts[0], parts[2], 0), in_order(low, parts[1], parts[3], 0)]


class Scatter:
    def __init__(self, table, sent, kept, order, line):
        self.table, self.kept = table, kept
        bits = lax.axis_size("dp").bit_length() - 1
        self.order = list(order) + [bit for bit in range(bits) if bit not in order]
        self.left = list(range(bits))
        self.pass_on(sent, line)

    def pass_on(self, sent, line):
        bit = self.order.pop(0)
        self.left.remove(bit)
        self.arriving = dp_swap(line.step(sent), bit)

    def relay(self, line):
        bit = self.order[0]
        sent, self.kept = relay(
            self.table, self.kept, line.step(self.arriving), self.left.index(bit), bit
        )
        line.mark(sent)
        self.pass_on(sent, line)

    def finish(self, line):
        while self.order:
            self.relay(line)
        total = self.kept.astype(F32) + line.step(self.arriving).astype(F32)
        total = lax.optimization_barrier(total)
        line.mark(total)
        return total


def shards(
    block_input,
    segment_ids,
    first_gain,
    qkv_weight,
    qkv_bias,
    output_weight,
    second_gain,
    gate_up_weight,
    down_weight,
    output_grad,
):
    count = lax.axis_size("dp")
    rank = lax.axis_index("dp")
    row = lax.axis_index("row")
    col = lax.axis_index("col")
    qkv_block = qkv_weight[0, 0]
    out_block = output_weight[0, 0]
    gate_up_block = gate_up_weight[0, 0]
    down_block = down_weight[0, 0]
    seq_len = segment_ids.shape[0]
    own_rows, half_width = block_input.shape
    model_width = 2 * half_width
    query_width = HEADS // 4 * HEAD_DIM
    own_units = down_block.shape[0] // 2
    segment = own_units // count
    step = max(16, 128 // count)
    padded = pl.cdiv(segment, 3 * step) * 3 * step
    feature_rows = half_width // count
    slot_rows = half_width // 8
    slots = quad_slots(rank)
    bits = count.bit_length() - 1

    def own_tokens(array):
        return lax.dynamic_slice_in_dim(array, row * own_rows, own_rows, 0)

    def slot_pair(array):
        parts = array.reshape((8, array.shape[0] // 8) + array.shape[1:])
        return [pick(parts, slot, 0) for slot in slots]

    def swap_pair(pair):
        return [swap(slot, "col") for slot in pair]

    table = jnp.stack([row, col] + [(rank >> bit) & 1 for bit in range(bits)]).astype(jnp.int32)
    line = Line()
    pair_first, line_first = [0, 1, 2], [1, 0, 2]

    def qkv_columns(side):
        heads = lax.dynamic_slice_in_dim(qkv_block, side * query_width, query_width, 1)
        return jnp.concatenate([heads, qkv_block[:, 2 * query_width :]], axis=1)

    gains = jnp.stack([first_gain, second_gain])
    gains = jnp.concatenate([gains, swap(gains, "col")], axis=1)
    early_send = slot_pair(jnp.concatenate([qkv_columns(1 - col), out_block], axis=1))
    early_send = lax.optimization_barrier(early_send)
    early_quad = Quad(swap_pair(early_send), rank)
    qkv_own = qkv_columns(col)
    qkv_width = qkv_own.shape[1]
    bias = qkv_bias[0]
    bias_own = jnp.concatenate(
        [lax.dynamic_slice_in_dim(bias, col * query_width, query_width, 0), bias[2 * query_width :]]
    )

    (send,) = unit_columns(
        after(gate_up_block, *early_send, gains), 1 - col, slots, count, slot_rows, padded, ((0, 0),)
    )
    line.mark(send)

    near = swap(block_input, "row")
    out_near = swap(out_block, "row")
    far = swap(after(block_input, *early_send), "col")

    position_index = jnp.arange(seq_len, dtype=jnp.int32)
    doc_first = jnp.concatenate([jnp.ones((1,), jnp.bool_), segment_ids[1:] != segment_ids[:-1]])
    positions = position_index - lax.cummax(jnp.where(doc_first, position_index, 0), axis=0)
    frequency = ROPE_BASE ** (-jnp.arange(0, HEAD_DIM, 2, dtype=F32) / HEAD_DIM)
    angles = positions.astype(F32)[:, None] * frequency[None, :]
    cosine, sine = jnp.cos(angles), jnp.sin(angles)
    cosine = jnp.concatenate([cosine, cosine], axis=1)
    sine = jnp.concatenate([-sine, sine], axis=1)
    seg_col, seg_row = segment_ids[:, None], segment_ids[None, :]

    low_slots, high_slots = jnp.arange(4), 4 + jnp.arange(4)
    early_quad.first_round(line)
    gate_up_quad = Quad(swap(line.step(send), "col"), rank)
    outs = ((0, 0), (0, 1), (1, 1))
    gate_up_own = unit_columns(
        line.step(gate_up_block), col, low_slots, count, slot_rows, padded, outs, low_slots, 8
    )
    line.mark(*gate_up_own)
    early_far = early_quad.second_round(line)
    far_halves = lax.optimization_barrier((far[: own_rows // 2], far[own_rows // 2 :]))
    far_near = [swap(half, "row") for half in far_halves]
    gate_up_own = unit_columns(
        line.step(gate_up_block), col, high_slots, count, slot_rows, padded, outs, high_slots, 8, gate_up_own
    )
    line.mark(*gate_up_own)
    *gate_up_own, send = [part.reshape(half_width, -1) for part in gate_up_own]
    out_near = line.step(out_near)
    line.mark(out_near)
    stream, first_normed, first_scale, query, key, value = project(
        table, line.step(block_input), near, far, far_near, gains[:1], qkv_own, early_far,
        bias_own[None], cosine, sine,
    )
    line.mark(query)
    gate_up_quad.first_round(line)
    attended, *attended_parts = attend(line.step(query), key, value, seg_col, seg_row)
    line.mark(attended)
    attended_far = [swap(part, "col") for part in attended_parts]
    attended_near = swap(attended, "row")
    gate_up_far = [gate_up_quad.second_round(line)]
    out_far = lax.optimization_barrier(
        laid_out([line.step(part)[:, qkv_width:] for part in early_far], rank)
    )
    line.mark(*out_far)
    out_far_near = [swap(part, "row") for part in out_far]
    share = count // 8
    send_ranks = (slots[:, None] * share + jnp.arange(share)[None, :]).reshape(-1)
    (down_send,) = unit_rows(line.step(down_block), 1 - col, send_ranks, count, padded, (0,))
    line.mark(down_send)
    down_own = unit_rows(line.step(down_block), col, jnp.arange(count), count, padded)
    line.mark(*down_own)
    down_own = [part.reshape(-1, half_width) for part in down_own]
    attended_far = [line.step(part) for part in attended_far]
    line.mark(*attended_far)
    attended_far_near = [swap(part, "row") for part in attended_far]
    down_quad = Quad(swap(line.step(down_send).reshape(2, -1, half_width), "col"), rank)
    grad_far = swap(line.step(output_grad), "col")
    hidden_one, second_normed, second_scale, attended_group = residual(
        table, line.step(stream), [attended, attended_near, *attended_far, *attended_far_near],
        out_block, out_near, out_far, out_far_near, gains[1:],
    )
    line.mark(second_normed)
    gate_up_far[0] = [line.step(part) for part in gate_up_far[0]]
    line.mark(*gate_up_far[0])
    down_quad.first_round(line)

    act0, gate_factor0, up_factor0 = activate(
        table, line.step(second_normed), gate_up_own[0], gate_up_far[0]
    )
    line.mark(act0)
    grad_far = line.step(grad_far)
    line.mark(grad_far)
    down_far = [down_quad.second_round(line)]
    grad_near = swap(line.step(output_grad), "row")
    grad_far_near = swap(grad_far, "row")
    gate_up_far.append([swap(line.step(send), "col")])
    grad_full = join(table, line.step(output_grad), grad_near, grad_far, grad_far_near)
    line.mark(grad_full)

    def down_terms(act, order):
        sent, kept = split_product(
            table, line.step(act), [(grad_full, 0, 2)], half_width, 1, count, [order[0]]
        )
        line.mark(sent)
        return sent, kept

    def gate_up_terms(d_gate, d_up, order, merge):
        tile = tile_of(d_gate.shape[1], 768)
        rights = [(part, 0, part.shape[1] // tile) for part in (d_gate, d_up)]
        terms = split_product(
            table, line.step(second_normed), rights, tile, 2, count, [order[0]] * 2, merge
        )
        line.mark(terms[0])
        return terms

    terms = down_terms(act0, pair_first)
    down_far[0] = [line.step(part) for part in down_far[0]]
    line.mark(*down_far[0])
    down_sum0 = Scatter(table, *terms, pair_first, line)
    begin, width, full = halves_of(segment, padded)[1]
    down_send = pick(line.step(down_block).reshape(count, 2, segment, half_width), 1 - col, 1)
    down_send = jnp.pad(down_send[:, begin : begin + width], ((0, 0), (0, full - width), (0, 0)))
    down_send = lax.optimization_barrier(down_send.reshape(-1, half_width))
    line.mark(down_send)
    down_far.append([swap(down_send, "col")])
    d_gate0, d_up0 = activate_back(
        table, line.step(grad_full), down_own[0], down_far[0], gate_factor0, up_factor0
    )
    line.mark(d_gate0)
    own_sent0, own_kept0, far_sent0, far_kept0 = gate_up_terms(d_gate0, d_up0, pair_first, False)
    far_sum0 = Scatter(table, far_sent0, far_kept0, pair_first, line)
    act1, gate_factor1, up_factor1 = activate(
        table, line.step(second_normed), gate_up_own[1], gate_up_far[1]
    )
    line.mark(act1)
    down_sum0.relay(line)
    down_far[1] = [line.step(down_far[1][0])]
    line.mark(*down_far[1])
    own_sum0 = Scatter(table, own_sent0, own_kept0, pair_first, line)
    d_gate1, d_up1 = activate_back(
        table, line.step(grad_full), down_own[1], down_far[1], gate_factor1, up_factor1
    )
    line.mark(d_gate1)
    d_second_own, *d_second_other = normed_grad(
        table, [line.step(d_gate0), d_up0, d_gate1, d_up1], gate_up_own, gate_up_far
    )
    line.mark(*d_second_other)
    d_second_near = [swap(part, "row") for part in d_second_other]
    down_terms1 = down_terms(act1, pair_first)
    down_sum0.relay(line)
    far_sum0.relay(line)
    d_second_chip, *d_second_low = chip_sum(line.step(d_second_own), d_second_near)
    line.mark(*d_second_low)
    d_second_far = [swap(part, "col") for part in d_second_low]
    gate_up_terms1 = gate_up_terms(d_gate1, d_up1, pair_first, True)
    mlp_own, mlp_other, mlp_other_far = down(table, [line.step(act0), act1], down_own, down_far)
    line.mark(mlp_other)
    far_sum0.relay(line)
    own_sum0.relay(line)
    down_sum0 = down_sum0.finish(line)[0]
    down_sum1 = Scatter(table, *down_terms1, pair_first, line)
    mlp_near = swap(line.step(mlp_other_far), "row")

    d_hidden, *d_hidden_low, second_gain_part = norm_back(
        table, line.step(d_second_chip), d_second_far, hidden_one, second_scale, grad_full, gains[1:]
    )
    line.mark(*d_hidden_low)
    d_hidden_near = [swap(part, "row") for part in d_hidden_low]
    mlp_sent = mlp_own[:, half_width:] + line.step(mlp_near).astype(F32)
    mlp_sent = lax.optimization_barrier(mlp_sent.astype(BF16))
    line.mark(mlp_sent)

    d_projected_sent, d_key_value = attend_back(
        table, line.step(query), key, value, seg_col, seg_row, [*d_hidden_low, *d_hidden_near], out_block, out_far,
        cosine, sine,
    )
    line.mark(d_projected_sent)
    arrived = swap(d_projected_sent, "col")
    down_sum1.relay(line)
    gate_up_sum1 = Scatter(table, *gate_up_terms1, pair_first, line)
    sent, kept, d_first_own, d_first_other, bias_part = project_back(
        table, line.step(d_projected_sent), d_key_value, arrived, first_normed, qkv_block, attended_group,
        d_hidden_low[0], d_hidden_near[0], count, 0,
    )
    line.mark(sent)
    heads_sum = Scatter(table, sent, kept, pair_first, line)
    d_first_near = swap(d_first_other, "row")
    own_sum0.relay(line)
    down_sum1.relay(line)
    far_sum0 = far_sum0.finish(line)[0]
    gate_up_sum1.relay(line)

    d_first = line.step(d_first_own) + d_first_near.astype(F32)
    stream_own = block_input.astype(F32)
    first_scale_own = own_tokens(first_scale)[:, :1]
    first_gain_part = jnp.sum(d_first * stream_own * first_scale_own, axis=0)
    weighted = d_first * first_gain
    inner = jnp.sum(weighted * stream_own, axis=1)
    inner = (inner + swap(inner, "col"))[:, None]
    input_grad = d_hidden + first_scale_own * (
        weighted - stream_own * (first_scale_own * first_scale_own) * (inner / model_width)
    )

    gain_parts = line.step(jnp.concatenate([first_gain_part, second_gain_part[0]]))
    gain_parts = lax.optimization_barrier(gain_parts + swap(gain_parts, "row"))
    line.mark(gain_parts)
    small = line.step(jnp.concatenate([gain_parts, bias_part[0]]))

    def dp_step(part, bit):
        part = lax.optimization_barrier(part + line.step(dp_swap(part, bit)))
        line.mark(part)
        return part

    heads_sum.relay(line)
    far_sum0 = swap(line.step(far_sum0.astype(BF16)), "col")
    down_sum0_far = swap(line.step(down_sum0[:, half_width:].astype(BF16)), "col")
    own_sum0 = own_sum0.finish(line)[0]
    down_sum1 = down_sum1.finish(line)[0]
    mlp_far = swap(line.step(mlp_sent), "col")
    down_sum1_far = swap(line.step(down_sum1[:, half_width:].astype(BF16)), "col")
    gate_up_sum1.relay(line)
    small = dp_step(small, 0)
    heads_sum.relay(line)
    hidden_own = own_tokens(hidden_one)[:, :half_width]
    mlp_near = swap(line.step(mlp_other), "row")
    mlp_chip = mlp_own[:, :half_width] + mlp_near.astype(F32)
    block_output = (hidden_own + (mlp_chip + line.step(mlp_far).astype(F32))).astype(BF16)
    small = dp_step(small, 1)
    own_sum1, far_sum1 = gate_up_sum1.finish(line)
    far_sum1 = swap(line.step(far_sum1.astype(BF16)), "col")
    far_sum1 = line.step(far_sum1)
    line.mark(far_sum1)
    for bit in range(2, bits):
        small = dp_step(small, bit)
    heads_sum = heads_sum.finish(line)[0]
    qkv_sum, out_sum = heads_sum[:, : bias.shape[0]], heads_sum[:, bias.shape[0] :]
    bias_width = bias.shape[0] // count
    bias_grad = lax.dynamic_slice_in_dim(small[model_width:], rank * bias_width, bias_width, 0)

    widths = [width for _, width, _ in halves_of(segment, padded)]
    own_rows_sum = [
        part[:width, :half_width] for part, width in zip((down_sum0, down_sum1), widths)
    ]
    far_rows_sum = [
        part[:width].astype(F32) for part, width in zip((down_sum0_far, down_sum1_far), widths)
    ]
    down_grad = in_order(
        col, jnp.concatenate(own_rows_sum, axis=0), jnp.concatenate(far_rows_sum, axis=0), 0
    )
    gate_up_grad = spread_columns(
        table, (own_sum0, own_sum1), (far_sum0, far_sum1), count, segment, padded
    )

    return (
        block_output,
        input_grad,
        small[:half_width],
        qkv_sum[None, None],
        bias_grad[None],
        out_sum[None, None],
        small[half_width:model_width],
        gate_up_grad[None, None],
        down_grad[None, None],
    )


def solution(mesh):
    placed = (
        P(("dp", "row"), "col"),
        P("dp"),
        P("col"),
        P("col", "row", None, None),
        P("row", None),
        P("row", "col", None, None),
        P("col"),
        P("col", "row", None, None),
        P("row", "col", None, None),
        P(("dp", "row"), "col"),
    )
    return jax.shard_map(
        shards,
        mesh=mesh,
        in_specs=placed,
        out_specs=(
            P(("dp", "row"), "col"),
            P(("dp", "row"), "col"),
            P("col"),
            P("col", "row", "dp", None),
            P("row", "dp"),
            P("row", "col", "dp", None),
            P("col"),
            P("col", "row", "dp", None),
            P("row", "col", "dp", None),
        ),
        check_vma=False,
    )
```
